128 devices in a mesh: dp: 8 (over x, z_lo), tensor: 16 (over z_hi, y, core).
Axes of the slice: x: 4, y: 4, z: 4 (z_hi: 2, z_lo: 2; z = z_hi * 2 + z_lo), core: 2. Of those that a mesh axis runs over, the one named last changes fastest.
Arguments:
- tokens: bfloat16 [8192, 2048], P('dp'), may hold values from -6 to 6
- cotangent: bfloat16 [8192, 2048], P('dp', 'tensor'), may hold values from -6 to 6
- expert_ids: int32 [8192, 6], P('dp'), may hold values from 0 to 15, all different within a row
- slot_order: int32 [8, 1024], P('dp'), may hold values from 0 to 1023, each once within a row
- image_starts: int32 [8, 2], P('dp'), may hold values from 0 to 768, as said below
- norm1_gain: float32 [2048], replicated, may hold values from 0.5 to 1.5
- w_query: bfloat16 [2048, 3072], P(None, 'tensor'), may hold values from -0.125 to 0.125
- w_latent: bfloat16 [2048, 576], P(None, 'tensor'), may hold values from -0.125 to 0.125
- latent_gain: float32 [512], replicated, may hold values from 0.5 to 1.5
- w_expand: bfloat16 [512, 4096], P(None, 'tensor'), may hold values from -0.25 to 0.25
- w_output: bfloat16 [2048, 2048], P('tensor'), may hold values from -0.75 to 0.75
- norm2_gain: float32 [2048], replicated, may hold values from 0.5 to 1.5
- w_router: bfloat16 [2048, 16], replicated, may hold values from -0.0625 to 0.0625
- expert_gate: bfloat16 [16, 2048, 1408], P('tensor', None, 'dp'), may hold values from -0.125 to 0.125
- expert_up: bfloat16 [16, 2048, 1408], P('tensor', None, 'dp'), may hold values from -0.125 to 0.125
- expert_down: bfloat16 [16, 2048, 1408], P('tensor', None, 'dp'), may hold values from -0.875 to 0.875
- shared_gate: bfloat16 [2048, 2816], P(None, 'tensor'), may hold values from -0.125 to 0.125
- shared_up: bfloat16 [2048, 2816], P(None, 'tensor'), may hold values from -0.125 to 0.125
- shared_down: bfloat16 [2816, 2048], P('tensor'), may hold values from -0.15625 to 0.15625
Outputs:
- output: bfloat16 [8192, 2048], P('dp', 'tensor')
- tokens_grad: float32 [8192, 2048], P('dp')
- norm1_gain_grad: float32 [2048], replicated
- w_query_grad: float32 [2048, 3072], P(None, 'tensor')
- w_latent_grad: float32 [2048, 576], P(None, 'tensor')
- latent_gain_grad: float32 [512], replicated
- w_expand_grad: float32 [512, 4096], P(None, 'tensor')
- w_output_grad: float32 [2048, 2048], P('tensor')
- norm2_gain_grad: float32 [2048], replicated
- w_router_grad: float32 [2048, 16], replicated
- expert_gate_grad: float32 [16, 2048, 1408], P('tensor', None, 'dp')
- expert_up_grad: float32 [16, 2048, 1408], P('tensor', None, 'dp')
- expert_down_grad: float32 [16, 2048, 1408], P('tensor', None, 'dp')
- shared_gate_grad: float32 [2048, 2816], P(None, 'tensor')
- shared_up_grad: float32 [2048, 2816], P(None, 'tensor')
- shared_down_grad: float32 [2816, 2048], P('tensor')
The draws below stay inside these ranges and needn't reach their ends.
Inputs may be any that keep to these rules, and one draw needn't show every extreme that they name: `expert_ids`: each row names 6 different experts. `slot_order`: each row is a permutation of the 1024 token indices of its group. `image_starts`: each sequence has 2 image spans of 256 tokens, given by their first positions in increasing order, that do not intersect and lie within the sequence.
All inputs are finite; a program needn't handle non-finite values.
Results may differ from the reference program's by a relative error of at most 0.035.
Values may be sent and summed in bfloat16 or wider, within the bound.
No kernel may reach another device: no remote copies, remote signals or barrier semaphores. Data moves between devices by JAX's collectives and lax.ppermute only.
A program may use at most 320 MiB of HBM per device.

```python
import math
import jax
import jax.numpy as jnp
from jax import lax

D = 2048
HEADS = 16
NOPE = 128
ROPE = 64
VDIM = 128
LATENT = 512
FF = 1408
SHARED = 2816
TOPK = 6
EXPERTS = 16
IMG = 256
SPANS = 2
LEN = 1024
ROWS = 1024
SEQS = 8
TOKENS = 8192
GROUPS = 8
CAP = 480


def draw_image_starts(key, part):
    key = jax.random.fold_in(key, 7)
    room = LEN - SPANS * IMG
    offsets = jax.random.randint(key, (SEQS, SPANS), 0, room + 1, dtype=jnp.int32)
    offsets = jnp.sort(offsets, axis=1)
    offsets = offsets.at[0, SPANS - 1].set(room)
    offsets = offsets.at[SEQS - 1, 0].set(0)
    return (offsets + jnp.arange(SPANS, dtype=jnp.int32)[None, :] * IMG).astype(jnp.int32)


def block_levels(rng, extent, cuts, least, top_value):
    loudness = 1.0
    for axis_at, blocks in cuts:
        steps = jax.random.uniform(jax.random.fold_in(jax.random.fold_in(rng, 6), axis_at), (blocks,), jnp.float32, least / len(cuts), top_value / len(cuts))
        loudness = loudness * jnp.repeat(jnp.exp(steps), extent[axis_at] // blocks).reshape((-1,) + (1,) * (len(extent) - 1 - axis_at))
    return loudness


def choose_distinct(stream_key, rows, amount, top, lift):
    order = jax.random.permutation(jax.random.fold_in(stream_key, 1), amount)
    pull = order
    for power in range(3):
        pull = pull * pull // amount
    pull = pull * lift // amount
    lots = jax.random.randint(jax.random.fold_in(stream_key, 2), (rows, amount), 0, 4096) + pull
    sure = jax.random.permutation(jax.random.fold_in(stream_key, 3), rows)[jnp.arange(amount) % rows]
    lots = jnp.where(jnp.arange(rows)[:, None] == sure[None, :], 1 << 14, lots)
    score = lots * amount + jnp.arange(amount)
    return lax.top_k(score.astype(jnp.int32), top)[1].astype(jnp.int32)


def normal_values(rng, shape, deviation, reach, cuts=(), held_as=jnp.bfloat16):
    array = deviation * jax.random.normal(rng, shape, jnp.float32)
    if cuts:
        array = array * block_levels(rng, shape, cuts, -0.22, 0.18)
    return jnp.clip(array, -reach, reach).astype(held_as)


def setup_inputs(seed: int = 0) -> dict:
    streams_of = jax.random.split(jax.random.key(seed), 20)
    return {
        "tokens": normal_values(streams_of[0], (TOKENS, D), 1.0, 6.0, ((0, 8),)),
        "cotangent": normal_values(streams_of[1], (TOKENS, D), 1.0, 6.0, ((0, 8), (1, 16))),
        "expert_ids": choose_distinct(streams_of[2], TOKENS, EXPERTS, TOPK, 3072),
        "slot_order": jax.vmap(lambda own: jax.random.permutation(own, ROWS))(jax.random.split(streams_of[3], GROUPS)).reshape((GROUPS, ROWS)).astype(jnp.int32),
        "image_starts": draw_image_starts(jax.random.fold_in(streams_of[19], 71), 0),
        "norm1_gain": jnp.clip(1.0 + 0.1 * jax.random.normal(streams_of[5], (D,), jnp.float32), 0.5, 1.5),
        "w_query": normal_values(streams_of[6], (D, HEADS * (NOPE + ROPE)), D ** -0.5, 0.125, ((1, 16),)),
        "w_latent": normal_values(streams_of[7], (D, LATENT + ROPE), D ** -0.5, 0.125, ((1, 16),)),
        "latent_gain": jnp.clip(1.0 + 0.1 * jax.random.normal(streams_of[8], (LATENT,), jnp.float32), 0.5, 1.5),
        "w_expand": normal_values(streams_of[9], (LATENT, HEADS * (NOPE + VDIM)), LATENT ** -0.5, 0.25, ((1, 16),)),
        "w_output": normal_values(streams_of[10], (HEADS * VDIM, D), (HEADS * VDIM // 32) ** -0.5, 0.75, ((0, 16),)),
        "norm2_gain": jnp.clip(1.0 + 0.1 * jax.random.normal(streams_of[11], (D,), jnp.float32), 0.5, 1.5),
        "w_router": normal_values(streams_of[12], (D, EXPERTS), (4 * D) ** -0.5, 0.0625),
        "expert_gate": normal_values(streams_of[13], (EXPERTS, D, FF), D ** -0.5, 0.125, ((0, 16), (2, 8))),
        "expert_up": normal_values(streams_of[14], (EXPERTS, D, FF), D ** -0.5, 0.125, ((0, 16), (2, 8))),
        "expert_down": normal_values(streams_of[15], (EXPERTS, D, FF), (FF // 32) ** -0.5, 0.875, ((0, 16), (2, 8))),
        "shared_gate": normal_values(streams_of[16], (D, SHARED), D ** -0.5, 0.125, ((1, 16),)),
        "shared_up": normal_values(streams_of[17], (D, SHARED), D ** -0.5, 0.125, ((1, 16),)),
        "shared_down": normal_values(streams_of[18], (SHARED, D), (SHARED // 2) ** -0.5, 0.15625, ((0, 16),)),
    }


@jax.custom_vjp
def low(v):
    return lax.optimization_barrier(v.astype(jnp.bfloat16)).astype(jnp.float32)

@jax.custom_vjp
def low_back(v):
    return v

def low_keep(v):
    return (low(v), None)

def low_pass(kept, grad):
    return (grad,)

def back_keep(v):
    return (v, None)

def back_low(kept, grad):
    return (low(grad),)
low.defvjp(low_keep, low_pass)
low_back.defvjp(back_keep, back_low)
epsilon = 1e-06
highest = lax.Precision.HIGHEST

def rounded(values):
    return low_back(low(values))

def rms_norm(values, gain_vec):
    return values * lax.rsqrt(lax.optimization_barrier(jnp.mean(values * values, axis=-1, keepdims=True)) + epsilon) * gain_vec

def rotary_tables(length):
    position = jnp.arange(length, dtype=jnp.float32)
    frequency = jnp.exp(jnp.arange(ROPE // 2, dtype=jnp.float32) * (-2.0 * math.log(10000.0) / ROPE))
    angles = position[:, None] * frequency[None, :]
    return (jnp.cos(angles), jnp.sin(angles))

def rotate(values, cos_table, sin_table):
    half_size = values.shape[-1] // 2
    lower_half = values[..., :half_size]
    upper_half = values[..., half_size:]
    return jnp.concatenate([lower_half * cos_table - upper_half * sin_table, upper_half * cos_table + lower_half * sin_table], axis=-1)

def seq_mask(span_starts):
    position = jnp.arange(LEN, dtype=jnp.int32)
    inside = (position[None, :] >= span_starts[:, None]) & (position[None, :] < span_starts[:, None] + IMG)
    labels = lax.optimization_barrier(jnp.sum(inside.astype(jnp.int32) * (jnp.arange(SPANS, dtype=jnp.int32)[:, None] + 1), axis=0))
    causal = position[None, :] <= position[:, None]
    return causal | (labels[:, None] == labels[None, :]) & (labels[:, None] > 0)

def attend_seq(pieces):
    query_raw, expanded, rope_raw, span_starts = pieces
    cos_table, sin_table = rotary_tables(LEN)
    query_rows = low(jnp.concatenate([query_raw[..., :NOPE], rotate(query_raw[..., NOPE:], cos_table[:, None, :], sin_table[:, None, :])], axis=-1))
    key_rope = low(rotate(rope_raw, cos_table, sin_table))
    key_rows = jnp.concatenate([expanded[..., :NOPE], jnp.broadcast_to(key_rope[:, None, :], (LEN, HEADS, ROPE))], axis=-1)
    values = expanded[..., NOPE:]
    scores = jnp.einsum('qhd,khd->hqk', query_rows, key_rows, precision=highest) * (NOPE + ROPE) ** (-0.5)
    scores = low_back(scores)
    scores = jnp.where(seq_mask(span_starts)[None], scores, -1e+30)
    attn_probs = low(jax.nn.softmax(scores, axis=-1))
    return rounded(jnp.einsum('hqk,khd->qhd', attn_probs, values, precision=highest))

def expert_group(normed, router_rows, id_rows, priority, gate_w, up_w, down_w):
    chosen = jnp.any(id_rows[:, :, None] == jnp.arange(EXPERTS, dtype=jnp.int32)[None, None, :], axis=1).astype(jnp.int32)
    ranked = chosen[priority]
    before = jnp.cumsum(ranked, axis=0) - ranked
    slot_rank = jnp.zeros_like(chosen).at[priority].set(before)
    kept_mask = (chosen > 0) & (slot_rank < CAP)
    target = jnp.where(kept_mask, slot_rank, CAP)
    token_index = jnp.broadcast_to(jnp.arange(ROWS, dtype=jnp.int32)[:, None], (ROWS, EXPERTS))
    expert_index = jnp.broadcast_to(jnp.arange(EXPERTS, dtype=jnp.int32)[None, :], (ROWS, EXPERTS))
    slot_table = jnp.full((EXPERTS, CAP + 1), ROWS, jnp.int32).at[expert_index, target].set(token_index)[:, :CAP]
    padded_in = jnp.concatenate([normed, jnp.zeros((1, D), jnp.float32)], axis=0)
    slot_inputs = padded_in[slot_table]
    padded_probs = jnp.concatenate([router_rows, jnp.zeros((1, EXPERTS), jnp.float32)], axis=0)
    slot_gates = padded_probs[slot_table, jnp.arange(EXPERTS, dtype=jnp.int32)[:, None]]
    gate_act = low_back(jnp.einsum('esd,edf->esf', slot_inputs, gate_w, precision=highest))
    up_act = low_back(jnp.einsum('esd,edf->esf', slot_inputs, up_w, precision=highest))
    expert_hidden = low(jax.nn.silu(gate_act) * up_act)
    slot_out = rounded(jnp.einsum('esf,edf->esd', expert_hidden, down_w, precision=highest))
    routed = jnp.zeros((ROWS + 1, D), jnp.float32).at[slot_table].add(slot_out * slot_gates[:, :, None])
    return routed[:ROWS]

def to_float(array_in):
    return array_in.astype(jnp.float32)

def reference(tokens, cotangent, expert_ids, slot_order, image_starts, norm1_gain, w_query, w_latent, latent_gain, w_expand, w_output, norm2_gain, w_router, expert_gate, expert_up, expert_down, shared_gate, shared_up, shared_down):
    group_count = slot_order.shape[0]
    seq_count = image_starts.shape[0]
    token_count = tokens.shape[0]

    def forward(resid, gain_one, query_w, latent_w, gain_latent, expand_w, output_w, gain_two, router_w, gate_w, up_w, down_w, shared_gate_w, shared_up_w, shared_down_w):
        normed1 = low(rms_norm(resid, gain_one))
        query_raw = low_back(jnp.dot(normed1, query_w, precision=highest))
        latent = rounded(jnp.dot(normed1, latent_w, precision=highest))
        compressed = low(rms_norm(latent[:, :LATENT], gain_latent))
        expanded = rounded(jnp.dot(compressed, expand_w, precision=highest))
        mixed_rows = lax.map(jax.checkpoint(attend_seq), (query_raw.reshape(seq_count, LEN, HEADS, NOPE + ROPE), expanded.reshape(seq_count, LEN, HEADS, NOPE + VDIM), latent[:, LATENT:].reshape(seq_count, LEN, ROPE), image_starts))
        attention = low_back(jnp.dot(mixed_rows.reshape(token_count, HEADS * VDIM), output_w, precision=highest))
        hidden_res = resid + attention
        normed2 = low(rms_norm(hidden_res, gain_two))
        logits = low_back(jnp.dot(normed2, router_w, precision=highest))
        router_probs = jax.nn.softmax(logits, axis=-1)

        def group_experts(pieces):
            return expert_group(pieces[0], pieces[1], pieces[2], pieces[3], gate_w, up_w, down_w)
        routed = lax.map(group_experts, (normed2.reshape(group_count, ROWS, D), router_probs.reshape(group_count, ROWS, EXPERTS), expert_ids.reshape(group_count, ROWS, TOPK), slot_order)).reshape(token_count, D)
        shared_gate_act = low_back(jnp.dot(normed2, shared_gate_w, precision=highest))
        shared_up_act = low_back(jnp.dot(normed2, shared_up_w, precision=highest))
        shared_hidden = low(jax.nn.silu(shared_gate_act) * shared_up_act)
        shared = jnp.dot(shared_hidden, shared_down_w, precision=highest)
        return hidden_res + routed + shared
    floats = tuple(map(to_float, (tokens, norm1_gain, w_query, w_latent, latent_gain, w_expand, w_output, norm2_gain, w_router, expert_gate, expert_up, expert_down, shared_gate, shared_up, shared_down)))
    output, pullback = jax.vjp(forward, *floats)
    gradients = pullback(cotangent.astype(jnp.float32))
    return (output.astype(jnp.bfloat16), gradients[0], gradients[1], gradients[2], gradients[3], gradients[4], gradients[5], gradients[6], gradients[7], gradients[8], gradients[9], gradients[10], gradients[11], gradients[12], gradients[13], gradients[14])
```

```python
import functools
import math

import jax
import jax.numpy as jnp
from jax import lax
from jax.experimental import pallas as pl
from jax.experimental.pallas import tpu as pltpu
from jax.sharding import PartitionSpec as P

D = 2048
NOPE = 128
ROPE = 64
VDIM = 128
LATENT = 512
TOPK = 6
EXPERTS = 16
IMG = 256
SPANS = 2
LEN = 1024
CAP = 480
FS = 176
LW = 36
LP = 48
LX = 640
RB = 64
PW = D + 128
BF = jnp.bfloat16
F32 = jnp.float32
EPS = 1e-06
MASKED = -1e30
SCALE = (NOPE + ROPE) ** (-0.5)
MB = 1024 * 1024

NN = (((1,), (0,)), ((), ()))
NT = (((1,), (1,)), ((), ()))
TN = (((0,), (0,)), ((), ()))


def dot(a, b, dims=NN):
    return lax.dot_general(a, b, dims, preferred_element_type=F32)


VM = pl.BlockSpec(memory_space=pltpu.VMEM)
SM = pl.BlockSpec(memory_space=pltpu.SMEM)


def whole(kernel, outs, ins, limit, flops=0):
    arrays = [i[0] if isinstance(i, tuple) else i for i in ins]
    specs = [i[1] if isinstance(i, tuple) else VM for i in ins]
    moved = sum(a.size * a.dtype.itemsize for a in arrays)
    moved += sum(math.prod(o.shape) * o.dtype.itemsize for o in outs)
    return pl.pallas_call(
        kernel,
        out_shape=outs,
        in_specs=specs,
        out_specs=[VM] * len(outs),
        compiler_params=pltpu.CompilerParams(vmem_limit_bytes=limit * MB),
        cost_estimate=pl.CostEstimate(flops=flops, bytes_accessed=moved, transcendentals=0),
    )(*arrays)


def sds(shape, dtype):
    return jax.ShapeDtypeStruct(shape, dtype)


def recv_t(a, zh=0, y=0, c=0):
    pairs = []
    for i in range(16):
        z, r, k = i // 8, i // 2 % 4, i % 2
        pairs.append((((z + zh) % 2) * 8 + ((r + y) % 4) * 2 + (k + c) % 2, i))
    return lax.ppermute(a, "tensor", pairs)


def recv_d(a, x=0, z=0):
    pairs = []
    for i in range(8):
        pairs.append((((i // 2 + x) % 4) * 2 + (i % 2 + z) % 2, i))
    return lax.ppermute(a, "dp", pairs)


def gather_t(a, axis=0):
    z0 = recv_t(a, zh=1)
    y1 = recv_t(a, y=1)
    y3 = recv_t(a, y=-1)
    y2 = recv_t(a, y=2)
    z1 = recv_t(z0, y=1)
    z3 = recv_t(z0, y=-1)
    z2 = recv_t(y2, zh=1)
    half = jnp.concatenate([a, y1, y2, y3, z0, z1, z2, z3], axis=axis)
    return half, recv_t(half, c=1)


def split_sum(keep, got, starts):
    width = keep.shape[1]

    def kernel(s, a, b, *outs):
        for i, o in enumerate(outs):
            rows = pl.ds(pl.multiple_of(s[i], RB), RB)
            o[...] = (a[rows, :].astype(F32) + b[rows, :].astype(F32)).astype(BF)

    return whole(kernel, [sds((RB, width), BF)] * 8, [(starts, SM), keep, got], 24)


def scatter_t(send, keep, starts):
    got = recv_t(send, c=1)
    b = split_sum(keep, got, starts)
    r11 = recv_t(b[5], y=-1)
    r13 = recv_t(b[7], y=1)
    r12 = recv_t(b[6], zh=1)
    s1 = recv_t(b[1], y=-1)
    s3 = recv_t(b[3], y=1)
    s2 = recv_t(b[2] + r12, y=2)
    sz = recv_t((b[4].astype(F32) + r11.astype(F32) + r13.astype(F32)).astype(BF), zh=1)
    return b[0], s1, s2, s3, sz


def sum_dp(rows, dr):
    x, z = dr // 2, dr % 2
    part = [lax.dynamic_slice_in_dim(rows, ((x + i) % 4) * 128, 128, 0) for i in range(4)]
    got = [recv_d(part[i], x=-i) for i in (1, 2, 3)]
    total = part[0].astype(F32) + sum(g.astype(F32) for g in got)
    total = total.astype(BF)
    send = lax.dynamic_slice_in_dim(total, (1 - z) * 64, 64, 0)
    keep = lax.dynamic_slice_in_dim(total, z * 64, 64, 0)
    own = (keep.astype(F32) + recv_d(send, z=1).astype(F32)).astype(BF)
    other = recv_d(own, z=1)
    mine = jnp.where(
        z == 0, jnp.concatenate([own, other], 0), jnp.concatenate([other, own], 0)
    )
    parts = [mine] + [recv_d(mine, x=i) for i in (1, 2, 3)]
    out = jnp.zeros((512, D), BF)
    for i, p in enumerate(parts):
        out = lax.dynamic_update_slice_in_dim(out, p, ((x + i) % 4) * 128, 0)
    return out


def sum_all(v):
    v = v + recv_t(v, zh=1)
    v = v + recv_t(v, c=1)
    pairs = [(i, (i // 8) * 8 + ((i // 2 % 4) ^ 1) * 2 + i % 2) for i in range(16)]
    v = v + lax.ppermute(v, "tensor", pairs)
    v = v + recv_t(v, y=2)
    v = v + recv_d(v, z=1)
    pairs = [(i, ((i // 2) ^ 1) * 2 + i % 2) for i in range(8)]
    v = v + lax.ppermute(v, "dp", pairs)
    return v + recv_d(v, x=2)


def rotary_tables(length):
    position = jnp.arange(length, dtype=F32)
    frequency = jnp.exp(jnp.arange(ROPE // 2, dtype=F32) * (-2.0 * math.log(10000.0) / ROPE))
    angles = position[:, None] * frequency[None, :]
    return jnp.cos(angles), jnp.sin(angles)


def rotate(v, cos, sin):
    a, b = v[:, : ROPE // 2], v[:, ROPE // 2 :]
    return jnp.concatenate([a * cos - b * sin, b * cos + a * sin], axis=-1)


def unrotate(v, cos, sin):
    a, b = v[:, : ROPE // 2], v[:, ROPE // 2 :]
    return jnp.concatenate([a * cos + b * sin, b * cos - a * sin], axis=-1)


QB = 256


def probs_of(starts, first, qn, qr, kn, kr):
    scores = (dot(qn, kn, NT) + dot(qr, kr, NT)) * SCALE
    i = first + lax.broadcasted_iota(jnp.int32, (QB, 1), 0)
    j = lax.broadcasted_iota(jnp.int32, (1, LEN), 1)
    allowed = j <= i
    for n in range(SPANS):
        s = starts[0, n]
        row_in = (i >= s) & (i < s + IMG)
        col_in = (j >= s) & (j < s + IMG)
        allowed = allowed | (row_in & col_in)
    scores = jnp.where(allowed, scores, MASKED)
    raised = jnp.exp(scores - jnp.max(scores, axis=-1, keepdims=True))
    return raised / jnp.sum(raised, axis=-1, keepdims=True)


def attend(starts, qn, qr, kn, kr, v):
    def kernel(s, qn, qr, kn, kr, v, o):
        p = probs_of(s, pl.program_id(0) * QB, qn[...], qr[...], kn[...], kr[...])
        o[...] = dot(p.astype(BF), v[...]).astype(BF)

    rows = lambda w: pl.BlockSpec((QB, w), lambda i: (i, 0))
    full = lambda w: pl.BlockSpec((LEN, w), lambda i: (0, 0))
    return pl.pallas_call(
        kernel,
        grid=(LEN // QB,),
        out_shape=sds((LEN, VDIM), BF),
        in_specs=[SM, rows(NOPE), rows(ROPE), full(NOPE), full(ROPE), full(VDIM)],
        out_specs=rows(VDIM),
        compiler_params=pltpu.CompilerParams(vmem_limit_bytes=32 * MB),
        cost_estimate=pl.CostEstimate(
            flops=2 * LEN * LEN * 320, bytes_accessed=2 * MB, transcendentals=LEN * LEN
        ),
    )(starts, qn, qr, kn, kr, v)


def attend_back(starts, qn, qr, kn, kr, v, mg):
    def kernel(s, qn, qr, kn, kr, v, mg, dqn, dqr, dkn, dkr, dv):
        step = pl.program_id(0)

        @pl.when(step == 0)
        def _():
            dkn[...] = jnp.zeros_like(dkn)
            dkr[...] = jnp.zeros_like(dkr)
            dv[...] = jnp.zeros_like(dv)

        p = probs_of(s, step * QB, qn[...], qr[...], kn[...], kr[...])
        m = mg[...]
        pg = dot(m, v[...], NT)
        sg = (p * (pg - jnp.sum(pg * p, axis=-1, keepdims=True))).astype(BF)
        dqn[...] = dot(sg, kn[...]) * SCALE
        dqr[...] = dot(sg, kr[...]) * SCALE
        dkn[...] += dot(sg, qn[...], TN) * SCALE
        dkr[...] += dot(sg, qr[...], TN) * SCALE
        dv[...] += dot(p.astype(BF), m, TN)

    rows = lambda w: pl.BlockSpec((QB, w), lambda i: (i, 0))
    full = lambda w: pl.BlockSpec((LEN, w), lambda i: (0, 0))
    return pl.pallas_call(
        kernel,
        grid=(LEN // QB,),
        out_shape=[sds((LEN, w), F32) for w in (NOPE, ROPE, NOPE, ROPE, VDIM)],
        in_specs=[SM, rows(NOPE), rows(ROPE), full(NOPE), full(ROPE), full(VDIM), rows(VDIM)],
        out_specs=[rows(NOPE), rows(ROPE), full(NOPE), full(ROPE), full(VDIM)],
        compiler_params=pltpu.CompilerParams(vmem_limit_bytes=40 * MB),
        cost_estimate=pl.CostEstimate(
            flops=2 * LEN * LEN * 960, bytes_accessed=4 * MB, transcendentals=LEN * LEN
        ),
    )(starts, qn, qr, kn, kr, v, mg)


def project(mixed, other, w_half, w_other, tokens, gain, w_router):
    rows_at = 256

    def kernel(m1, m2, w1, w2, x, gain, wr, hid, nrm, inv, probs):
        h = x[...].astype(F32) + (dot(m1[...], w1[...]) + dot(m2[...], w2[...]))
        r = lax.rsqrt(jnp.mean(h * h, axis=-1, keepdims=True) + EPS)
        n = (h * r * gain[...]).astype(BF)
        hid[...] = h
        nrm[...] = n
        inv[...] = r
        logits = dot(n, wr[...])
        e = jnp.exp(logits - jnp.max(logits, axis=-1, keepdims=True))
        probs[...] = e / jnp.sum(e, axis=-1, keepdims=True)

    rows = lambda w: pl.BlockSpec((rows_at, w), lambda i: (i, 0))
    once = lambda a: pl.BlockSpec(a.shape, lambda i: (0, 0), pipeline_mode=pl.Buffered(1))
    return pl.pallas_call(
        kernel,
        grid=(LEN // rows_at,),
        out_shape=[sds((LEN, D), F32), sds((LEN, D), BF), sds((LEN, 1), F32), sds((LEN, EXPERTS), F32)],
        in_specs=[rows(D // 2), rows(D // 2), once(w_half), once(w_other), rows(D), once(gain), once(w_router)],
        out_specs=[rows(D), rows(D), rows(1), rows(EXPERTS)],
        compiler_params=pltpu.CompilerParams(vmem_limit_bytes=48 * MB),
        cost_estimate=pl.CostEstimate(flops=2 * LEN * D * D, bytes_accessed=30 * MB, transcendentals=0),
    )(mixed, other, w_half, w_other, tokens, gain, w_router)


def dispatch(rank_row, probs_row, normed2, grad):
    cols = 512

    def kernel(rank, probs, n, g, x, dy, dyg, gates):
        hit = lax.broadcasted_iota(jnp.int32, (CAP, 1), 0) == rank[...]
        gate = jnp.sum(jnp.where(hit, probs[...], 0.0), axis=-1, keepdims=True)
        pick = jnp.where(hit, 1.0, 0.0).astype(BF)
        x[...] = dot(pick, n[...]).astype(BF)
        got = dot(pick, g[...])
        dyg[...] = got.astype(BF)
        dy[...] = (got * gate).astype(BF)
        gates[...] = gate

    part = pl.BlockSpec((LEN, cols), lambda i: (0, i))
    slot = pl.BlockSpec((CAP, cols), lambda i: (0, i))
    row = pl.BlockSpec((1, LEN), lambda i: (0, 0))
    return pl.pallas_call(
        kernel,
        grid=(D // cols,),
        out_shape=[sds((CAP, D), BF)] * 3 + [sds((CAP, 1), F32)],
        in_specs=[row, row, part, part],
        out_specs=[slot, slot, slot, pl.BlockSpec((CAP, 1), lambda i: (0, 0))],
        compiler_params=pltpu.CompilerParams(vmem_limit_bytes=40 * MB),
        cost_estimate=pl.CostEstimate(flops=4 * LEN * CAP * D, bytes_accessed=16 * MB, transcendentals=0),
    )(rank_row, probs_row, normed2, grad)


def ffn_chunk(x, dy, gu, dn, dgu, ddn):
    act = dot(gu[...], x, NT)
    g, u = act[:FS], act[FS:]
    sg = jax.nn.sigmoid(g)
    h = (g * sg * u).astype(BF)
    dh = dot(dn[...], dy, NT)
    dg = (dh * u * sg * (1.0 + g * (1.0 - sg))).astype(BF)
    du = (dh * g * sg).astype(BF)
    da = jnp.concatenate([dg, du], axis=0)
    ddn[...] = dot(h, dy).astype(BF)
    dgu[...] = dot(da, x).astype(BF)
    return dot(h, dn[...], TN), dot(da, gu[...], TN)


def chunk_outs(n):
    return [sds((2 * FS, D), BF), sds((FS, D), BF)] * n


FLOPS = 2 * 9 * FS * D


def experts_first(x, dy, chunks):
    n = len(chunks)

    def kernel(x, dy, *refs):
        w, outs, (out, dx) = refs[: 2 * n], refs[2 * n : 4 * n], refs[4 * n :]
        xv, dyv = x[...], dy[...]
        for i in range(n):
            o, d = ffn_chunk(xv, dyv, *w[2 * i : 2 * i + 2], *outs[2 * i : 2 * i + 2])
            if i == 0:
                out[...] = o
                dx[...] = d
            else:
                out[...] += o
                dx[...] += d

    flat = [a for c in chunks for a in c]
    res = whole(kernel, chunk_outs(n) + [sds((CAP, D), F32)] * 2, [x, dy] + flat, 56, n * FLOPS * CAP)
    return [(res[2 * i], res[2 * i + 1]) for i in range(n)], res[2 * n], res[2 * n + 1]


def experts_last(x, dy, dyg, chunks, out, dx, me):
    n = len(chunks)

    def kernel(me, x, dy, dyg, out0, dx0, *refs):
        w, outs, (out, dx) = refs[: 2 * n], refs[2 * n : 4 * n], refs[4 * n :]
        xv, dyv = x[...], dy[...]
        sum_o, sum_d = out0[...], dx0[...]
        for i in range(n):
            o, d = ffn_chunk(xv, dyv, *w[2 * i : 2 * i + 2], *outs[2 * i : 2 * i + 2])
            sum_o, sum_d = sum_o + o, sum_d + d
        so = sum_o.astype(BF)
        out[...] = so
        dx[:, :D] = sum_d.astype(BF)
        gg = jnp.sum(so.astype(F32) * dyg[...].astype(F32), axis=-1, keepdims=True)
        lane = lax.broadcasted_iota(jnp.int32, (1, 128), 1)
        dx[:, D:] = jnp.where(lane == me[0], gg, 0.0).astype(BF)

    flat = [a for c in chunks for a in c]
    outs = chunk_outs(n) + [sds((CAP, D), BF), sds((CAP, PW), BF)]
    res = whole(kernel, outs, [(me, SM), x, dy, dyg, out, dx] + flat, 60, n * FLOPS * CAP)
    return [(res[2 * i], res[2 * i + 1]) for i in range(n)], res[2 * n], res[2 * n + 1]


def shared_ffn(x, dy, gu, dn):
    def kernel(x, dy, gu, dn, dgu, ddn, out, dx):
        o, d = ffn_chunk(x[...], dy[...], gu, dn, dgu, ddn)
        out[...] = o.astype(BF)
        dx[...] = d.astype(BF)

    outs = chunk_outs(1) + [sds((LEN, D), BF)] * 2
    return whole(kernel, outs, [x, dy, gu, dn], 58, FLOPS * LEN)


def combine_grad(which, rank_col, dx, shared_dx):
    rows_at = 256

    def kernel(which, rank, dx, sd, o):
        hit = rank[...] == lax.broadcasted_iota(jnp.int32, (1, CAP), 1)
        pick = jnp.where(hit, 1.0, 0.0).astype(BF)
        t = dot(pick, dx[...])
        o[:, :D] = (t[:, :D] + sd[...].astype(F32)).astype(BF)
        o[:, D:] = t[:, D:].astype(BF)

    at = lambda w: pl.BlockSpec((rows_at, w), lambda i, which: (which[0] * 2 + i, 0))
    return pl.pallas_call(
        kernel,
        grid_spec=pltpu.PrefetchScalarGridSpec(
            num_scalar_prefetch=1,
            grid=(2,),
            in_specs=[at(1), pl.BlockSpec((CAP, PW), lambda i, which: (0, 0)), at(D)],
            out_specs=pl.BlockSpec((rows_at, PW), lambda i, which: (i, 0)),
        ),
        out_shape=sds((LEN // 2, PW), BF),
        compiler_params=pltpu.CompilerParams(vmem_limit_bytes=40 * MB),
        cost_estimate=pl.CostEstimate(flops=LEN * CAP * PW, bytes_accessed=7 * MB, transcendentals=0),
    )(which, rank_col, dx, shared_dx)


def combine_out(rank_col, probs_col, slot_out, shared_out):
    rows_at = 256

    def kernel(rank, probs, so, sh, o):
        hit = rank[...] == lax.broadcasted_iota(jnp.int32, (1, CAP), 1)
        pick = jnp.where(hit, 1.0, 0.0).astype(BF)
        o[...] = (dot(pick, so[...]) * probs[...] + sh[...].astype(F32)).astype(BF)

    at = lambda w: pl.BlockSpec((rows_at, w), lambda i: (i, 0))
    return pl.pallas_call(
        kernel,
        grid=(LEN // rows_at,),
        out_shape=sds((LEN, D), BF),
        in_specs=[at(1), at(1), pl.BlockSpec((CAP, D), lambda i: (0, 0)), at(D)],
        out_specs=at(D),
        compiler_params=pltpu.CompilerParams(vmem_limit_bytes=40 * MB),
        cost_estimate=pl.CostEstimate(flops=2 * LEN * CAP * D, bytes_accessed=10 * MB, transcendentals=0),
    )(rank_col, probs_col, slot_out, shared_out)


def norm_back(v, inv, gain, incoming):
    weighted = incoming * gain
    inner = jnp.mean(weighted * v, axis=-1, keepdims=True)
    return inv * weighted - v * (inv * inv * inv) * inner, jnp.sum(incoming * v * inv, axis=0, keepdims=True)


def rows_two(terms, hidden, inv, probs, grad, gain, w_router_t):
    def kernel(a, b, c, d, e, h, inv, p, g, gain, wr, hg, pay, gg):
        t = a[...].astype(F32) + b[...].astype(F32) + c[...].astype(F32)
        t = t + d[...].astype(F32) + e[...].astype(F32)
        gates = t[:, D : D + EXPERTS]
        pv = p[...]
        lg = (pv * (gates - jnp.sum(pv * gates, axis=-1, keepdims=True))).astype(BF)
        n2 = t[:, :D] + dot(lg, wr[...])
        r, gain_grad = norm_back(h[...], inv[...], gain[...], n2)
        r = r + g[...].astype(F32)
        hg[...] = r
        pay[:, :D] = r.astype(BF)
        pay[:, D:] = jnp.concatenate([lg, jnp.zeros((RB, 128 - EXPERTS), BF)], axis=1)
        gg[...] = gain_grad

    outs = [sds((RB, D), F32), sds((RB, PW), BF), sds((1, D), F32)]
    return whole(kernel, outs, [*terms, hidden, inv, probs, grad, gain, w_router_t], 24)


def rows_one(terms, lat, w_lat, x, inv, hg, gain):
    def kernel(a, b, c, d, e, lat, wl, x, inv, hg, gain, o, gg):
        t = a[...].astype(F32) + b[...].astype(F32) + c[...].astype(F32)
        t = t + d[...].astype(F32) + e[...].astype(F32)
        t = t + dot(lat[...], wl[...])
        r, gain_grad = norm_back(x[...].astype(F32), inv[...], gain[...], t)
        o[...] = (hg[...] + r).astype(BF)
        gg[...] = gain_grad

    outs = [sds((RB, D), BF), sds((1, D), F32)]
    return whole(kernel, outs, [*terms, lat, w_lat, x, inv, hg, gain], 24, 2 * RB * LX * D)


def mixed_back(starts, half, other, w_out):
    def kernel(s, a, b, w, o):
        for n, ref in enumerate((a, b)):
            t = dot(ref[:, :D], w[...], NT).astype(BF)
            for i in range(8):
                rows = pl.ds(pl.multiple_of(s[n * 8 + i], RB), RB)
                o[rows, :] = t[i * RB : (i + 1) * RB]

    return whole(kernel, [sds((LEN, VDIM), BF)], [(starts, SM), half, other, w_out], 32, 2 * LEN * D * VDIM)[0]


def output_grads(starts, half, other, mixed, normed2):
    def kernel(s, a, b, m, n2, wo, wr):
        sum_o = jnp.zeros((VDIM, D), F32)
        sum_r = jnp.zeros((EXPERTS, D), F32)
        for n, ref in enumerate((a, b)):
            at = [pl.ds(pl.multiple_of(s[n * 8 + i], RB), RB) for i in range(8)]
            mix = jnp.concatenate([m[r, :] for r in at], axis=0)
            sum_o = sum_o + dot(mix, ref[:, :D], TN)
            for i, r in enumerate(at):
                lg = ref[i * RB : (i + 1) * RB, D:]
                sum_r = sum_r + dot(lg, n2[r, :], TN)[:EXPERTS]
        wo[...] = sum_o.astype(BF)
        wr[...] = sum_r.astype(BF)

    outs = [sds((VDIM, D), BF), sds((EXPERTS, D), BF)]
    return whole(kernel, outs, [(starts, SM), half, other, mixed, normed2], 40, 2 * LEN * D * 256)


def latent_w_grad(starts, half, other, normed1, pick):
    def kernel(s, a, b, n1, pick, o):
        total = jnp.zeros((LP, D), F32)
        for n, ref in enumerate((a, b)):
            rows = jnp.concatenate(
                [n1[pl.ds(pl.multiple_of(s[n * 8 + i], RB), RB), :] for i in range(8)], axis=0
            )
            own = dot(pick[...], ref[...], NT).astype(BF)
            total = total + dot(own, rows)
        o[...] = total.astype(BF)

    outs = [sds((LP, D), BF)]
    return whole(kernel, outs, [(starts, SM), half, other, normed1, pick], 32, 2 * LEN * LX * 256)[0]


def spread(starts, half, other):
    def kernel(s, a, b, o):
        for n, ref in enumerate((a, b)):
            for i in range(8):
                rows = pl.ds(pl.multiple_of(s[n * 8 + i], RB), RB)
                o[rows, :] = ref[i * RB : (i + 1) * RB].astype(F32)

    return whole(kernel, [sds((LEN, D), F32)], [(starts, SM), half, other], 32)[0]


def local(
    tokens,
    cotangent,
    expert_ids,
    slot_order,
    image_starts,
    norm1_gain,
    w_query,
    w_latent,
    latent_gain,
    w_expand,
    w_output,
    norm2_gain,
    w_router,
    expert_gate,
    expert_up,
    expert_down,
    shared_gate,
    shared_up,
    shared_down,
):
    tr = lax.axis_index("tensor")
    dr = lax.axis_index("dp")
    zh, yy, cc = tr // 8, tr // 2 % 4, tr % 2
    peers = [
        ((zh + z) % 2, (yy + y) % 4, (cc + c) % 2) for c in range(2) for z in range(2) for y in range(4)
    ]
    starts16 = jnp.stack([(c * 8 + z * 4 + y) * RB for z, y, c in peers]).astype(jnp.int32)
    starts8 = jnp.stack([(z * 4 + y) * RB for z, y, c in peers[:8]]).astype(jnp.int32)
    ranks16 = jnp.stack([z * 8 + y * 2 + c for z, y, c in peers]).astype(jnp.int32)
    own_row = (cc * 8 + zh * 4 + yy) * RB
    own_rows = lambda a: lax.dynamic_slice_in_dim(a, own_row, RB, 0)
    me = jnp.full((1,), tr, jnp.int32)

    lat_t = jnp.pad(w_latent.T, [(0, LP - LW), (0, 0)])
    lat_half, lat_other = gather_t(lat_t)
    own = (
        jnp.concatenate([expert_gate[0].T, expert_up[0].T], axis=0),
        expert_down[0].T,
    )
    move = lambda pair, **k: tuple(recv_d(a, **k) for a in pair)
    ap, am, zz = move(own, x=1), move(own, x=-1), move(own, z=1)
    a2 = move(own, x=2)
    b2 = move(zz, x=2)
    bp = (recv_d(ap[0], z=1), recv_d(zz[1], x=1))
    bm = (recv_d(am[0], z=1), recv_d(zz[1], x=-1))
    wo_half, wo_other = gather_t(w_output)
    out_grad = lax.all_gather(cotangent, "tensor", axis=1, tiled=True)

    chosen = jnp.any(expert_ids == tr, axis=1)
    order = slot_order[0]
    token = jnp.arange(LEN, dtype=jnp.int32)
    place = jnp.sum(jnp.where(order[:, None] == token[None, :], token[:, None], 0), axis=0)
    before = (place[:, None] < place[None, :]) & chosen[:, None]
    rank = jnp.sum(before.astype(jnp.int32), axis=0)
    rank = jnp.where(chosen, rank, -1)
    rank_row, rank_col = rank[None, :], rank[:, None]

    resid = tokens.astype(F32)
    inv1 = lax.rsqrt(jnp.mean(resid * resid, axis=-1, keepdims=True) + EPS)
    normed1 = (resid * inv1 * norm1_gain).astype(BF)
    cos, sin = rotary_tables(LEN)
    query = dot(normed1, w_query)
    qn = query[:, :NOPE].astype(BF)
    qr = rotate(query[:, NOPE:], cos, sin).astype(BF)
    column = jnp.arange(LP, dtype=jnp.int32)
    target = jnp.where(column[None, :] < LW, ranks16[:, None] * LW + column[None, :], -1).reshape(-1)
    lat_place = (jnp.arange(LX, dtype=jnp.int32)[:, None] == target[None, :]).astype(BF)
    w_lat = (
        dot(lat_place[:, : 8 * LP], lat_half) + dot(lat_place[:, 8 * LP :], lat_other)
    ).astype(BF)
    latent = dot(normed1, w_lat, NT).astype(BF)
    lat_in = latent[:, :LATENT].astype(F32)
    inv_lat = lax.rsqrt(jnp.mean(lat_in * lat_in, axis=-1, keepdims=True) + EPS)
    compressed = (lat_in * inv_lat * latent_gain).astype(BF)
    expanded = dot(compressed, w_expand).astype(BF)
    kn, v = expanded[:, :NOPE], expanded[:, NOPE:]
    kr = rotate(latent[:, LATENT : LATENT + ROPE].astype(F32), cos, sin).astype(BF)
    mixed = attend(image_starts, qn, qr, kn, kr, v)
    mix_half, mix_other = gather_t(mixed, axis=1)
    hidden, normed2, inv2, probs = project(
        mix_half, mix_other, wo_half, wo_other, tokens, norm2_gain[None, :], w_router
    )
    probs_col = lax.dynamic_slice_in_dim(probs, tr, 1, 1)

    x, dy, dyg, _ = dispatch(rank_row, probs_col.reshape(1, LEN), normed2, out_grad)
    near, part_out, part_dx = experts_first(x, dy, [own, ap, am, zz])
    sh_gu = jnp.concatenate([shared_gate.T, shared_up.T], axis=0)
    s_dgu, s_ddn, s_out, s_dx = shared_ffn(normed2, out_grad, sh_gu, shared_down)
    far, slot_out, dx = experts_last(x, dy, dyg, [bp, bm, b2, a2], part_out, part_dx, me)
    half_of = lambda k: jnp.full((1,), k, jnp.int32)
    n2_send = combine_grad(half_of(1 - cc), rank_col, dx, s_dx)
    n2_keep = combine_grad(half_of(cc), rank_col, dx, s_dx)
    n2_terms = scatter_t(n2_send, n2_keep, starts8)

    g_own, g_ap, g_am, g_z = near
    g_bp, g_bm, g_b2, g_a2 = far
    got_b2 = move(g_b2, x=2)
    got_a2 = move(g_a2, x=2)
    ap_gu = g_ap[0] + recv_d(g_bp[0], z=1)
    am_gu = g_am[0] + recv_d(g_bm[0], z=1)
    z_gu = g_z[0] + got_b2[0]
    z_dn = (
        g_z[1].astype(F32)
        + got_b2[1].astype(F32)
        + recv_d(g_bp[1], x=-1).astype(F32)
        + recv_d(g_bm[1], x=1).astype(F32)
    ).astype(BF)
    terms = [g_own, got_a2, move((ap_gu, g_ap[1]), x=-1), move((am_gu, g_am[1]), x=1), move((z_gu, z_dn), z=1)]
    gu_sum = sum(t[0].astype(F32) for t in terms)
    dn_sum = sum(t[1].astype(F32) for t in terms)
    expert_gate_grad = gu_sum[:FS].T[None]
    expert_up_grad = gu_sum[FS:].T[None]
    expert_down_grad = dn_sum.T[None]

    branch = combine_out(rank_col, probs_col, slot_out, s_out)
    branch_sum = lax.psum_scatter(branch, "tensor", scatter_dimension=1, tiled=True)
    own_cols = lax.dynamic_slice_in_dim(hidden, tr * 128, 128, 1)
    output = (own_cols + branch_sum.astype(F32)).astype(BF)
    s_dgu, s_ddn = lax.psum((s_dgu, s_ddn), "dp")

    hid_grad, payload, gain2 = rows_two(
        n2_terms,
        own_rows(hidden),
        own_rows(inv2),
        own_rows(probs),
        own_rows(out_grad),
        norm2_gain[None, :],
        w_router.T,
    )
    pay_half, pay_other = gather_t(payload)
    mixed_grad = mixed_back(starts16, pay_half, pay_other, w_output)

    dqn, dqr, dkn, dkr, dv = attend_back(image_starts, qn, qr, kn, kr, v, mixed_grad)
    query_grad = jnp.concatenate([dqn, unrotate(dqr, cos, sin)], axis=1).astype(BF)
    expanded_grad = jnp.concatenate([dkn, dv], axis=1).astype(BF)
    comp_grad = dot(expanded_grad, w_expand, NT)
    lat_head, gain_lat = norm_back(lat_in, inv_lat, latent_gain, comp_grad)
    lat_part = jnp.concatenate(
        [lat_head, unrotate(dkr, cos, sin), jnp.zeros((LEN, LX - LATENT - ROPE), F32)], axis=1
    ).astype(BF)
    half_rows = lambda a, k: lax.dynamic_slice_in_dim(a, k * (LEN // 2), LEN // 2, 0)
    lat_terms = scatter_t(half_rows(lat_part, 1 - cc), half_rows(lat_part, cc), starts8)
    n1_send = dot(half_rows(query_grad, 1 - cc), w_query, NT).astype(BF)
    n1_keep = dot(half_rows(query_grad, cc), w_query, NT).astype(BF)
    n1_terms = scatter_t(n1_send, n1_keep, starts8)
    lat_rows = sum(t.astype(F32) for t in lat_terms).astype(BF)
    lg_half, lg_other = gather_t(lat_rows)
    tok_rows, gain1 = rows_one(
        n1_terms, lat_rows, w_lat, own_rows(tokens), own_rows(inv1), hid_grad, norm1_gain[None, :]
    )
    tok_half, tok_other = gather_t(tok_rows)
    tokens_grad = spread(starts16, tok_half, tok_other)

    w_out_g, w_router_g = output_grads(starts16, pay_half, pay_other, mixed, normed2)
    w_query_g = dot(query_grad, normed1, TN).astype(BF)
    w_expand_g = dot(compressed, expanded_grad, TN).astype(BF).reshape(64, D)
    pick = (
        (jnp.arange(LX, dtype=jnp.int32)[None, :] == tr * LW + column[:, None]) & (column[:, None] < LW)
    ).astype(BF)
    w_lat_g = latent_w_grad(starts16, lg_half, lg_other, normed1, pick)
    rows = jnp.concatenate(
        [w_query_g, w_out_g, w_expand_g, w_lat_g, w_router_g, jnp.zeros((64, D), BF)], axis=0
    )
    rows = sum_dp(rows, dr).astype(F32)
    gains = jnp.concatenate([gain1.reshape(16, 128), gain2.reshape(16, 128), gain_lat.reshape(4, 128), jnp.zeros((4, 128), F32)], axis=0)
    gains = sum_all(gains)
    return (
        output,
        tokens_grad,
        gains[:16].reshape(D),
        rows[:192].T,
        rows[384 : 384 + LW].T,
        gains[32:36].reshape(LATENT),
        rows[320:384].reshape(LATENT, 256),
        rows[192:320],
        gains[16:32].reshape(D),
        rows[432:448].T,
        expert_gate_grad,
        expert_up_grad,
        expert_down_grad,
        s_dgu[:FS].astype(F32).T,
        s_dgu[FS:].astype(F32).T,
        s_ddn.astype(F32),
    )


def solution(mesh):
    in_specs = (
        P("dp", None),
        P("dp", "tensor"),
        P("dp", None),
        P("dp", None),
        P("dp", None),
        P(),
        P(None, "tensor"),
        P(None, "tensor"),
        P(),
        P(None, "tensor"),
        P("tensor", None),
        P(),
        P(),
        P("tensor", None, "dp"),
        P("tensor", None, "dp"),
        P("tensor", None, "dp"),
        P(None, "tensor"),
        P(None, "tensor"),
        P("tensor", None),
    )
    out_specs = (
        P("dp", "tensor"),
        P("dp", None),
        P(),
        P(None, "tensor"),
        P(None, "tensor"),
        P(),
        P(None, "tensor"),
        P("tensor", None),
        P(),
        P(),
        P("tensor", None, "dp"),
        P("tensor", None, "dp"),
        P("tensor", None, "dp"),
        P(None, "tensor"),
        P(None, "tensor"),
        P("tensor", None),
    )
    return jax.shard_map(local, mesh=mesh, in_specs=in_specs, out_specs=out_specs, check_vma=False)
```

```python
import functools
import math

import jax
import jax.numpy as jnp
from jax import lax
from jax.experimental import pallas as pl
from jax.experimental.pallas import tpu as pltpu
from jax.sharding import PartitionSpec as P

D = 2048
NOPE = 128
ROPE = 64
VDIM = 128
LATENT = 512
TOPK = 6
EXPERTS = 16
IMG = 256
SPANS = 2
LEN = 1024
CAP = 480
FS = 176
LW = 36
LW48 = 48
LP = 80
LX = 640
RB = 128
PW = D + 128
QW = D + LX
FA = 3 * FS
BF = jnp.bfloat16
F32 = jnp.float32
EPS = 1e-06
MASKED = -1e30
SCALE = (NOPE + ROPE) ** (-0.5)
MB = 1024 * 1024

NN = (((1,), (0,)), ((), ()))
NT = (((1,), (1,)), ((), ()))
TN = (((0,), (0,)), ((), ()))


def dot(a, b, dims=NN):
    return lax.dot_general(a, b, dims, preferred_element_type=F32)


VM = pl.BlockSpec(memory_space=pltpu.VMEM)
SM = pl.BlockSpec(memory_space=pltpu.SMEM)


def whole(kernel, outs, ins, limit, flops=0):
    arrays = [i[0] if isinstance(i, tuple) else i for i in ins]
    specs = [i[1] if isinstance(i, tuple) else VM for i in ins]
    return pl.pallas_call(
        kernel,
        out_shape=outs,
        in_specs=specs,
        out_specs=[VM] * len(outs),
        compiler_params=pltpu.CompilerParams(vmem_limit_bytes=limit * MB),
        cost_estimate=LIGHT,
    )(*arrays)


LIGHT = pl.CostEstimate(flops=1, bytes_accessed=1, transcendentals=0)


def sds(shape, dtype):
    return jax.ShapeDtypeStruct(shape, dtype)


def recv_t(a, zh=0, y=0, c=0):
    pairs = []
    for i in range(16):
        z, r, k = i // 8, i // 2 % 4, i % 2
        pairs.append((((z + zh) % 2) * 8 + ((r + y) % 4) * 2 + (k + c) % 2, i))
    return lax.ppermute(a, "tensor", pairs)


def recv_d(a, x=0, z=0):
    pairs = []
    for i in range(8):
        pairs.append((((i // 2 + x) % 4) * 2 + (i % 2 + z) % 2, i))
    return lax.ppermute(a, "dp", pairs)


def from_y(a):
    y1, y3 = recv_t(a, y=1), recv_t(a, y=-1)
    across, y1, y3 = sync(a, y1, y3)
    return [y1, recv_t(across, y=2), y3]


def to_y(b):
    y1, y3 = recv_t(b[1], y=-1), recv_t(b[3], y=1)
    across, y1, y3 = sync(b[2], y1, y3)
    return [y1, recv_t(across, y=2), y3]


def cat(*arrays):
    return jnp.concatenate(arrays, axis=0)


def split_sum(keep, got, starts):
    width = keep.shape[1]

    def kernel(s, a, b, *outs):
        for i, o in enumerate(outs):
            rows = pl.ds(pl.multiple_of(s[i], RB), RB)
            o[...] = (a[rows, :].astype(F32) + b[rows, :].astype(F32)).astype(BF)

    return whole(kernel, [sds((RB, width), BF)] * 4, [(starts, SM), keep, got], 16)


def add(*terms):
    return sum(t.astype(F32) for t in terms).astype(BF)


def swap_x(a):
    return lax.ppermute(a, "dp", [(i, ((i // 2) ^ 1) * 2 + i % 2) for i in range(8)])


def halves(a, k):
    n = a.shape[1] // 2
    return lax.dynamic_slice_in_dim(a, k * n, n, 1), lax.dynamic_slice_in_dim(a, (1 - k) * n, n, 1)


def sum_d(v, turn):
    if turn == 0:
        got = recv_d(v, z=1)
    elif turn == 1:
        got = swap_x(v)
    else:
        got = recv_d(v, x=2)
    return (v.astype(F32) + got.astype(F32)).astype(v.dtype)


def sync(*arrays):
    return lax.optimization_barrier(arrays)


def rotary_tables(length):
    position = jnp.arange(length, dtype=F32)
    frequency = jnp.exp(jnp.arange(ROPE // 2, dtype=F32) * (-2.0 * math.log(10000.0) / ROPE))
    angles = position[:, None] * frequency[None, :]
    return jnp.cos(angles), jnp.sin(angles)


def rotate(v, cos, sin):
    a, b = v[:, : ROPE // 2], v[:, ROPE // 2 :]
    return jnp.concatenate([a * cos - b * sin, b * cos + a * sin], axis=-1)


def unrotate(v, cos, sin):
    a, b = v[:, : ROPE // 2], v[:, ROPE // 2 :]
    return jnp.concatenate([a * cos + b * sin, b * cos - a * sin], axis=-1)


QB = 256


def probs_of(starts, first, qn, qr, kn, kr):
    scores = (dot(qn, kn, NT) + dot(qr, kr, NT)) * SCALE
    i = first + lax.broadcasted_iota(jnp.int32, (QB, 1), 0)
    j = lax.broadcasted_iota(jnp.int32, (1, LEN), 1)
    allowed = j <= i
    for n in range(SPANS):
        s = starts[0, n]
        row_in = (i >= s) & (i < s + IMG)
        col_in = (j >= s) & (j < s + IMG)
        allowed = allowed | (row_in & col_in)
    scores = jnp.where(allowed, scores, MASKED)
    raised = jnp.exp(scores - jnp.max(scores, axis=-1, keepdims=True))
    return raised / jnp.sum(raised, axis=-1, keepdims=True)


def attend(starts, qn, qr, kn, kr, v):
    def kernel(s, qn, qr, kn, kr, v, o):
        p = probs_of(s, pl.program_id(0) * QB, qn[...], qr[...], kn[...], kr[...])
        o[...] = dot(p.astype(BF), v[...]).astype(BF)

    rows = lambda w: pl.BlockSpec((QB, w), lambda i: (i, 0))
    full = lambda w: pl.BlockSpec((LEN, w), lambda i: (0, 0))
    return pl.pallas_call(
        kernel,
        grid=(LEN // QB,),
        out_shape=sds((LEN, VDIM), BF),
        in_specs=[SM, rows(NOPE), rows(ROPE), full(NOPE), full(ROPE), full(VDIM)],
        out_specs=rows(VDIM),
        compiler_params=pltpu.CompilerParams(vmem_limit_bytes=14 * MB),
        cost_estimate=LIGHT,
    )(starts, qn, qr, kn, kr, v)


def half_turn(v):
    return jnp.concatenate([v[:, ROPE // 2 :], v[:, : ROPE // 2]], axis=1)


def attend_back(starts, qn, qr, kn, kr, v, mg, cos2, sin2):
    def kernel(s, qn, qr, kn, kr, v, mg, cos, sin, qg, eg, rg, dkn, dkr, dv):
        step = pl.program_id(0)

        @pl.when(step == 0)
        def _():
            dkn[...] = jnp.zeros_like(dkn)
            dkr[...] = jnp.zeros_like(dkr)
            dv[...] = jnp.zeros_like(dv)

        p = probs_of(s, step * QB, qn[...], qr[...], kn[...], kr[...])
        m = mg[...]
        pg = dot(m, v[...], NT)
        sg = (p * (pg - jnp.sum(pg * p, axis=-1, keepdims=True))).astype(BF)
        qg[:, :NOPE] = (dot(sg, kn[...]) * SCALE).astype(BF)
        dqr = dot(sg, kr[...]) * SCALE
        rows = pl.ds(step * QB, QB)
        qg[:, NOPE:] = (dqr * cos[rows, :] - half_turn(dqr) * sin[rows, :]).astype(BF)
        dkn[...] += dot(sg, qn[...], TN) * SCALE
        dkr[...] += dot(sg, qr[...], TN) * SCALE
        dv[...] += dot(p.astype(BF), m, TN)

        @pl.when(step == LEN // QB - 1)
        def _():
            eg[:, :NOPE] = dkn[...].astype(BF)
            eg[:, NOPE:] = dv[...].astype(BF)
            d = dkr[...]
            rg[...] = (d * cos[...] - half_turn(d) * sin[...]).astype(BF)

    rows = lambda w: pl.BlockSpec((QB, w), lambda i: (i, 0))
    full = lambda w: pl.BlockSpec((LEN, w), lambda i: (0, 0))
    return pl.pallas_call(
        kernel,
        grid=(LEN // QB,),
        out_shape=[sds((LEN, w), BF) for w in (NOPE + ROPE, NOPE + VDIM, ROPE)],
        in_specs=[SM, rows(NOPE), rows(ROPE), full(NOPE), full(ROPE), full(VDIM), rows(VDIM), full(ROPE), full(ROPE)],
        out_specs=[rows(NOPE + ROPE), full(NOPE + VDIM), full(ROPE)],
        scratch_shapes=[pltpu.VMEM((LEN, w), F32) for w in (NOPE, ROPE, VDIM)],
        compiler_params=pltpu.CompilerParams(vmem_limit_bytes=18 * MB),
        cost_estimate=LIGHT,
    )(starts, qn, qr, kn, kr, v, mg, cos2, sin2)


def keys(normed1, place, lat_half, lat_other, gain, w_expand, cos2, sin2):
    n = lat_half.shape[0]

    def kernel(n1, place, a, b, gain, we, cos, sin, wl, lat, inv, comp, kn, kr, v):
        @pl.when(pl.program_id(0) == 0)
        def _():
            wl[...] = (dot(place[:, :n], a[...]) + dot(place[:, n:], b[...])).astype(BF)

        t = dot(n1[...], wl[...], NT).astype(BF)
        lat[...] = t
        t = t.astype(F32)
        c = t[:, :LATENT]
        r = lax.rsqrt(jnp.mean(c * c, axis=-1, keepdims=True) + EPS)
        c = (c * r * gain[...]).astype(BF)
        inv[...] = r
        comp[...] = c
        e = dot(c, we[...]).astype(BF)
        kn[...] = e[:, :NOPE]
        v[...] = e[:, NOPE:]
        d = t[:, LATENT : LATENT + ROPE]
        kr[...] = (d * cos[...] + half_turn(d) * sin[...]).astype(BF)

    rows = lambda w: pl.BlockSpec((QB, w), lambda i: (i, 0))
    full = lambda a: pl.BlockSpec(a.shape, lambda i: (0, 0))
    outs = [(LX, BF), (1, F32), (LATENT, BF), (NOPE, BF), (ROPE, BF), (VDIM, BF)]
    return pl.pallas_call(
        kernel,
        grid=(LEN // QB,),
        out_shape=[sds((LX, D), BF)] + [sds((LEN, w), t) for w, t in outs],
        in_specs=[rows(D), full(place), full(lat_half), full(lat_other), full(gain), full(w_expand), rows(ROPE), rows(ROPE)],
        out_specs=[pl.BlockSpec((LX, D), lambda i: (0, 0))] + [rows(w) for w, _ in outs],
        compiler_params=pltpu.CompilerParams(vmem_limit_bytes=26 * MB),
        cost_estimate=LIGHT,
    )(normed1, place, lat_half, lat_other, gain, w_expand, cos2, sin2)


def attention_part(which, mixed, w_out):
    def kernel(which, m, w, o):
        o[...] = dot(m[...], w[...]).astype(BF)

    return pl.pallas_call(
        kernel,
        grid_spec=pltpu.PrefetchScalarGridSpec(
            num_scalar_prefetch=1,
            grid=(2,),
            in_specs=[
                pl.BlockSpec((QB, VDIM), lambda i, which: (which[0] * 2 + i, 0)),
                pl.BlockSpec((VDIM, D), lambda i, which: (0, 0)),
            ],
            out_specs=pl.BlockSpec((QB, D), lambda i, which: (i, 0)),
        ),
        out_shape=sds((LEN // 2, D), BF),
        compiler_params=pltpu.CompilerParams(vmem_limit_bytes=16 * MB),
        cost_estimate=LIGHT,
    )(which, mixed, w_out)


def softmax(logits):
    e = jnp.exp(logits - jnp.max(logits, axis=-1, keepdims=True))
    return e / jnp.sum(e, axis=-1, keepdims=True)


def total_of(refs):
    t = refs[0][...].astype(F32)
    for r in refs[1:]:
        t = t + r[...].astype(F32)
    return t


def rows_mid(terms, x, gain, w_router):
    def kernel(a, b, x, gain, wr, hid, nrm, inv, probs):
        h = x[...].astype(F32) + total_of((a, b))
        r = lax.rsqrt(jnp.mean(h * h, axis=-1, keepdims=True) + EPS)
        n = (h * r * gain[...]).astype(BF)
        hid[...] = h
        nrm[...] = n
        inv[...] = r
        probs[...] = softmax(dot(n, wr[...]))

    outs = [sds((RB, D), F32), sds((RB, D), BF), sds((RB, 1), F32), sds((RB, EXPERTS), F32)]
    return whole(kernel, outs, [*terms, x, gain, w_router], 16)


def experts_front(starts, me, half, other, w_router, w_router_t, rank_row, grad, gu, dn):
    def kernel(s, me, a, b, wr, wrt, rank, g, gu, dn, n2, col, x, dy, dyg, dw, out, dx):
        lane = lax.broadcasted_iota(jnp.int32, (1, EXPERTS), 1)
        for n, ref in enumerate((a, b)):
            p = softmax(dot(ref[...], wr[...]))
            p = jnp.sum(jnp.where(lane == me[0], p, 0.0), axis=-1, keepdims=True)
            for i in range(4):
                rows = pl.ds(pl.multiple_of(s[n * 4 + i], RB), RB)
                n2[rows, :] = ref[i * RB : (i + 1) * RB]
                col[rows, :] = p[i * RB : (i + 1) * RB]
        nv, gv = n2[...], g[...]
        t = dot(wrt[...], nv, NT)
        t = jnp.exp(t - jnp.max(t, axis=0, keepdims=True))
        t = t / jnp.sum(t, axis=0, keepdims=True)
        mine = lax.broadcasted_iota(jnp.int32, (EXPERTS, 1), 0) == me[0]
        row = jnp.sum(jnp.where(mine, t, 0.0), axis=0, keepdims=True)
        hit = lax.broadcasted_iota(jnp.int32, (CAP, 1), 0) == rank[...]
        gate = jnp.sum(jnp.where(hit, row, 0.0), axis=-1, keepdims=True)
        pick = jnp.where(hit, 1.0, 0.0).astype(BF)
        x[...] = dot(pick, nv).astype(BF)
        got = dot(pick, gv)
        dyg[...] = got.astype(BF)
        dy[...] = (got * gate).astype(BF)
        h, da = ffn_back(nv, gv, gu[...], dn[...])
        dw[: 2 * FS] = dot(da, nv).astype(BF)
        dw[2 * FS :] = dot(h, gv).astype(BF)
        out[...] = dot(h, dn[...], TN).astype(BF)
        dx[...] = dot(da, gu[...], TN).astype(BF)

    outs = [sds((LEN, D), BF), sds((LEN, 1), F32)] + [sds((CAP, D), BF)] * 3
    outs += [sds((FA, D), BF)] + [sds((LEN, D), BF)] * 2
    ins = [(starts, SM), (me, SM), half, other, w_router, w_router_t, rank_row, grad, gu, dn]
    return whole(kernel, outs, ins, 56)


ANY = pl.BlockSpec(memory_space=pl.ANY)
FLOPS = 2 * 9 * FS * D


def ffn_back(x, dy, gu, dn):
    act = dot(gu, x, NT)
    g, u = act[:FS], act[FS:]
    sg = jax.nn.sigmoid(g)
    h = (g * sg * u).astype(BF)
    dh = dot(dn, dy, NT)
    dg = (dh * u * sg * (1.0 + g * (1.0 - sg))).astype(BF)
    du = (dh * g * sg).astype(BF)
    return h, jnp.concatenate([dg, du], axis=0)


def experts(x, dy, chunks, last=None):
    n = len(chunks)
    n_in = 2 if last is None else 6
    pieces = [(i, first, a) for i, c in enumerate(chunks) for first, a in zip((0, 2 * FS), c)]
    m = len(pieces)

    def kernel(*refs):
        if last is None:
            x, dy = refs[:2]
        else:
            me, x, dy, dyg, out0, dx0 = refs[:6]
        w, outs, (out, dx) = refs[n_in : n_in + m], refs[n_in + m : n_in + 2 * m], refs[n_in + 2 * m : n_in + 2 * m + 2]
        wgu, wdn, hs, das, grads, sem_in, sem_out = refs[n_in + 2 * m + 2 :]
        loads = [[] for _ in range(n)]
        for k, (i, first, a) in enumerate(pieces):
            for part, (size, ref) in enumerate(((2 * FS, wgu), (FS, wdn))):
                at = 2 * FS * part - first
                if 0 <= at < a.shape[0]:
                    src = w[k].at[pl.ds(at, size)]
                    loads[i].append(
                        pltpu.make_async_copy(src, ref.at[pl.ds(size * i, size)], sem_in.at[2 * i + part])
                    )
        for c in loads:
            for d in c:
                d.start()
        xv, dyv = x[...], dy[...]
        stores = []
        for i in range(n):
            for c in loads[i]:
                c.wait()
            h, da = ffn_back(xv, dyv, wgu[2 * FS * i : 2 * FS * (i + 1)], wdn[FS * i : FS * (i + 1)])
            hs[FS * i : FS * (i + 1)] = h
            das[2 * FS * i : 2 * FS * (i + 1)] = da
            grads[i, : 2 * FS] = dot(da, xv).astype(BF)
            grads[i, 2 * FS :] = dot(h, dyv).astype(BF)
            for k, (o, first, a) in enumerate(pieces):
                if o == i:
                    src = grads.at[i, pl.ds(first, a.shape[0])]
                    stores.append(pltpu.make_async_copy(src, outs[k], sem_out.at[k]))
                    stores[-1].start()
        sum_o = dot(hs[...], wdn[...], TN)
        sum_d = dot(das[...], wgu[...], TN)
        if last is None:
            out[...] = sum_o
            dx[...] = sum_d
        else:
            so = (out0[...] + sum_o).astype(BF)
            out[...] = so
            dx[:, :D] = (dx0[...] + sum_d).astype(BF)
            gg = jnp.sum(so.astype(F32) * dyg[...].astype(F32), axis=-1, keepdims=True)
            lane = lax.broadcasted_iota(jnp.int32, (1, 128), 1)
            dx[:, D:] = jnp.where(lane == me[0], gg, 0.0).astype(BF)
        for c in stores:
            c.wait()

    if last is None:
        arrays, specs = [x, dy], [VM] * 2
        ends = [sds((CAP, D), F32)] * 2
    else:
        dyg, out, dx, me = last
        arrays, specs = [me, x, dy, dyg, out, dx], [SM] + [VM] * 5
        ends = [sds((CAP, D), BF), sds((CAP, PW), BF)]
    res = pl.pallas_call(
        kernel,
        out_shape=[sds(a.shape, BF) for _, _, a in pieces] + ends,
        in_specs=specs + [ANY] * m,
        out_specs=[ANY] * m + [VM] * 2,
        scratch_shapes=[
            pltpu.VMEM((2 * FS * n, D), BF),
            pltpu.VMEM((FS * n, D), BF),
            pltpu.VMEM((FS * n, CAP), BF),
            pltpu.VMEM((2 * FS * n, CAP), BF),
            pltpu.VMEM((n, FA, D), BF),
            pltpu.SemaphoreType.DMA((2 * n,)),
            pltpu.SemaphoreType.DMA((m,)),
        ],
        compiler_params=pltpu.CompilerParams(vmem_limit_bytes=52 * MB),
        cost_estimate=LIGHT,
    )(*arrays, *[a for _, _, a in pieces])
    return res[:m], res[m], res[m + 1]


def combine_grad(which, rank_col, dx, shared_dx):
    rows_at = 256

    def kernel(which, rank, dx, sd, o):
        hit = rank[...] == lax.broadcasted_iota(jnp.int32, (1, CAP), 1)
        pick = jnp.where(hit, 1.0, 0.0).astype(BF)
        t = dot(pick, dx[...])
        o[:, :D] = (t[:, :D] + sd[...].astype(F32)).astype(BF)
        o[:, D:] = t[:, D:].astype(BF)

    at = lambda w: pl.BlockSpec((rows_at, w), lambda i, which: (which[0] * 2 + i, 0))
    return pl.pallas_call(
        kernel,
        grid_spec=pltpu.PrefetchScalarGridSpec(
            num_scalar_prefetch=1,
            grid=(2,),
            in_specs=[at(1), pl.BlockSpec((CAP, PW), lambda i, which: (0, 0)), at(D)],
            out_specs=pl.BlockSpec((rows_at, PW), lambda i, which: (i, 0)),
        ),
        out_shape=sds((LEN // 2, PW), BF),
        compiler_params=pltpu.CompilerParams(vmem_limit_bytes=40 * MB),
        cost_estimate=LIGHT,
    )(which, rank_col, dx, shared_dx)


def combine_out(rank_col, probs_col, slot_out, shared_out, mixed, w_out):
    rows_at = 256

    def kernel(rank, probs, so, sh, m, w, o):
        hit = rank[...] == lax.broadcasted_iota(jnp.int32, (1, CAP), 1)
        pick = jnp.where(hit, 1.0, 0.0).astype(BF)
        t = dot(pick, so[...]) * probs[...] + sh[...].astype(F32)
        t = (t + dot(m[...], w[...])).astype(BF)
        for i in range(D // 128):
            o[i] = t[:, 128 * i : 128 * (i + 1)]

    at = lambda w: pl.BlockSpec((rows_at, w), lambda i: (i, 0))
    return pl.pallas_call(
        kernel,
        grid=(LEN // rows_at,),
        out_shape=sds((D // 128, LEN, 128), BF),
        in_specs=[
            at(1),
            at(1),
            pl.BlockSpec((CAP, D), lambda i: (0, 0)),
            at(D),
            at(VDIM),
            pl.BlockSpec((VDIM, D), lambda i: (0, 0)),
        ],
        out_specs=pl.BlockSpec((D // 128, rows_at, 128), lambda i: (0, i, 0)),
        compiler_params=pltpu.CompilerParams(vmem_limit_bytes=24 * MB),
        cost_estimate=LIGHT,
    )(rank_col, probs_col, slot_out, shared_out, mixed, w_out)


def normed1_part(which, query_grad, expanded_grad, rope_grad, w_query, w_expand):
    rows_at = 256

    def kernel(which, q, e, r, wq, we, o):
        o[:, :D] = dot(q[...], wq[...]).astype(BF)
        o[:, D : D + LATENT] = dot(e[...], we[...], NT).astype(BF)
        o[:, D + LATENT :] = jnp.concatenate([r[...], jnp.zeros((rows_at, LX - LATENT - ROPE), BF)], axis=1)

    at = lambda w: pl.BlockSpec((rows_at, w), lambda i, which: (which[0] * 2 + i, 0))
    full = lambda a: pl.BlockSpec(a.shape, lambda i, which: (0, 0))
    return pl.pallas_call(
        kernel,
        grid_spec=pltpu.PrefetchScalarGridSpec(
            num_scalar_prefetch=1,
            grid=(2,),
            in_specs=[at(NOPE + ROPE), at(NOPE + VDIM), at(ROPE), full(w_query), full(w_expand)],
            out_specs=pl.BlockSpec((rows_at, QW), lambda i, which: (i, 0)),
        ),
        out_shape=sds((LEN // 2, QW), BF),
        compiler_params=pltpu.CompilerParams(vmem_limit_bytes=14 * MB),
        cost_estimate=LIGHT,
    )(which, query_grad, expanded_grad, rope_grad, w_query, w_expand)


def norm_back(v, inv, gain, incoming):
    weighted = incoming * gain
    inner = jnp.mean(weighted * v, axis=-1, keepdims=True)
    return inv * weighted - v * (inv * inv * inv) * inner, jnp.sum(incoming * v * inv, axis=0, keepdims=True)


def rows_two(terms, hidden, inv, probs, grad, gain, w_router_t):
    def kernel(a, b, h, inv, p, g, gain, wr, hg, pay, gg):
        t = total_of((a, b))
        gates = t[:, D : D + EXPERTS]
        pv = p[...]
        lg = (pv * (gates - jnp.sum(pv * gates, axis=-1, keepdims=True))).astype(BF)
        n2 = t[:, :D] + dot(lg, wr[...])
        r, gain_grad = norm_back(h[...], inv[...], gain[...], n2)
        r = r + g[...].astype(F32)
        hg[...] = r
        pay[:, :D] = r.astype(BF)
        pay[:, D:] = jnp.concatenate([lg, jnp.zeros((RB, 128 - EXPERTS), BF)], axis=1)
        gg[...] = gain_grad

    outs = [sds((RB, D), F32), sds((RB, PW), BF), sds((1, D), F32)]
    return whole(kernel, outs, [*terms, hidden, inv, probs, grad, gain, w_router_t], 16)


GAINS = 2 * D + LATENT
FREE = LX - LATENT - ROPE


def rows_one(terms, w_lat, x, inv, hg, gain, latent, inv_lat, gain_lat, gain_two):
    def kernel(a, b, wl, x, inv, hg, gain, lat, inv_lat, gain_lat, two, o):
        t = total_of((a, b))
        head, g_lat = norm_back(lat[:, :LATENT].astype(F32), inv_lat[...], gain_lat[...], t[:, D : D + LATENT])
        lg = jnp.concatenate([head, t[:, D + LATENT :]], axis=1).astype(BF)
        t = t[:, :D] + dot(lg, wl[...])
        r, g_one = norm_back(x[...].astype(F32), inv[...], gain[...], t)
        o[:, :D] = (hg[...] + r).astype(BF)
        o[:, D : D + LATENT] = lg[:, :LATENT]
        g = jnp.concatenate([g_one, two[...], g_lat], axis=1)
        g = [g[:, FREE * i : FREE * (i + 1)] for i in range(GAINS // FREE)]
        g = jnp.concatenate(g + [jnp.zeros((RB - len(g), FREE), F32)], axis=0)
        o[:, D + LATENT :] = jnp.concatenate([lg[:, LATENT : LATENT + ROPE], g.astype(BF)], axis=1)

    ins = [*terms, w_lat, x, inv, hg, gain, latent, inv_lat, gain_lat, gain_two]
    return whole(kernel, [sds((RB, QW), BF)], ins, 20)[0]


def mixed_back(starts, half, other, w_out):
    def kernel(s, a, b, w, o):
        for n, ref in enumerate((a, b)):
            t = dot(ref[:, :D], w[...], NT).astype(BF)
            for i in range(4):
                rows = pl.ds(pl.multiple_of(s[n * 4 + i], RB), RB)
                o[rows, :] = t[i * RB : (i + 1) * RB]

    return whole(kernel, [sds((LEN, VDIM), BF)], [(starts, SM), half, other, w_out], 16, 2 * LEN * D * VDIM)[0]


def output_grads(starts, half, other, mixed, normed2):
    def kernel(s, a, b, m, n2, wo, wr):
        sum_o = jnp.zeros((VDIM, D), F32)
        sum_r = jnp.zeros((EXPERTS, D), F32)
        for n, ref in enumerate((a, b)):
            at = [pl.ds(pl.multiple_of(s[n * 4 + i], RB), RB) for i in range(4)]
            mix = jnp.concatenate([m[r, :] for r in at], axis=0)
            sum_o = sum_o + dot(mix, ref[:, :D], TN)
            for i, r in enumerate(at):
                lg = ref[i * RB : (i + 1) * RB, D:]
                sum_r = sum_r + dot(lg, n2[r, :], TN)[:EXPERTS]
        wo[...] = sum_o.astype(BF)
        wr[...] = sum_r.astype(BF)

    outs = [sds((VDIM, D), BF), sds((EXPERTS, D), BF)]
    return whole(kernel, outs, [(starts, SM), half, other, mixed, normed2], 24, 2 * LEN * D * 256)


def column_blocks(offsets, blocks):
    for i, ref in enumerate(blocks):
        for j in range(2):
            off = pl.multiple_of(offsets[2 * i + j], 256)
            yield off, lambda a, b, ref=ref, j=j: ref[a:b, 256 * j : 256 * (j + 1)].astype(F32)


def finish_rest(offsets, blocks):
    def kernel(off, *refs):
        wq, wo, we, wr = refs[4:]
        for at, block in column_blocks(off, refs[:4]):
            cols = pl.ds(at, 256)
            wq[:, cols] = block(0, 192)
            wo[:, cols] = block(192, 320)
            we[pl.ds(pl.multiple_of(at // 4, 64), 64), :] = block(320, 384)
            wr[:, cols] = block(384, 400)

    outs = [sds((192, D), F32), sds((VDIM, D), F32), sds((LATENT, 256), F32), sds((EXPERTS, D), F32)]
    return whole(kernel, outs, [(offsets, SM), *blocks], 16)


def finish_shared(offsets, near, far):
    def kernel(off, a, b, gate, up, down):
        refs = [r.at[:, 512 * i : 512 * (i + 1)] for r in (a, b) for i in range(2)]
        for at, block in column_blocks(off, refs):
            cols = pl.ds(at, 256)
            gate[:, cols] = block(0, FS)
            up[:, cols] = block(FS, 2 * FS)
            down[:, cols] = block(2 * FS, 3 * FS)

    return whole(kernel, [sds((FS, D), F32)] * 3, [(offsets, SM), near, far], 16)


def finish_experts(gu, dn):
    def kernel(*refs):
        gu, dn, (gate, up, down) = refs[:5], refs[5:10], refs[10:]
        t = total_of(gu)
        gate[...] = t[:FS]
        up[...] = t[FS:]
        down[...] = total_of(dn)

    return whole(kernel, [sds((FS, D), F32)] * 3, [*gu, *dn], 24)


def latent_w_grad(starts, half, other, normed1, pick):
    def kernel(s, a, b, n1, pick, o, gains, parts):
        total = jnp.zeros((LW48, D), F32)
        for n, ref in enumerate((a, b)):
            at = [pl.multiple_of(s[n * 4 + i], RB) for i in range(4)]
            rows = jnp.concatenate([n1[pl.ds(r, RB), :] for r in at], axis=0)
            own = dot(pick[...], ref[:, D:], NT).astype(BF)
            total = total + dot(own, rows)
            for i, r in enumerate(at):
                parts[pl.ds(r, RB), :] = ref[i * RB : (i + 1) * RB, QW - 128 :].astype(F32)
        o[...] = total.astype(BF)
        g = parts[:RB]
        for i in range(1, LEN // RB):
            g = g + parts[i * RB : (i + 1) * RB]
        gains[...] = g

    return pl.pallas_call(
        kernel,
        out_shape=[sds((LW48, D), BF), sds((RB, 128), F32)],
        in_specs=[SM, VM, VM, VM, VM],
        out_specs=[VM, VM],
        scratch_shapes=[pltpu.VMEM((LEN, 128), F32)],
        compiler_params=pltpu.CompilerParams(vmem_limit_bytes=24 * MB),
        cost_estimate=LIGHT,
    )(starts, half, other, normed1, pick)


def spread(starts, half, other):
    def kernel(s, a, b, o):
        for n, ref in enumerate((a, b)):
            for i in range(4):
                rows = pl.ds(pl.multiple_of(s[n * 4 + i], RB), RB)
                o[rows, :] = ref[i * RB : (i + 1) * RB, :D].astype(F32)

    return whole(kernel, [sds((LEN, D), F32)], [(starts, SM), half, other], 24)[0]


def local(
    tokens,
    cotangent,
    expert_ids,
    slot_order,
    image_starts,
    norm1_gain,
    w_query,
    w_latent,
    latent_gain,
    w_expand,
    w_output,
    norm2_gain,
    w_router,
    expert_gate,
    expert_up,
    expert_down,
    shared_gate,
    shared_up,
    shared_down,
):
    tr = lax.axis_index("tensor")
    dr = lax.axis_index("dp")
    zh, yy, cc = tr // 8, tr // 2 % 4, tr % 2
    peers = [((yy + y) % 4, (cc + c) % 2) for c in range(2) for y in range(4)]
    starts8 = jnp.stack([(c * 4 + y) * RB for y, c in peers]).astype(jnp.int32)
    starts4 = jnp.stack([y * RB for y, c in peers[:4]]).astype(jnp.int32)
    own_row = (cc * 4 + yy) * RB
    own_rows = lambda a: lax.dynamic_slice_in_dim(a, own_row, RB, 0)
    me = jnp.full((1,), tr, jnp.int32)

    half_at = lambda k: jnp.full((1,), k, jnp.int32)
    half_rows = lambda a, k: lax.dynamic_slice_in_dim(a, k * (LEN // 2), LEN // 2, 0)

    x, z = dr // 2, dr % 2

    lat_t = w_latent.T
    lat_z = recv_t(lat_t, zh=1)
    own_gu = cat(expert_gate[0].T, expert_up[0].T)
    own_dn = expert_down[0].T
    resid = tokens.astype(F32)
    inv1 = lax.rsqrt(jnp.mean(resid * resid, axis=-1, keepdims=True) + EPS)
    normed1 = (resid * inv1 * norm1_gain).astype(BF)
    lat_z, lat_t, own_gu, own_dn, normed1 = sync(lat_z, lat_t, own_gu, own_dn, normed1)

    lat = jnp.pad(cat(lat_t, lat_z), [(0, LP - 2 * LW), (0, 0)])
    lat_y = from_y(lat)
    ap_dn, zz_dn = recv_d(own_dn, x=1), recv_d(own_dn, z=1)
    chosen = jnp.any(expert_ids == tr, axis=1)
    order = slot_order[0]
    token = jnp.arange(LEN, dtype=jnp.int32)
    place = jnp.sum(jnp.where(order[:, None] == token[None, :], token[:, None], 0), axis=0)
    before = (place[:, None] < place[None, :]) & chosen[:, None]
    rank = jnp.sum(before.astype(jnp.int32), axis=0)
    rank = jnp.where(chosen, rank, -1)
    rank_row, rank_col = rank[None, :], rank[:, None]
    cos, sin = rotary_tables(LEN)
    cos2, sin2 = jnp.concatenate([cos, cos], axis=1), jnp.concatenate([-sin, sin], axis=1)
    w_query_t = w_query.T
    query = dot(normed1, w_query_t, NT)
    qn = query[:, :NOPE].astype(BF)
    qr = rotate(query[:, NOPE:], cos, sin).astype(BF)
    column = jnp.arange(LP, dtype=jnp.int32)
    owner = jnp.stack([(zh + column // LW) % 2 * 8 + y * 2 + c for y, c in peers])
    target = jnp.where(column < 2 * LW, owner * LW + column % LW, -1).reshape(-1)
    lat_place = (jnp.arange(LX, dtype=jnp.int32)[:, None] == target[None, :]).astype(BF)
    lat, *lat_y, ap_dn, zz_dn, qn, qr, rank_row, rank_col, cotangent, own_gu, own_dn, lat_place, cos2, sin2 = sync(
        lat, *lat_y, ap_dn, zz_dn, qn, qr, rank_row, rank_col, cotangent, own_gu, own_dn, lat_place, cos2, sin2
    )

    lat_half = cat(lat, *lat_y)
    lat_other = recv_t(lat_half, c=1)
    zz_gu, ap_gu, am_gu = recv_d(own_gu, z=1), recv_d(own_gu, x=1), recv_d(own_gu, x=-1)
    out_grad = lax.all_gather(cotangent, "tensor", axis=1, tiled=True)
    sh_gu = cat(shared_gate.T, shared_up.T)
    lat_half, lat_other, sh_gu = sync(lat_half, lat_other, sh_gu)

    w_lat, latent, inv_lat, compressed, kn, kr, v = keys(
        normed1, lat_place, lat_half, lat_other, latent_gain[None, :], w_expand, cos2, sin2
    )
    mixed = attend(image_starts, qn, qr, kn, kr, v)
    at_send = attention_part(half_at(1 - cc), mixed, w_output)
    at_send, zz_gu, ap_gu, am_gu, own_dn, own_gu = sync(at_send, zz_gu, ap_gu, am_gu, own_dn, own_gu)
    at_got = recv_t(at_send, c=1)
    at_keep = attention_part(half_at(cc), mixed, w_output)
    bp_gu, am_dn = recv_d(ap_gu, z=1), recv_d(own_dn, x=-1)
    at_got, at_keep, own_gu = sync(at_got, at_keep, own_gu)

    at_b = split_sum(at_keep, at_got, starts4)
    at_y = to_y(at_b)
    a2_gu = recv_d(own_gu, x=2)
    *at_y, bp_gu, am_dn, ap_dn, own_dn, am_gu = sync(*at_y, bp_gu, am_dn, ap_dn, own_dn, am_gu)
    at_sum = add(at_b[0], *at_y)
    at_other = recv_t(at_sum, zh=1)
    at_sum, at_other, ap_dn, am_gu, own_dn = sync(at_sum, at_other, ap_dn, am_gu, own_dn)
    hidden, rows2, inv2, probs = rows_mid((at_sum, at_other), own_rows(tokens), norm2_gain[None, :], w_router)
    n2_y = from_y(rows2)
    bp_dn, bm_gu = recv_d(ap_dn, z=1), recv_d(am_gu, z=1)
    rows2, *n2_y, bp_dn, a2_gu, own_dn, am_dn, zz_gu, zz_dn = sync(
        rows2, *n2_y, bp_dn, a2_gu, own_dn, am_dn, zz_gu, zz_dn
    )
    n2_half = cat(rows2, *n2_y)
    n2_other = recv_t(n2_half, c=1)
    a2_dn, bm_dn = recv_d(own_dn, x=2), recv_d(am_dn, z=1)
    b2_gu = recv_d(zz_gu, x=2)
    w_router_t = w_router.T
    n2_half, n2_other, out_grad, rank_row, w_router_t = sync(n2_half, n2_other, out_grad, rank_row, w_router_t)

    normed2, probs_col, slots, dy, dyg, sh_sum, s_out, s_dx = experts_front(
        starts8, me, n2_half, n2_other, w_router, w_router_t, rank_row, out_grad, sh_gu, shared_down
    )
    slots, dy, a2_dn, bm_gu, zz_dn, own_gu = sync(slots, dy, a2_dn, bm_gu, zz_dn, own_gu)
    b2_dn = recv_d(zz_dn, x=2)
    near, part_out, part_dx = experts(
        slots, dy, [(own_gu, own_dn), (ap_gu, ap_dn), (am_gu, am_dn), (zz_gu, zz_dn)]
    )
    sh_half, sh_send = halves(sh_sum, x // 2)
    part_out, part_dx, bm_dn, b2_gu, b2_dn, sh_half, sh_send = sync(
        part_out, part_dx, bm_dn, b2_gu, b2_dn, sh_half, sh_send
    )
    sh_got = recv_d(sh_send, x=2)
    far, slot_out, dx = experts(
        slots,
        dy,
        [(a2_gu, a2_dn), (bp_gu, bp_dn), (b2_gu, b2_dn), (bm_gu, bm_dn)],
        (dyg, part_out, part_dx, me),
    )
    g_own_gu, g_own_dn, g_ap_gu, g_ap_dn, g_am_gu, g_am_dn, g_z_gu, g_z_dn = near
    g_a2_gu, g_a2_dn, g_bp_gu, g_bp_dn, g_b2_gu, g_b2_dn, g_bm_gu, g_bm_dn = far
    dx, sh_half, sh_got, g_b2_gu, g_bp_gu, slot_out = sync(dx, sh_half, sh_got, g_b2_gu, g_bp_gu, slot_out)

    n2_send = combine_grad(half_at(1 - cc), rank_col, dx, s_dx)
    n2_send, g_b2_gu, g_bp_gu, slot_out = sync(n2_send, g_b2_gu, g_bp_gu, slot_out)
    n2_got = recv_t(n2_send, c=1)
    branch = combine_out(rank_col, probs_col, slot_out, s_out, mixed, w_output)
    n2_keep = combine_grad(half_at(cc), rank_col, dx, s_dx)
    r_b2_gu, r_bp_gu = recv_d(g_b2_gu, x=2), recv_d(g_bp_gu, z=1)
    n2_got, n2_keep, branch, sh_half, sh_got = sync(n2_got, n2_keep, branch, sh_half, sh_got)
    branch_sum = lax.psum_scatter(branch.reshape(-1, 128), "tensor", scatter_dimension=0, tiled=True)
    n2_b = split_sum(n2_keep, n2_got, starts4)
    n2_y = to_y(n2_b)
    sh_keep, sh_send = halves(add(sh_half, sh_got), x % 2)
    sh_got = swap_x(sh_send)
    *n2_y, r_b2_gu, r_bp_gu, g_b2_dn, g_bp_dn, g_a2_gu, sh_keep, sh_got = sync(
        *n2_y, r_b2_gu, r_bp_gu, g_b2_dn, g_bp_dn, g_a2_gu, sh_keep, sh_got
    )
    sh_sum = add(sh_keep, sh_got)
    n2_sum = add(n2_b[0], *n2_y)
    n2_other = recv_t(n2_sum, zh=1)
    r_b2_dn = recv_d(g_b2_dn, x=2)
    n2_sum, n2_other, g_bp_dn, g_a2_gu, r_b2_dn, sh_sum, g_bm_gu = sync(
        n2_sum, n2_other, g_bp_dn, g_a2_gu, r_b2_dn, sh_sum, g_bm_gu
    )

    hid_grad, payload, gain2 = rows_two(
        (n2_sum, n2_other), hidden, inv2, probs, own_rows(out_grad), norm2_gain[None, :], w_router_t
    )
    p_y = from_y(payload)
    r_bp_dn, r_a2_gu = recv_d(g_bp_dn, z=1), recv_d(g_a2_gu, x=2)
    sh_keep, sh_send = halves(sh_sum, z)
    sh_z = recv_d(sh_send, z=1)
    z_gu_sum, ap_gu_sum, z_dn_sum = add(g_z_gu, r_b2_gu), add(g_ap_gu, r_bp_gu), add(g_z_dn, r_b2_dn)
    payload, *p_y, r_bp_dn, g_bm_gu, r_a2_gu, g_a2_dn, sh_keep, sh_z, z_gu_sum, ap_gu_sum, z_dn_sum = sync(
        payload, *p_y, r_bp_dn, g_bm_gu, r_a2_gu, g_a2_dn, sh_keep, sh_z, z_gu_sum, ap_gu_sum, z_dn_sum
    )
    pay_half = cat(payload, *p_y)
    pay_other = recv_t(pay_half, c=1)
    sh_own = add(sh_keep, sh_z)
    sh_pair = recv_d(sh_own, z=1)
    r_a2_dn = recv_d(g_a2_dn, x=2)
    pay_half, pay_other, g_bm_gu, sh_own, sh_pair = sync(pay_half, pay_other, g_bm_gu, sh_own, sh_pair)
    r_bm_gu = recv_d(g_bm_gu, z=1)
    mixed_grad = mixed_back(starts8, pay_half, pay_other, w_output)
    sh_pair = jnp.concatenate([sh_own, sh_pair], axis=1)
    sh_next = swap_x(sh_pair)
    w_out_g, w_router_g = output_grads(starts8, pay_half, pay_other, mixed, normed2)

    query_grad, expanded_grad, rope_grad = attend_back(image_starts, qn, qr, kn, kr, v, mixed_grad, cos2, sin2)
    n1_send = normed1_part(half_at(1 - cc), query_grad, expanded_grad, rope_grad, w_query_t, w_expand)
    n1_send, r_a2_dn, r_bm_gu, sh_pair, sh_next, z_gu_sum = sync(n1_send, r_a2_dn, r_bm_gu, sh_pair, sh_next, z_gu_sum)
    n1_got = recv_t(n1_send, c=1)
    n1_keep = normed1_part(half_at(cc), query_grad, expanded_grad, rope_grad, w_query_t, w_expand)
    r_z_gu = recv_d(z_gu_sum, z=1)
    n1_got, n1_keep, query_grad, expanded_grad, ap_gu_sum, g_am_gu, sh_pair, sh_next = sync(
        n1_got, n1_keep, query_grad, expanded_grad, ap_gu_sum, g_am_gu, sh_pair, sh_next
    )
    n1_b = split_sum(n1_keep, n1_got, starts4)
    n1_y1, n1_y3 = recv_t(n1_b[1], y=-1), recv_t(n1_b[3], y=1)
    r_ap_gu = recv_d(ap_gu_sum, x=-1)

    w_query_g = dot(query_grad, normed1, TN).astype(BF)
    w_expand_g = dot(compressed, expanded_grad, TN).astype(BF)
    w_expand_g = jnp.concatenate([w_expand_g[64 * i : 64 * (i + 1)] for i in range(8)], axis=1)
    rest = cat(w_query_g, w_out_g, w_expand_g, w_router_g)
    rest_half, rest_send = halves(rest, x // 2)
    rest_got = recv_d(rest_send, x=2)
    n1_y1, n1_y3, n1_b2, rest_half, g_am_gu, g_ap_dn, sh_pair = sync(
        n1_y1, n1_y3, n1_b[2], rest_half, g_am_gu, g_ap_dn, sh_pair
    )
    n1_y2 = recv_t(n1_b2, y=2)
    am_gu_sum, ap_dn_sum = add(g_am_gu, r_bm_gu), add(g_ap_dn, r_bp_dn)
    r_am_gu = recv_d(am_gu_sum, x=1)
    sh_near = jnp.concatenate([sh_pair, sh_next], axis=1)
    n1_y1, n1_y3, n1_y2, rest_half, rest_got, r_z_gu, r_ap_gu, ap_dn_sum, sh_near = sync(
        n1_y1, n1_y3, n1_y2, rest_half, rest_got, r_z_gu, r_ap_gu, ap_dn_sum, sh_near
    )
    n1_sum = add(n1_b[0], n1_y1, n1_y2, n1_y3)
    n1_other = recv_t(n1_sum, zh=1)
    rest_keep, rest_send = halves(add(rest_half, rest_got), x % 2)
    rest_got = swap_x(rest_send)
    n1_sum, n1_other, rest_keep, rest_got, sh_near = sync(n1_sum, n1_other, rest_keep, rest_got, sh_near)
    sh_far = recv_d(sh_near, x=2)
    tok_rows = rows_one(
        (n1_sum, n1_other),
        w_lat,
        own_rows(tokens),
        own_rows(inv1),
        hid_grad,
        norm1_gain[None, :],
        own_rows(latent),
        own_rows(inv_lat),
        latent_gain[None, :],
        gain2,
    )
    t1, t3 = recv_t(tok_rows, y=1), recv_t(tok_rows, y=-1)
    rest_keep, rest_send = halves(add(rest_keep, rest_got), z)
    rest_got = recv_d(rest_send, z=1)
    tok_rows, t1, t3, rest_keep, rest_got, r_am_gu, g_bm_dn, ap_dn_sum = sync(
        tok_rows, t1, t3, rest_keep, rest_got, r_am_gu, g_bm_dn, ap_dn_sum
    )
    t2 = recv_t(tok_rows, y=2)
    rest_own = add(rest_keep, rest_got)
    rest_pair = recv_d(rest_own, z=1)
    r_bm_dn, r_ap_dn = recv_d(g_bm_dn, z=1), recv_d(ap_dn_sum, x=-1)
    tok_rows, t1, t2, t3, rest_own, rest_pair, sh_far, r_ap_dn = sync(
        tok_rows, t1, t2, t3, rest_own, rest_pair, sh_far, r_ap_dn
    )
    tok_half = cat(tok_rows, t1, t2, t3)
    tok_other = recv_t(tok_half, c=1)
    pair = jnp.concatenate([rest_own, rest_pair], axis=1)
    blocks = [pair] + [recv_d(pair, x=i) for i in (1, 2, 3)]
    tok_half, tok_other, r_bm_dn, g_am_dn, z_dn_sum = sync(tok_half, tok_other, r_bm_dn, g_am_dn, z_dn_sum)
    pick = (
        (jnp.arange(LX, dtype=jnp.int32)[None, :] == tr * LW + column[:LW48, None]) & (column[:LW48, None] < LW)
    ).astype(BF)
    offsets = jnp.stack([((x + i) % 4 * 2 + (z + j) % 2) * 256 for i in range(4) for j in range(2)])
    w_lat_g, gains = latent_w_grad(starts8, tok_half, tok_other, normed1, pick)
    gains = jnp.pad(gains[: GAINS // FREE, 128 - FREE :].reshape(-1), (0, 16 * D - GAINS)).reshape(16, D)
    small = cat(w_lat_g, gains.astype(BF))
    small, z_dn_sum, g_am_dn, r_bm_dn, tok_half = sync(small, z_dn_sum, g_am_dn, r_bm_dn, tok_half)
    small = sum_d(small, 0)
    tokens_grad = spread(starts8, tok_half, tok_other)
    small, tokens_grad, z_dn_sum, g_am_dn, *blocks = sync(small, tokens_grad, z_dn_sum, g_am_dn, *blocks)
    small = sum_d(small, 1)
    r_z_dn, r_am_dn = recv_d(z_dn_sum, z=1), recv_d(add(g_am_dn, r_bm_dn), x=1)
    wq_grad, wo_grad, we_grad, wr_grad = finish_rest(offsets, blocks)
    sh_offsets = jnp.stack([((x ^ i) * 2 + (z + j) % 2) * 256 for i in range(4) for j in range(2)])
    sg_grad, su_grad, sd_grad = finish_shared(sh_offsets, sh_near, sh_far)
    small, sg_grad, su_grad, sd_grad = sync(small, sg_grad, su_grad, sd_grad)
    small = sum_d(small, 2).astype(F32)
    eg_grad, eu_grad, ed_grad = finish_experts(
        (g_own_gu, r_a2_gu, r_ap_gu, r_am_gu, r_z_gu), (g_own_dn, r_a2_dn, r_ap_dn, r_am_dn, r_z_dn)
    )
    gains = small[LW48:].reshape(-1)

    own_cols = lax.dynamic_slice_in_dim(tokens, tr * 128, 128, 1)
    output = (own_cols.astype(F32) + branch_sum.astype(F32)).astype(BF)
    return (
        output,
        tokens_grad,
        gains[:D],
        wq_grad.T,
        small[:LW].T,
        gains[2 * D : GAINS],
        we_grad,
        wo_grad,
        gains[D : 2 * D],
        wr_grad.T,
        eg_grad.T[None],
        eu_grad.T[None],
        ed_grad.T[None],
        sg_grad.T,
        su_grad.T,
        sd_grad,
    )


def solution(mesh):
    in_specs = (
        P("dp", None),
        P("dp", "tensor"),
        P("dp", None),
        P("dp", None),
        P("dp", None),
        P(),
        P(None, "tensor"),
        P(None, "tensor"),
        P(),
        P(None, "tensor"),
        P("tensor", None),
        P(),
        P(),
        P("tensor", None, "dp"),
        P("tensor", None, "dp"),
        P("tensor", None, "dp"),
        P(None, "tensor"),
        P(None, "tensor"),
        P("tensor", None),
    )
    out_specs = (
        P("dp", "tensor"),
        P("dp", None),
        P(),
        P(None, "tensor"),
        P(None, "tensor"),
        P(),
        P(None, "tensor"),
        P("tensor", None),
        P(),
        P(),
        P("tensor", None, "dp"),
        P("tensor", None, "dp"),
        P("tensor", None, "dp"),
        P(None, "tensor"),
        P(None, "tensor"),
        P("tensor", None),
    )
    return jax.shard_map(local, mesh=mesh, in_specs=in_specs, out_specs=out_specs, check_vma=False)
```

```python
import functools
import math

import jax
import jax.numpy as jnp
from jax import lax
from jax.experimental import pallas as pl
from jax.experimental.pallas import tpu as pltpu
from jax.sharding import PartitionSpec as P

D = 2048
NOPE = 128
ROPE = 64
VDIM = 128
LATENT = 512
TOPK = 6
EXPERTS = 16
IMG = 256
SPANS = 2
LEN = 1024
CAP = 480
FS = 176
LW = 36
LW48 = 48
LP = 80
LX = 640
RB = 128
PW = D + 128
QW = D + LX
FA = 3 * FS
BF = jnp.bfloat16
F32 = jnp.float32
EPS = 1e-06
MASKED = -1e30
SCALE = (NOPE + ROPE) ** (-0.5)
MB = 1024 * 1024

NN = (((1,), (0,)), ((), ()))
NT = (((1,), (1,)), ((), ()))
TN = (((0,), (0,)), ((), ()))


def dot(a, b, dims=NN):
    return lax.dot_general(a, b, dims, preferred_element_type=F32)


VM = pl.BlockSpec(memory_space=pltpu.VMEM)
SM = pl.BlockSpec(memory_space=pltpu.SMEM)


def whole(kernel, outs, ins, limit, flops=0):
    arrays = [i[0] if isinstance(i, tuple) else i for i in ins]
    specs = [i[1] if isinstance(i, tuple) else VM for i in ins]
    return pl.pallas_call(
        kernel,
        out_shape=outs,
        in_specs=specs,
        out_specs=[VM] * len(outs),
        compiler_params=pltpu.CompilerParams(vmem_limit_bytes=limit * MB),
        cost_estimate=LIGHT,
    )(*arrays)


LIGHT = pl.CostEstimate(flops=1, bytes_accessed=1, transcendentals=0)


def sds(shape, dtype):
    return jax.ShapeDtypeStruct(shape, dtype)


def recv_t(a, zh=0, y=0, c=0):
    pairs = []
    for i in range(16):
        z, r, k = i // 8, i // 2 % 4, i % 2
        pairs.append((((z + zh) % 2) * 8 + ((r + y) % 4) * 2 + (k + c) % 2, i))
    return lax.ppermute(a, "tensor", pairs)


def recv_d(a, x=0, z=0):
    pairs = []
    for i in range(8):
        pairs.append((((i // 2 + x) % 4) * 2 + (i % 2 + z) % 2, i))
    return lax.ppermute(a, "dp", pairs)


def stack(*arrays):
    n = arrays[0].shape[0]

    def kernel(*refs):
        for i, r in enumerate(refs[:-1]):
            refs[-1][n * i : n * (i + 1)] = r[...]

    shape = (n * len(arrays), arrays[0].shape[1])
    return whole(kernel, [sds(shape, BF)], list(arrays), 12)[0]


def from_y(a):
    y1, y3 = recv_t(a, y=1), recv_t(a, y=-1)
    across, y1, y3 = sync(a, y1, y3)
    return [y1, recv_t(across, y=2), y3]


def to_y(b):
    y1, y3 = recv_t(b[1], y=-1), recv_t(b[3], y=1)
    across, y1, y3 = sync(b[2], y1, y3)
    return [y1, recv_t(across, y=2), y3]


def cat(*arrays):
    return jnp.concatenate(arrays, axis=0)


def split_sum(keep, got, starts):
    width = keep.shape[1]

    def kernel(s, a, b, *outs):
        for i, o in enumerate(outs):
            rows = pl.ds(pl.multiple_of(s[i], RB), RB)
            o[...] = (a[rows, :].astype(F32) + b[rows, :].astype(F32)).astype(BF)

    return whole(kernel, [sds((RB, width), BF)] * 4, [(starts, SM), keep, got], 16)


def add(*terms):
    return sum(t.astype(F32) for t in terms).astype(BF)


def swap_x(a):
    return lax.ppermute(a, "dp", [(i, ((i // 2) ^ 1) * 2 + i % 2) for i in range(8)])


def halves(a, k):
    n = a.shape[1] // 2
    return lax.dynamic_slice_in_dim(a, k * n, n, 1), lax.dynamic_slice_in_dim(a, (1 - k) * n, n, 1)


def sum_d(v, turn):
    if turn == 0:
        got = recv_d(v, z=1)
    elif turn == 1:
        got = swap_x(v)
    else:
        got = recv_d(v, x=2)
    return (v.astype(F32) + got.astype(F32)).astype(v.dtype)


def sync(*arrays):
    return lax.optimization_barrier(arrays)


def rotary_tables(length):
    position = jnp.arange(length, dtype=F32)
    frequency = jnp.exp(jnp.arange(ROPE // 2, dtype=F32) * (-2.0 * math.log(10000.0) / ROPE))
    angles = position[:, None] * frequency[None, :]
    return jnp.cos(angles), jnp.sin(angles)


def rotate(v, cos, sin):
    a, b = v[:, : ROPE // 2], v[:, ROPE // 2 :]
    return jnp.concatenate([a * cos - b * sin, b * cos + a * sin], axis=-1)


def unrotate(v, cos, sin):
    a, b = v[:, : ROPE // 2], v[:, ROPE // 2 :]
    return jnp.concatenate([a * cos + b * sin, b * cos - a * sin], axis=-1)


QB = 256


def probs_of(starts, first, qn, qr, kn, kr):
    scores = (dot(qn, kn, NT) + dot(qr, kr, NT)) * SCALE
    i = first + lax.broadcasted_iota(jnp.int32, (QB, 1), 0)
    j = lax.broadcasted_iota(jnp.int32, (1, LEN), 1)
    allowed = j <= i
    for n in range(SPANS):
        s = starts[0, n]
        row_in = (i >= s) & (i < s + IMG)
        col_in = (j >= s) & (j < s + IMG)
        allowed = allowed | (row_in & col_in)
    scores = jnp.where(allowed, scores, MASKED)
    raised = jnp.exp(scores - jnp.max(scores, axis=-1, keepdims=True))
    return raised / jnp.sum(raised, axis=-1, keepdims=True)


def attend(starts, qn, qr, kn, kr, v):
    def kernel(s, qn, qr, kn, kr, v, o):
        p = probs_of(s, pl.program_id(0) * QB, qn[...], qr[...], kn[...], kr[...])
        o[...] = dot(p.astype(BF), v[...]).astype(BF)

    rows = lambda w: pl.BlockSpec((QB, w), lambda i: (i, 0))
    full = lambda w: pl.BlockSpec((LEN, w), lambda i: (0, 0))
    return pl.pallas_call(
        kernel,
        grid=(LEN // QB,),
        out_shape=sds((LEN, VDIM), BF),
        in_specs=[SM, rows(NOPE), rows(ROPE), full(NOPE), full(ROPE), full(VDIM)],
        out_specs=rows(VDIM),
        compiler_params=pltpu.CompilerParams(vmem_limit_bytes=14 * MB),
        cost_estimate=LIGHT,
    )(starts, qn, qr, kn, kr, v)


def half_turn(v):
    return jnp.concatenate([v[:, ROPE // 2 :], v[:, : ROPE // 2]], axis=1)


def attend_back(starts, qn, qr, kn, kr, v, mg, cos2, sin2):
    def kernel(s, qn, qr, kn, kr, v, mg, cos, sin, qg, eg, rg, dkn, dkr, dv):
        step = pl.program_id(0)

        @pl.when(step == 0)
        def _():
            dkn[...] = jnp.zeros_like(dkn)
            dkr[...] = jnp.zeros_like(dkr)
            dv[...] = jnp.zeros_like(dv)

        p = probs_of(s, step * QB, qn[...], qr[...], kn[...], kr[...])
        m = mg[...]
        pg = dot(m, v[...], NT)
        sg = (p * (pg - jnp.sum(pg * p, axis=-1, keepdims=True))).astype(BF)
        qg[:, :NOPE] = (dot(sg, kn[...]) * SCALE).astype(BF)
        dqr = dot(sg, kr[...]) * SCALE
        rows = pl.ds(step * QB, QB)
        qg[:, NOPE:] = (dqr * cos[rows, :] - half_turn(dqr) * sin[rows, :]).astype(BF)
        dkn[...] += dot(sg, qn[...], TN) * SCALE
        dkr[...] += dot(sg, qr[...], TN) * SCALE
        dv[...] += dot(p.astype(BF), m, TN)

        @pl.when(step == LEN // QB - 1)
        def _():
            eg[:, :NOPE] = dkn[...].astype(BF)
            eg[:, NOPE:] = dv[...].astype(BF)
            d = dkr[...]
            rg[...] = (d * cos[...] - half_turn(d) * sin[...]).astype(BF)

    rows = lambda w: pl.BlockSpec((QB, w), lambda i: (i, 0))
    full = lambda w: pl.BlockSpec((LEN, w), lambda i: (0, 0))
    return pl.pallas_call(
        kernel,
        grid=(LEN // QB,),
        out_shape=[sds((LEN, w), BF) for w in (NOPE + ROPE, NOPE + VDIM, ROPE)],
        in_specs=[SM, rows(NOPE), rows(ROPE), full(NOPE), full(ROPE), full(VDIM), rows(VDIM), full(ROPE), full(ROPE)],
        out_specs=[rows(NOPE + ROPE), full(NOPE + VDIM), full(ROPE)],
        scratch_shapes=[pltpu.VMEM((LEN, w), F32) for w in (NOPE, ROPE, VDIM)],
        compiler_params=pltpu.CompilerParams(vmem_limit_bytes=18 * MB),
        cost_estimate=LIGHT,
    )(starts, qn, qr, kn, kr, v, mg, cos2, sin2)


def keys(normed1, place, lat_half, lat_other, gain, w_expand, cos2, sin2):
    n = lat_half.shape[0]

    def kernel(n1, place, a, b, gain, we, cos, sin, wl, lat, inv, comp, kn, kr, v):
        @pl.when(pl.program_id(0) == 0)
        def _():
            wl[...] = (dot(place[:, :n], a[...]) + dot(place[:, n:], b[...])).astype(BF)

        t = dot(n1[...], wl[...], NT).astype(BF)
        lat[...] = t
        t = t.astype(F32)
        c = t[:, :LATENT]
        r = lax.rsqrt(jnp.mean(c * c, axis=-1, keepdims=True) + EPS)
        c = (c * r * gain[...]).astype(BF)
        inv[...] = r
        comp[...] = c
        e = dot(c, we[...]).astype(BF)
        kn[...] = e[:, :NOPE]
        v[...] = e[:, NOPE:]
        d = t[:, LATENT : LATENT + ROPE]
        kr[...] = (d * cos[...] + half_turn(d) * sin[...]).astype(BF)

    rows = lambda w: pl.BlockSpec((QB, w), lambda i: (i, 0))
    full = lambda a: pl.BlockSpec(a.shape, lambda i: (0, 0))
    outs = [(LX, BF), (1, F32), (LATENT, BF), (NOPE, BF), (ROPE, BF), (VDIM, BF)]
    return pl.pallas_call(
        kernel,
        grid=(LEN // QB,),
        out_shape=[sds((LX, D), BF)] + [sds((LEN, w), t) for w, t in outs],
        in_specs=[rows(D), full(place), full(lat_half), full(lat_other), full(gain), full(w_expand), rows(ROPE), rows(ROPE)],
        out_specs=[pl.BlockSpec((LX, D), lambda i: (0, 0))] + [rows(w) for w, _ in outs],
        compiler_params=pltpu.CompilerParams(vmem_limit_bytes=26 * MB),
        cost_estimate=LIGHT,
    )(normed1, place, lat_half, lat_other, gain, w_expand, cos2, sin2)


def attention_part(which, mixed, w_out):
    def kernel(which, m, w, o):
        o[...] = dot(m[...], w[...]).astype(BF)

    return pl.pallas_call(
        kernel,
        grid_spec=pltpu.PrefetchScalarGridSpec(
            num_scalar_prefetch=1,
            grid=(2,),
            in_specs=[
                pl.BlockSpec((QB, VDIM), lambda i, which: (which[0] * 2 + i, 0)),
                pl.BlockSpec((VDIM, D), lambda i, which: (0, 0)),
            ],
            out_specs=pl.BlockSpec((QB, D), lambda i, which: (i, 0)),
        ),
        out_shape=sds((LEN // 2, D), BF),
        compiler_params=pltpu.CompilerParams(vmem_limit_bytes=16 * MB),
        cost_estimate=LIGHT,
    )(which, mixed, w_out)


def softmax(logits):
    e = jnp.exp(logits - jnp.max(logits, axis=-1, keepdims=True))
    return e / jnp.sum(e, axis=-1, keepdims=True)


def total_of(refs):
    t = refs[0][...].astype(F32)
    for r in refs[1:]:
        t = t + r[...].astype(F32)
    return t


def rows_mid(terms, x, gain, w_router):
    def kernel(a, b, x, gain, wr, hid, nrm, inv, probs):
        h = x[...].astype(F32) + total_of((a, b))
        r = lax.rsqrt(jnp.mean(h * h, axis=-1, keepdims=True) + EPS)
        n = (h * r * gain[...]).astype(BF)
        hid[...] = h
        nrm[...] = n
        inv[...] = r
        probs[...] = softmax(dot(n, wr[...]))

    outs = [sds((RB, D), F32), sds((RB, D), BF), sds((RB, 1), F32), sds((RB, EXPERTS), F32)]
    return whole(kernel, outs, [*terms, x, gain, w_router], 16)


def experts_front(starts, me, half, other, w_router, w_router_t, rank_row, grad, gu, dn):
    def kernel(s, me, a, b, wr, wrt, rank, g, gu, dn, n2, col, x, dy, dyg, dw, out, dx):
        lane = lax.broadcasted_iota(jnp.int32, (1, EXPERTS), 1)
        for n, ref in enumerate((a, b)):
            p = softmax(dot(ref[...], wr[...]))
            p = jnp.sum(jnp.where(lane == me[0], p, 0.0), axis=-1, keepdims=True)
            for i in range(4):
                rows = pl.ds(pl.multiple_of(s[n * 4 + i], RB), RB)
                n2[rows, :] = ref[i * RB : (i + 1) * RB]
                col[rows, :] = p[i * RB : (i + 1) * RB]
        nv, gv = n2[...], g[...]
        t = dot(wrt[...], nv, NT)
        t = jnp.exp(t - jnp.max(t, axis=0, keepdims=True))
        t = t / jnp.sum(t, axis=0, keepdims=True)
        mine = lax.broadcasted_iota(jnp.int32, (EXPERTS, 1), 0) == me[0]
        row = jnp.sum(jnp.where(mine, t, 0.0), axis=0, keepdims=True)
        hit = lax.broadcasted_iota(jnp.int32, (CAP, 1), 0) == rank[...]
        gate = jnp.sum(jnp.where(hit, row, 0.0), axis=-1, keepdims=True)
        pick = jnp.where(hit, 1.0, 0.0).astype(BF)
        x[...] = dot(pick, nv).astype(BF)
        got = dot(pick, gv)
        dyg[...] = got.astype(BF)
        dy[...] = (got * gate).astype(BF)
        h, da = ffn_back(nv, gv, gu[...], dn[...])
        dw[: 2 * FS] = dot(da, nv).astype(BF)
        dw[2 * FS :] = dot(h, gv).astype(BF)
        out[...] = dot(h, dn[...], TN).astype(BF)
        dx[...] = dot(da, gu[...], TN).astype(BF)

    outs = [sds((LEN, D), BF), sds((LEN, 1), F32)] + [sds((CAP, D), BF)] * 3
    outs += [sds((FA, D), BF)] + [sds((LEN, D), BF)] * 2
    ins = [(starts, SM), (me, SM), half, other, w_router, w_router_t, rank_row, grad, gu, dn]
    return whole(kernel, outs, ins, 56)


ANY = pl.BlockSpec(memory_space=pl.ANY)
FLOPS = 2 * 9 * FS * D


def ffn_back(x, dy, gu, dn):
    act = dot(gu, x, NT)
    g, u = act[:FS], act[FS:]
    sg = jax.nn.sigmoid(g)
    h = (g * sg * u).astype(BF)
    dh = dot(dn, dy, NT)
    dg = (dh * u * sg * (1.0 + g * (1.0 - sg))).astype(BF)
    du = (dh * g * sg).astype(BF)
    return h, jnp.concatenate([dg, du], axis=0)


def experts(x, dy, chunks, last=None):
    n = len(chunks)
    n_in = 2 if last is None else 6
    pieces = [(i, first, a) for i, c in enumerate(chunks) for first, a in zip((0, 2 * FS), c)]
    m = len(pieces)

    def kernel(*refs):
        if last is None:
            x, dy = refs[:2]
        else:
            me, x, dy, dyg, out0, dx0 = refs[:6]
        w, outs, (out, dx) = refs[n_in : n_in + m], refs[n_in + m : n_in + 2 * m], refs[n_in + 2 * m : n_in + 2 * m + 2]
        wgu, wdn, hs, das, grads, sem_in, sem_out = refs[n_in + 2 * m + 2 :]
        loads = [[] for _ in range(n)]
        for k, (i, first, a) in enumerate(pieces):
            for part, (size, ref) in enumerate(((2 * FS, wgu), (FS, wdn))):
                at = 2 * FS * part - first
                if 0 <= at < a.shape[0]:
                    src = w[k].at[pl.ds(at, size)]
                    loads[i].append(
                        pltpu.make_async_copy(src, ref.at[pl.ds(size * i, size)], sem_in.at[2 * i + part])
                    )
        for c in loads:
            for d in c:
                d.start()
        xv, dyv = x[...], dy[...]
        stores = []
        for i in range(n):
            for c in loads[i]:
                c.wait()
            h, da = ffn_back(xv, dyv, wgu[2 * FS * i : 2 * FS * (i + 1)], wdn[FS * i : FS * (i + 1)])
            hs[FS * i : FS * (i + 1)] = h
            das[2 * FS * i : 2 * FS * (i + 1)] = da
            grads[i, : 2 * FS] = dot(da, xv).astype(BF)
            grads[i, 2 * FS :] = dot(h, dyv).astype(BF)
            for k, (o, first, a) in enumerate(pieces):
                if o == i:
                    src = grads.at[i, pl.ds(first, a.shape[0])]
                    stores.append(pltpu.make_async_copy(src, outs[k], sem_out.at[k]))
                    stores[-1].start()
        sum_o = dot(hs[...], wdn[...], TN)
        sum_d = dot(das[...], wgu[...], TN)
        if last is None:
            out[...] = sum_o
            dx[...] = sum_d
        else:
            so = (out0[...] + sum_o).astype(BF)
            out[...] = so
            dx[:, :D] = (dx0[...] + sum_d).astype(BF)
            gg = jnp.sum(so.astype(F32) * dyg[...].astype(F32), axis=-1, keepdims=True)
            lane = lax.broadcasted_iota(jnp.int32, (1, 128), 1)
            dx[:, D:] = jnp.where(lane == me[0], gg, 0.0).astype(BF)
        for c in stores:
            c.wait()

    if last is None:
        arrays, specs = [x, dy], [VM] * 2
        ends = [sds((CAP, D), F32)] * 2
    else:
        dyg, out, dx, me = last
        arrays, specs = [me, x, dy, dyg, out, dx], [SM] + [VM] * 5
        ends = [sds((CAP, D), BF), sds((CAP, PW), BF)]
    res = pl.pallas_call(
        kernel,
        out_shape=[sds(a.shape, BF) for _, _, a in pieces] + ends,
        in_specs=specs + [ANY] * m,
        out_specs=[ANY] * m + [VM] * 2,
        scratch_shapes=[
            pltpu.VMEM((2 * FS * n, D), BF),
            pltpu.VMEM((FS * n, D), BF),
            pltpu.VMEM((FS * n, CAP), BF),
            pltpu.VMEM((2 * FS * n, CAP), BF),
            pltpu.VMEM((n, FA, D), BF),
            pltpu.SemaphoreType.DMA((2 * n,)),
            pltpu.SemaphoreType.DMA((m,)),
        ],
        compiler_params=pltpu.CompilerParams(vmem_limit_bytes=52 * MB),
        cost_estimate=LIGHT,
    )(*arrays, *[a for _, _, a in pieces])
    return res[:m], res[m], res[m + 1]


def combine_grad(which, rank_col, dx, shared_dx):
    rows_at = 256

    def kernel(which, rank, dx, sd, o):
        hit = rank[...] == lax.broadcasted_iota(jnp.int32, (1, CAP), 1)
        pick = jnp.where(hit, 1.0, 0.0).astype(BF)
        t = dot(pick, dx[...])
        o[:, :D] = (t[:, :D] + sd[...].astype(F32)).astype(BF)
        o[:, D:] = t[:, D:].astype(BF)

    at = lambda w: pl.BlockSpec((rows_at, w), lambda i, which: (which[0] * 2 + i, 0))
    return pl.pallas_call(
        kernel,
        grid_spec=pltpu.PrefetchScalarGridSpec(
            num_scalar_prefetch=1,
            grid=(2,),
            in_specs=[at(1), pl.BlockSpec((CAP, PW), lambda i, which: (0, 0)), at(D)],
            out_specs=pl.BlockSpec((rows_at, PW), lambda i, which: (i, 0)),
        ),
        out_shape=sds((LEN // 2, PW), BF),
        compiler_params=pltpu.CompilerParams(vmem_limit_bytes=40 * MB),
        cost_estimate=LIGHT,
    )(which, rank_col, dx, shared_dx)


def combine_out(rank_col, probs_col, slot_out, shared_out, mixed, w_out):
    rows_at = 256

    def kernel(rank, probs, so, sh, m, w, o):
        hit = rank[...] == lax.broadcasted_iota(jnp.int32, (1, CAP), 1)
        pick = jnp.where(hit, 1.0, 0.0).astype(BF)
        t = dot(pick, so[...]) * probs[...] + sh[...].astype(F32)
        t = (t + dot(m[...], w[...])).astype(BF)
        for i in range(D // 128):
            o[i] = t[:, 128 * i : 128 * (i + 1)]

    at = lambda w: pl.BlockSpec((rows_at, w), lambda i: (i, 0))
    return pl.pallas_call(
        kernel,
        grid=(LEN // rows_at,),
        out_shape=sds((D // 128, LEN, 128), BF),
        in_specs=[
            at(1),
            at(1),
            pl.BlockSpec((CAP, D), lambda i: (0, 0)),
            at(D),
            at(VDIM),
            pl.BlockSpec((VDIM, D), lambda i: (0, 0)),
        ],
        out_specs=pl.BlockSpec((D // 128, rows_at, 128), lambda i: (0, i, 0)),
        compiler_params=pltpu.CompilerParams(vmem_limit_bytes=24 * MB),
        cost_estimate=LIGHT,
    )(rank_col, probs_col, slot_out, shared_out, mixed, w_out)


def normed1_part(which, query_grad, expanded_grad, rope_grad, w_query, w_expand):
    rows_at = 256

    def kernel(which, q, e, r, wq, we, o):
        o[:, :D] = dot(q[...], wq[...]).astype(BF)
        o[:, D : D + LATENT] = dot(e[...], we[...], NT).astype(BF)
        o[:, D + LATENT :] = jnp.concatenate([r[...], jnp.zeros((rows_at, LX - LATENT - ROPE), BF)], axis=1)

    at = lambda w: pl.BlockSpec((rows_at, w), lambda i, which: (which[0] * 2 + i, 0))
    full = lambda a: pl.BlockSpec(a.shape, lambda i, which: (0, 0))
    return pl.pallas_call(
        kernel,
        grid_spec=pltpu.PrefetchScalarGridSpec(
            num_scalar_prefetch=1,
            grid=(2,),
            in_specs=[at(NOPE + ROPE), at(NOPE + VDIM), at(ROPE), full(w_query), full(w_expand)],
            out_specs=pl.BlockSpec((rows_at, QW), lambda i, which: (i, 0)),
        ),
        out_shape=sds((LEN // 2, QW), BF),
        compiler_params=pltpu.CompilerParams(vmem_limit_bytes=14 * MB),
        cost_estimate=LIGHT,
    )(which, query_grad, expanded_grad, rope_grad, w_query, w_expand)


def norm_back(v, inv, gain, incoming):
    weighted = incoming * gain
    inner = jnp.mean(weighted * v, axis=-1, keepdims=True)
    return inv * weighted - v * (inv * inv * inv) * inner, jnp.sum(incoming * v * inv, axis=0, keepdims=True)


def rows_two(terms, hidden, inv, probs, grad, gain, w_router_t):
    def kernel(a, b, h, inv, p, g, gain, wr, hg, pay, gg):
        t = total_of((a, b))
        gates = t[:, D : D + EXPERTS]
        pv = p[...]
        lg = (pv * (gates - jnp.sum(pv * gates, axis=-1, keepdims=True))).astype(BF)
        n2 = t[:, :D] + dot(lg, wr[...])
        r, gain_grad = norm_back(h[...], inv[...], gain[...], n2)
        r = r + g[...].astype(F32)
        hg[...] = r
        pay[:, :D] = r.astype(BF)
        pay[:, D:] = jnp.concatenate([lg, jnp.zeros((RB, 128 - EXPERTS), BF)], axis=1)
        gg[...] = gain_grad

    outs = [sds((RB, D), F32), sds((RB, PW), BF), sds((1, D), F32)]
    return whole(kernel, outs, [*terms, hidden, inv, probs, grad, gain, w_router_t], 16)


GAINS = 2 * D + LATENT
FREE = LX - LATENT - ROPE


def rows_one(terms, w_lat, x, inv, hg, gain, latent, inv_lat, gain_lat, gain_two):
    def kernel(a, b, wl, x, inv, hg, gain, lat, inv_lat, gain_lat, two, o):
        t = total_of((a, b))
        head, g_lat = norm_back(lat[:, :LATENT].astype(F32), inv_lat[...], gain_lat[...], t[:, D : D + LATENT])
        lg = jnp.concatenate([head, t[:, D + LATENT :]], axis=1).astype(BF)
        t = t[:, :D] + dot(lg, wl[...])
        r, g_one = norm_back(x[...].astype(F32), inv[...], gain[...], t)
        o[:, :D] = (hg[...] + r).astype(BF)
        o[:, D : D + LATENT] = lg[:, :LATENT]
        g = jnp.concatenate([g_one, two[...], g_lat], axis=1)
        g = [g[:, FREE * i : FREE * (i + 1)] for i in range(GAINS // FREE)]
        g = jnp.concatenate(g + [jnp.zeros((RB - len(g), FREE), F32)], axis=0)
        o[:, D + LATENT :] = jnp.concatenate([lg[:, LATENT : LATENT + ROPE], g.astype(BF)], axis=1)

    ins = [*terms, w_lat, x, inv, hg, gain, latent, inv_lat, gain_lat, gain_two]
    return whole(kernel, [sds((RB, QW), BF)], ins, 20)[0]


def mixed_back(starts, half, other, w_out):
    def kernel(s, a, b, w, o):
        for n, ref in enumerate((a, b)):
            t = dot(ref[:, :D], w[...], NT).astype(BF)
            for i in range(4):
                rows = pl.ds(pl.multiple_of(s[n * 4 + i], RB), RB)
                o[rows, :] = t[i * RB : (i + 1) * RB]

    return whole(kernel, [sds((LEN, VDIM), BF)], [(starts, SM), half, other, w_out], 16, 2 * LEN * D * VDIM)[0]


def output_grads(starts, half, other, mixed, normed2):
    def kernel(s, a, b, m, n2, wo, wr):
        sum_o = jnp.zeros((VDIM, D), F32)
        sum_r = jnp.zeros((EXPERTS, D), F32)
        for n, ref in enumerate((a, b)):
            at = [pl.ds(pl.multiple_of(s[n * 4 + i], RB), RB) for i in range(4)]
            mix = jnp.concatenate([m[r, :] for r in at], axis=0)
            sum_o = sum_o + dot(mix, ref[:, :D], TN)
            for i, r in enumerate(at):
                lg = ref[i * RB : (i + 1) * RB, D:]
                sum_r = sum_r + dot(lg, n2[r, :], TN)[:EXPERTS]
        wo[...] = sum_o.astype(BF)
        wr[...] = sum_r.astype(BF)

    outs = [sds((VDIM, D), BF), sds((EXPERTS, D), BF)]
    return whole(kernel, outs, [(starts, SM), half, other, mixed, normed2], 24, 2 * LEN * D * 256)


def column_blocks(offsets, blocks):
    for i, ref in enumerate(blocks):
        for j in range(2):
            off = pl.multiple_of(offsets[2 * i + j], 256)
            yield off, lambda a, b, ref=ref, j=j: ref[a:b, 256 * j : 256 * (j + 1)].astype(F32)


def finish_rest(offsets, blocks):
    def kernel(off, *refs):
        wq, wo, we, wr = refs[4:]
        for at, block in column_blocks(off, refs[:4]):
            cols = pl.ds(at, 256)
            wq[:, cols] = block(0, 192)
            wo[:, cols] = block(192, 320)
            we[pl.ds(pl.multiple_of(at // 4, 64), 64), :] = block(320, 384)
            wr[:, cols] = block(384, 400)

    outs = [sds((192, D), F32), sds((VDIM, D), F32), sds((LATENT, 256), F32), sds((EXPERTS, D), F32)]
    return whole(kernel, outs, [(offsets, SM), *blocks], 16)


def finish_shared(offsets, near, far):
    def kernel(off, a, b, gate, up, down):
        for i in range(8):
            ref, cols = (a, b)[i // 4], slice(256 * (i % 4), 256 * (i % 4 + 1))
            at = pl.ds(pl.multiple_of(off[i], 256), 256)
            gate[:, at] = ref[:FS, cols].astype(F32)
            up[:, at] = ref[FS : 2 * FS, cols].astype(F32)
            down[:, at] = ref[2 * FS :, cols].astype(F32)

    return whole(kernel, [sds((FS, D), F32)] * 3, [(offsets, SM), near, far], 16)


def finish_experts(gu, dn):
    def kernel(*refs):
        gu, dn, (gate, up, down) = refs[:5], refs[5:10], refs[10:]
        t = total_of(gu)
        gate[...] = t[:FS]
        up[...] = t[FS:]
        down[...] = total_of(dn)

    return whole(kernel, [sds((FS, D), F32)] * 3, [*gu, *dn], 24)


def latent_w_grad(starts, half, other, normed1, pick):
    def kernel(s, a, b, n1, pick, o, gains, parts):
        total = jnp.zeros((LW48, D), F32)
        for n, ref in enumerate((a, b)):
            at = [pl.multiple_of(s[n * 4 + i], RB) for i in range(4)]
            rows = jnp.concatenate([n1[pl.ds(r, RB), :] for r in at], axis=0)
            own = dot(pick[...], ref[:, D:], NT).astype(BF)
            total = total + dot(own, rows)
            for i, r in enumerate(at):
                parts[pl.ds(r, RB), :] = ref[i * RB : (i + 1) * RB, QW - 128 :].astype(F32)
        o[...] = total.astype(BF)
        g = parts[:RB]
        for i in range(1, LEN // RB):
            g = g + parts[i * RB : (i + 1) * RB]
        gains[...] = g

    return pl.pallas_call(
        kernel,
        out_shape=[sds((LW48, D), BF), sds((RB, 128), F32)],
        in_specs=[SM, VM, VM, VM, VM],
        out_specs=[VM, VM],
        scratch_shapes=[pltpu.VMEM((LEN, 128), F32)],
        compiler_params=pltpu.CompilerParams(vmem_limit_bytes=24 * MB),
        cost_estimate=LIGHT,
    )(starts, half, other, normed1, pick)


def spread(starts, half, other):
    def kernel(s, a, b, o):
        for n, ref in enumerate((a, b)):
            for i in range(4):
                rows = pl.ds(pl.multiple_of(s[n * 4 + i], RB), RB)
                o[rows, :] = ref[i * RB : (i + 1) * RB, :D].astype(F32)

    return whole(kernel, [sds((LEN, D), F32)], [(starts, SM), half, other], 24)[0]


def local(
    tokens,
    cotangent,
    expert_ids,
    slot_order,
    image_starts,
    norm1_gain,
    w_query,
    w_latent,
    latent_gain,
    w_expand,
    w_output,
    norm2_gain,
    w_router,
    expert_gate,
    expert_up,
    expert_down,
    shared_gate,
    shared_up,
    shared_down,
):
    tr = lax.axis_index("tensor")
    dr = lax.axis_index("dp")
    zh, yy, cc = tr // 8, tr // 2 % 4, tr % 2
    peers = [((yy + y) % 4, (cc + c) % 2) for c in range(2) for y in range(4)]
    starts8 = jnp.stack([(c * 4 + y) * RB for y, c in peers]).astype(jnp.int32)
    starts4 = jnp.stack([y * RB for y, c in peers[:4]]).astype(jnp.int32)
    own_row = (cc * 4 + yy) * RB
    own_rows = lambda a: lax.dynamic_slice_in_dim(a, own_row, RB, 0)
    me = jnp.full((1,), tr, jnp.int32)

    half_at = lambda k: jnp.full((1,), k, jnp.int32)
    half_rows = lambda a, k: lax.dynamic_slice_in_dim(a, k * (LEN // 2), LEN // 2, 0)

    x, z = dr // 2, dr % 2

    out_grad = lax.all_gather(cotangent, "tensor", axis=1, tiled=True)
    lat_t = w_latent.T
    lat_z = recv_t(lat_t, zh=1)
    own_gu = cat(expert_gate[0].T, expert_up[0].T)
    own_dn = expert_down[0].T
    resid = tokens.astype(F32)
    inv1 = lax.rsqrt(jnp.mean(resid * resid, axis=-1, keepdims=True) + EPS)
    normed1 = (resid * inv1 * norm1_gain).astype(BF)
    lat_z, lat_t, own_gu, own_dn, normed1 = sync(lat_z, lat_t, own_gu, own_dn, normed1)

    lat = jnp.pad(cat(lat_t, lat_z), [(0, LP - 2 * LW), (0, 0)])
    lat_y = from_y(lat)
    ap_dn, zz_dn = recv_d(own_dn, x=1), recv_d(own_dn, z=1)
    chosen = jnp.any(expert_ids == tr, axis=1)
    order = slot_order[0]
    token = jnp.arange(LEN, dtype=jnp.int32)
    place = jnp.sum(jnp.where(order[:, None] == token[None, :], token[:, None], 0), axis=0)
    before = (place[:, None] < place[None, :]) & chosen[:, None]
    rank = jnp.sum(before.astype(jnp.int32), axis=0)
    rank = jnp.where(chosen, rank, -1)
    rank_row, rank_col = rank[None, :], rank[:, None]
    cos, sin = rotary_tables(LEN)
    cos2, sin2 = jnp.concatenate([cos, cos], axis=1), jnp.concatenate([-sin, sin], axis=1)
    w_query_t = w_query.T
    query = dot(normed1, w_query_t, NT)
    qn = query[:, :NOPE].astype(BF)
    qr = rotate(query[:, NOPE:], cos, sin).astype(BF)
    column = jnp.arange(LP, dtype=jnp.int32)
    owner = jnp.stack([(zh + column // LW) % 2 * 8 + y * 2 + c for y, c in peers])
    target = jnp.where(column < 2 * LW, owner * LW + column % LW, -1).reshape(-1)
    lat_place = (jnp.arange(LX, dtype=jnp.int32)[:, None] == target[None, :]).astype(BF)
    lat, *lat_y, ap_dn, zz_dn, qn, qr, rank_row, rank_col, own_gu, own_dn, lat_place, cos2, sin2 = sync(
        lat, *lat_y, ap_dn, zz_dn, qn, qr, rank_row, rank_col, own_gu, own_dn, lat_place, cos2, sin2
    )

    lat_half = stack(lat, *lat_y)
    lat_other = recv_t(lat_half, c=1)
    zz_gu, ap_gu, am_gu = recv_d(own_gu, z=1), recv_d(own_gu, x=1), recv_d(own_gu, x=-1)
    sh_gu = cat(shared_gate.T, shared_up.T)
    lat_half, lat_other, sh_gu = sync(lat_half, lat_other, sh_gu)

    w_lat, latent, inv_lat, compressed, kn, kr, v = keys(
        normed1, lat_place, lat_half, lat_other, latent_gain[None, :], w_expand, cos2, sin2
    )
    mixed = attend(image_starts, qn, qr, kn, kr, v)
    at_send = attention_part(half_at(1 - cc), mixed, w_output)
    at_send, zz_gu, ap_gu, am_gu, own_dn, own_gu = sync(at_send, zz_gu, ap_gu, am_gu, own_dn, own_gu)
    at_got = recv_t(at_send, c=1)
    at_keep = attention_part(half_at(cc), mixed, w_output)
    bp_gu, am_dn = recv_d(ap_gu, z=1), recv_d(own_dn, x=-1)
    at_got, at_keep, own_gu = sync(at_got, at_keep, own_gu)

    at_b = split_sum(at_keep, at_got, starts4)
    at_y1, at_y3 = recv_t(at_b[1], y=-1), recv_t(at_b[3], y=1)
    at_y1, at_y3, at_b2, am_dn, own_gu = sync(at_y1, at_y3, at_b[2], am_dn, own_gu)
    at_y = [at_y1, recv_t(at_b2, y=2), at_y3]
    a2_gu = recv_d(own_gu, x=2)
    *at_y, bp_gu, ap_dn, own_dn, am_gu = sync(*at_y, bp_gu, ap_dn, own_dn, am_gu)
    at_sum = add(at_b[0], *at_y)
    at_other = recv_t(at_sum, zh=1)
    at_sum, at_other, ap_dn, am_gu, own_dn = sync(at_sum, at_other, ap_dn, am_gu, own_dn)
    hidden, rows2, inv2, probs = rows_mid((at_sum, at_other), own_rows(tokens), norm2_gain[None, :], w_router)
    n2_y1, n2_y3 = recv_t(rows2, y=1), recv_t(rows2, y=-1)
    bp_dn = recv_d(ap_dn, z=1)
    rows2, n2_y1, n2_y3, a2_gu, own_dn = sync(rows2, n2_y1, n2_y3, a2_gu, own_dn)
    n2_y2 = recv_t(rows2, y=2)
    a2_dn = recv_d(own_dn, x=2)
    rows2, n2_y1, n2_y2, n2_y3, bp_dn, am_gu, am_dn, zz_gu, zz_dn, a2_dn = sync(
        rows2, n2_y1, n2_y2, n2_y3, bp_dn, am_gu, am_dn, zz_gu, zz_dn, a2_dn
    )
    n2_y = [n2_y1, n2_y2, n2_y3]
    n2_half = stack(rows2, *n2_y)
    n2_other = recv_t(n2_half, c=1)
    bm_gu, bm_dn = recv_d(am_gu, z=1), recv_d(am_dn, z=1)
    b2_gu, b2_dn = recv_d(zz_gu, x=2), recv_d(zz_dn, x=2)
    w_router_t = w_router.T
    n2_half, n2_other, out_grad, rank_row, w_router_t = sync(n2_half, n2_other, out_grad, rank_row, w_router_t)

    normed2, probs_col, slots, dy, dyg, sh_sum, s_out, s_dx = experts_front(
        starts8, me, n2_half, n2_other, w_router, w_router_t, rank_row, out_grad, sh_gu, shared_down
    )
    near, part_out, part_dx = experts(
        slots, dy, [(own_gu, own_dn), (ap_gu, ap_dn), (am_gu, am_dn), (zz_gu, zz_dn)]
    )
    sh_half, sh_send = halves(sh_sum, z)
    part_out, part_dx, bm_gu, bm_dn, b2_gu, b2_dn, sh_half, sh_send = sync(
        part_out, part_dx, bm_gu, bm_dn, b2_gu, b2_dn, sh_half, sh_send
    )
    sh_got = recv_d(sh_send, z=1)
    far, slot_out, dx = experts(
        slots,
        dy,
        [(a2_gu, a2_dn), (bp_gu, bp_dn), (b2_gu, b2_dn), (bm_gu, bm_dn)],
        (dyg, part_out, part_dx, me),
    )
    g_own_gu, g_own_dn, g_ap_gu, g_ap_dn, g_am_gu, g_am_dn, g_z_gu, g_z_dn = near
    g_a2_gu, g_a2_dn, g_bp_gu, g_bp_dn, g_b2_gu, g_b2_dn, g_bm_gu, g_bm_dn = far
    dx, sh_half, sh_got, g_b2_gu, g_bp_gu, slot_out = sync(dx, sh_half, sh_got, g_b2_gu, g_bp_gu, slot_out)

    n2_send = combine_grad(half_at(1 - cc), rank_col, dx, s_dx)
    n2_send, g_b2_gu, g_bp_gu, slot_out = sync(n2_send, g_b2_gu, g_bp_gu, slot_out)
    n2_got = recv_t(n2_send, c=1)
    n2_keep = combine_grad(half_at(cc), rank_col, dx, s_dx)
    r_b2_gu, r_bp_gu = recv_d(g_b2_gu, x=2), recv_d(g_bp_gu, z=1)
    n2_got, n2_keep, slot_out, sh_half, sh_got = sync(n2_got, n2_keep, slot_out, sh_half, sh_got)
    n2_b = split_sum(n2_keep, n2_got, starts4)
    n2_y1, n2_y3 = recv_t(n2_b[1], y=-1), recv_t(n2_b[3], y=1)
    sh_keep, sh_send = halves(add(sh_half, sh_got), x // 2)
    branch = combine_out(rank_col, probs_col, slot_out, s_out, mixed, w_output)
    n2_y1, n2_y3, n2_b2, sh_keep, sh_send, g_b2_dn, branch = sync(
        n2_y1, n2_y3, n2_b[2], sh_keep, sh_send, g_b2_dn, branch
    )
    branch_sum = lax.psum_scatter(branch.reshape(-1, 128), "tensor", scatter_dimension=0, tiled=True)
    n2_y = [n2_y1, recv_t(n2_b2, y=2), n2_y3]
    r_b2_dn = recv_d(g_b2_dn, x=2)
    *n2_y, r_b2_gu, r_bp_gu, g_bp_dn, g_a2_gu = sync(*n2_y, r_b2_gu, r_bp_gu, g_bp_dn, g_a2_gu)
    n2_sum = add(n2_b[0], *n2_y)
    n2_other = recv_t(n2_sum, zh=1)
    r_a2_gu = recv_d(g_a2_gu, x=2)
    r_bm_gu = recv_d(g_bm_gu, z=1)
    n2_sum, n2_other, r_b2_dn, g_bp_dn, sh_keep, sh_send, r_b2_gu, r_bp_gu, g_z_gu, g_ap_gu, g_z_dn = sync(
        n2_sum, n2_other, r_b2_dn, g_bp_dn, sh_keep, sh_send, r_b2_gu, r_bp_gu, g_z_gu, g_ap_gu, g_z_dn
    )

    hid_grad, payload, gain2 = rows_two(
        (n2_sum, n2_other), hidden, inv2, probs, own_rows(out_grad), norm2_gain[None, :], w_router_t
    )
    p_y = from_y(payload)
    z_gu_sum, ap_gu_sum, z_dn_sum = add(g_z_gu, r_b2_gu), add(g_ap_gu, r_bp_gu), add(g_z_dn, r_b2_dn)
    payload, *p_y, r_bm_gu, r_a2_gu, g_a2_dn, g_bp_dn, sh_keep, sh_send, z_gu_sum, ap_gu_sum, z_dn_sum = sync(
        payload, *p_y, r_bm_gu, r_a2_gu, g_a2_dn, g_bp_dn, sh_keep, sh_send, z_gu_sum, ap_gu_sum, z_dn_sum
    )
    r_a2_dn, r_bp_dn, sh_got = recv_d(g_a2_dn, x=2), recv_d(g_bp_dn, z=1), recv_d(sh_send, x=2)
    pay_half = stack(payload, *p_y)
    pay_other = recv_t(pay_half, c=1)
    pay_half, pay_other = sync(pay_half, pay_other)
    mixed_grad = mixed_back(starts8, pay_half, pay_other, w_output)

    query_grad, expanded_grad, rope_grad = attend_back(image_starts, qn, qr, kn, kr, v, mixed_grad, cos2, sin2)
    n1_send = normed1_part(half_at(1 - cc), query_grad, expanded_grad, rope_grad, w_query_t, w_expand)
    n1_send, r_a2_dn, r_bp_dn, z_gu_sum = sync(n1_send, r_a2_dn, r_bp_dn, z_gu_sum)
    n1_got = recv_t(n1_send, c=1)
    r_z_gu = recv_d(z_gu_sum, z=1)
    n1_keep = normed1_part(half_at(cc), query_grad, expanded_grad, rope_grad, w_query_t, w_expand)
    n1_got, n1_keep, query_grad, expanded_grad, g_am_gu, mixed, pay_half = sync(
        n1_got, n1_keep, query_grad, expanded_grad, g_am_gu, mixed, pay_half
    )
    n1_b = split_sum(n1_keep, n1_got, starts4)
    n1_y1, n1_y3 = recv_t(n1_b[1], y=-1), recv_t(n1_b[3], y=1)

    w_query_g = dot(query_grad, normed1, TN).astype(BF)
    w_expand_g = dot(compressed, expanded_grad, TN).astype(BF)
    w_expand_g = jnp.concatenate([w_expand_g[64 * i : 64 * (i + 1)] for i in range(8)], axis=1)
    w_out_g, w_router_g = output_grads(starts8, pay_half, pay_other, mixed, normed2)
    rest = cat(w_query_g, w_out_g, w_expand_g, w_router_g)
    rest_half, rest_send = halves(rest, x // 2)
    rest_got = recv_d(rest_send, x=2)
    n1_y1, n1_y3, n1_b2, rest_half, g_am_gu, g_ap_dn, sh_keep, sh_got, g_bm_dn = sync(
        n1_y1, n1_y3, n1_b[2], rest_half, g_am_gu, g_ap_dn, sh_keep, sh_got, g_bm_dn
    )
    n1_y2 = recv_t(n1_b2, y=2)
    r_bm_dn = recv_d(g_bm_dn, z=1)
    am_gu_sum, ap_dn_sum = add(g_am_gu, r_bm_gu), add(g_ap_dn, r_bp_dn)
    sh_keep, sh_send = halves(add(sh_keep, sh_got), x % 2)
    sh_got = swap_x(sh_send)
    n1_y1, n1_y3, n1_y2, rest_half, rest_got, r_bm_dn, r_z_gu, am_gu_sum, ap_dn_sum, sh_keep, sh_got = sync(
        n1_y1, n1_y3, n1_y2, rest_half, rest_got, r_bm_dn, r_z_gu, am_gu_sum, ap_dn_sum, sh_keep, sh_got
    )
    n1_sum = add(n1_b[0], n1_y1, n1_y2, n1_y3)
    n1_other = recv_t(n1_sum, zh=1)
    rest_keep, rest_send = halves(add(rest_half, rest_got), x % 2)
    rest_got = swap_x(rest_send)
    sh_own = add(sh_keep, sh_got)
    sh_next = swap_x(sh_own)
    am_dn_sum = add(g_am_dn, r_bm_dn)
    n1_sum, n1_other, rest_keep, rest_got, sh_own, sh_next, am_gu_sum, ap_gu_sum, ap_dn_sum, am_dn_sum, z_dn_sum = sync(
        n1_sum, n1_other, rest_keep, rest_got, sh_own, sh_next, am_gu_sum, ap_gu_sum, ap_dn_sum, am_dn_sum, z_dn_sum
    )
    tok_rows = rows_one(
        (n1_sum, n1_other),
        w_lat,
        own_rows(tokens),
        own_rows(inv1),
        hid_grad,
        norm1_gain[None, :],
        own_rows(latent),
        own_rows(inv_lat),
        latent_gain[None, :],
        gain2,
    )
    t1, t3 = recv_t(tok_rows, y=1), recv_t(tok_rows, y=-1)
    r_ap_gu, r_am_gu = recv_d(ap_gu_sum, x=-1), recv_d(am_gu_sum, x=1)
    rest_keep, rest_send = halves(add(rest_keep, rest_got), z)
    rest_got = recv_d(rest_send, z=1)
    sh_pair = jnp.concatenate([sh_own, sh_next], axis=1)
    tok_rows, t1, t3, rest_keep, rest_got, sh_pair, z_dn_sum = sync(
        tok_rows, t1, t3, rest_keep, rest_got, sh_pair, z_dn_sum
    )
    t2 = recv_t(tok_rows, y=2)
    rest_own = add(rest_keep, rest_got)
    rest_pair = recv_d(rest_own, z=1)
    tok_rows, t1, t2, t3, rest_own, rest_pair, sh_pair, ap_dn_sum, am_dn_sum, z_dn_sum, r_ap_gu, r_am_gu = sync(
        tok_rows, t1, t2, t3, rest_own, rest_pair, sh_pair, ap_dn_sum, am_dn_sum, z_dn_sum, r_ap_gu, r_am_gu
    )
    sh_far = recv_d(sh_pair, x=2)
    tok_half = stack(tok_rows, t1, t2, t3)
    tok_other = recv_t(tok_half, c=1)
    r_z_dn = recv_d(z_dn_sum, z=1)
    pair = jnp.concatenate([rest_own, rest_pair], axis=1)
    tok_half, tok_other, pair, sh_pair, sh_far = sync(tok_half, tok_other, pair, sh_pair, sh_far)
    blocks = [pair] + [recv_d(pair, x=i) for i in (1, 2, 3)]
    sh_half = jnp.concatenate([sh_pair, sh_far], axis=1)
    sh_across = recv_d(sh_half, z=1)
    pick = (
        (jnp.arange(LX, dtype=jnp.int32)[None, :] == tr * LW + column[:LW48, None]) & (column[:LW48, None] < LW)
    ).astype(BF)
    offsets = jnp.stack([((x + i) % 4 * 2 + (z + j) % 2) * 256 for i in range(4) for j in range(2)])
    w_lat_g, gains = latent_w_grad(starts8, tok_half, tok_other, normed1, pick)
    gains = jnp.pad(gains[: GAINS // FREE, 128 - FREE :].reshape(-1), (0, 16 * D - GAINS)).reshape(16, D)
    small = cat(w_lat_g, gains.astype(BF))
    own_cols = lax.dynamic_slice_in_dim(tokens, tr * 128, 128, 1).astype(F32)
    small = sum_d(small, 1)
    tokens_grad = spread(starts8, tok_half, tok_other)
    small, tokens_grad, r_z_dn, ap_dn_sum, am_dn_sum, *blocks = sync(
        small, tokens_grad, r_z_dn, ap_dn_sum, am_dn_sum, *blocks
    )
    small = sum_d(small, 2)
    r_ap_dn, r_am_dn = recv_d(ap_dn_sum, x=-1), recv_d(am_dn_sum, x=1)
    wq_grad, wo_grad, we_grad, wr_grad = finish_rest(offsets, blocks)
    output = (own_cols + branch_sum.astype(F32)).astype(BF)
    small, wq_grad, wo_grad, we_grad, wr_grad, output, sh_across = sync(
        small, wq_grad, wo_grad, we_grad, wr_grad, output, sh_across
    )
    small = sum_d(small, 0)
    sh_offsets = jnp.stack([((z + j) % 2 * 4 + (x ^ i)) * 256 for j in range(2) for i in range(4)])
    sg_grad, su_grad, sd_grad = finish_shared(sh_offsets, sh_half, sh_across)
    eg_grad, eu_grad, ed_grad = finish_experts(
        (g_own_gu, r_a2_gu, r_ap_gu, r_am_gu, r_z_gu), (g_own_dn, r_a2_dn, r_ap_dn, r_am_dn, r_z_dn)
    )
    small = small.astype(F32)
    gains = small[LW48:].reshape(-1)

    return (
        output,
        tokens_grad,
        gains[:D],
        wq_grad.T,
        small[:LW].T,
        gains[2 * D : GAINS],
        we_grad,
        wo_grad,
        gains[D : 2 * D],
        wr_grad.T,
        eg_grad.T[None],
        eu_grad.T[None],
        ed_grad.T[None],
        sg_grad.T,
        su_grad.T,
        sd_grad,
    )


def solution(mesh):
    in_specs = (
        P("dp", None),
        P("dp", "tensor"),
        P("dp", None),
        P("dp", None),
        P("dp", None),
        P(),
        P(None, "tensor"),
        P(None, "tensor"),
        P(),
        P(None, "tensor"),
        P("tensor", None),
        P(),
        P(),
        P("tensor", None, "dp"),
        P("tensor", None, "dp"),
        P("tensor", None, "dp"),
        P(None, "tensor"),
        P(None, "tensor"),
        P("tensor", None),
    )
    out_specs = (
        P("dp", "tensor"),
        P("dp", None),
        P(),
        P(None, "tensor"),
        P(None, "tensor"),
        P(),
        P(None, "tensor"),
        P("tensor", None),
        P(),
        P(),
        P("tensor", None, "dp"),
        P("tensor", None, "dp"),
        P("tensor", None, "dp"),
        P(None, "tensor"),
        P(None, "tensor"),
        P("tensor", None),
    )
    return jax.shard_map(local, mesh=mesh, in_specs=in_specs, out_specs=out_specs, check_vma=False)
```

```python
import functools
import math

import jax
import jax.numpy as jnp
from jax import lax
from jax.experimental import pallas as pl
from jax.experimental.pallas import tpu as pltpu
from jax.sharding import PartitionSpec as P

D = 2048
NOPE = 128
ROPE = 64
VDIM = 128
LATENT = 512
TOPK = 6
EXPERTS = 16
IMG = 256
SPANS = 2
LEN = 1024
CAP = 480
FS = 176
LW = 36
LW48 = 48
LP = 80
LX = 640
RB = 128
PW = D + 128
QW = D + LX
FA = 3 * FS
BF = jnp.bfloat16
F32 = jnp.float32
EPS = 1e-06
MASKED = -1e30
SCALE = (NOPE + ROPE) ** (-0.5)
MB = 1024 * 1024

NN = (((1,), (0,)), ((), ()))
NT = (((1,), (1,)), ((), ()))
TN = (((0,), (0,)), ((), ()))


def dot(a, b, dims=NN):
    return lax.dot_general(a, b, dims, preferred_element_type=F32)


VM = pl.BlockSpec(memory_space=pltpu.VMEM)
SM = pl.BlockSpec(memory_space=pltpu.SMEM)


def whole(kernel, outs, ins, limit, flops=0):
    arrays = [i[0] if isinstance(i, tuple) else i for i in ins]
    specs = [i[1] if isinstance(i, tuple) else VM for i in ins]
    return pl.pallas_call(
        kernel,
        out_shape=outs,
        in_specs=specs,
        out_specs=[VM] * len(outs),
        compiler_params=pltpu.CompilerParams(vmem_limit_bytes=limit * MB),
        cost_estimate=LIGHT,
    )(*arrays)


LIGHT = pl.CostEstimate(flops=1, bytes_accessed=1, transcendentals=0)


def sds(shape, dtype):
    return jax.ShapeDtypeStruct(shape, dtype)


def recv_t(a, zh=0, y=0, c=0):
    pairs = []
    for i in range(16):
        z, r, k = i // 8, i // 2 % 4, i % 2
        pairs.append((((z + zh) % 2) * 8 + ((r + y) % 4) * 2 + (k + c) % 2, i))
    return lax.ppermute(a, "tensor", pairs)


def recv_d(a, x=0, z=0):
    pairs = []
    for i in range(8):
        pairs.append((((i // 2 + x) % 4) * 2 + (i % 2 + z) % 2, i))
    return lax.ppermute(a, "dp", pairs)


def stack(*arrays):
    n = arrays[0].shape[0]

    def kernel(*refs):
        for i, r in enumerate(refs[:-1]):
            refs[-1][n * i : n * (i + 1)] = r[...]

    shape = (n * len(arrays), arrays[0].shape[1])
    return whole(kernel, [sds(shape, BF)], list(arrays), 12)[0]


def from_y(a):
    y1, y3 = recv_t(a, y=1), recv_t(a, y=-1)
    across, y1, y3 = sync(a, y1, y3)
    return [y1, recv_t(across, y=2), y3]


def to_y(b):
    y1, y3 = recv_t(b[1], y=-1), recv_t(b[3], y=1)
    across, y1, y3 = sync(b[2], y1, y3)
    return [y1, recv_t(across, y=2), y3]


def cat(*arrays):
    return jnp.concatenate(arrays, axis=0)


def split_sum(keep, got, starts):
    width = keep.shape[1]

    def kernel(s, a, b, *outs):
        for i, o in enumerate(outs):
            rows = pl.ds(pl.multiple_of(s[i], RB), RB)
            o[...] = (a[rows, :].astype(F32) + b[rows, :].astype(F32)).astype(BF)

    return whole(kernel, [sds((RB, width), BF)] * 4, [(starts, SM), keep, got], 16)


def add(*terms):
    return sum(t.astype(F32) for t in terms).astype(BF)


def swap_x(a):
    return lax.ppermute(a, "dp", [(i, ((i // 2) ^ 1) * 2 + i % 2) for i in range(8)])


def halves(a, k):
    n = a.shape[1] // 2
    return lax.dynamic_slice_in_dim(a, k * n, n, 1), lax.dynamic_slice_in_dim(a, (1 - k) * n, n, 1)


def sum_d(v, turn):
    if turn == 0:
        got = recv_d(v, z=1)
    elif turn == 1:
        got = swap_x(v)
    else:
        got = recv_d(v, x=2)
    return (v.astype(F32) + got.astype(F32)).astype(v.dtype)


def sync(*arrays):
    return lax.optimization_barrier(arrays)


def rotary_tables(length):
    position = jnp.arange(length, dtype=F32)
    frequency = jnp.exp(jnp.arange(ROPE // 2, dtype=F32) * (-2.0 * math.log(10000.0) / ROPE))
    angles = position[:, None] * frequency[None, :]
    return jnp.cos(angles), jnp.sin(angles)


def rotate(v, cos, sin):
    a, b = v[:, : ROPE // 2], v[:, ROPE // 2 :]
    return jnp.concatenate([a * cos - b * sin, b * cos + a * sin], axis=-1)


def unrotate(v, cos, sin):
    a, b = v[:, : ROPE // 2], v[:, ROPE // 2 :]
    return jnp.concatenate([a * cos + b * sin, b * cos - a * sin], axis=-1)


QB = 256


def probs_of(starts, first, qn, qr, kn, kr):
    scores = (dot(qn, kn, NT) + dot(qr, kr, NT)) * SCALE
    i = first + lax.broadcasted_iota(jnp.int32, (QB, 1), 0)
    j = lax.broadcasted_iota(jnp.int32, (1, LEN), 1)
    allowed = j <= i
    for n in range(SPANS):
        s = starts[0, n]
        row_in = (i >= s) & (i < s + IMG)
        col_in = (j >= s) & (j < s + IMG)
        allowed = allowed | (row_in & col_in)
    scores = jnp.where(allowed, scores, MASKED)
    raised = jnp.exp(scores - jnp.max(scores, axis=-1, keepdims=True))
    return raised / jnp.sum(raised, axis=-1, keepdims=True)


def attend(starts, qn, qr, kn, kr, v):
    def kernel(s, qn, qr, kn, kr, v, o):
        p = probs_of(s, pl.program_id(0) * QB, qn[...], qr[...], kn[...], kr[...])
        o[...] = dot(p.astype(BF), v[...]).astype(BF)

    rows = lambda w: pl.BlockSpec((QB, w), lambda i: (i, 0))
    full = lambda w: pl.BlockSpec((LEN, w), lambda i: (0, 0))
    return pl.pallas_call(
        kernel,
        grid=(LEN // QB,),
        out_shape=sds((LEN, VDIM), BF),
        in_specs=[SM, rows(NOPE), rows(ROPE), full(NOPE), full(ROPE), full(VDIM)],
        out_specs=rows(VDIM),
        compiler_params=pltpu.CompilerParams(vmem_limit_bytes=14 * MB),
        cost_estimate=LIGHT,
    )(starts, qn, qr, kn, kr, v)


def half_turn(v):
    return jnp.concatenate([v[:, ROPE // 2 :], v[:, : ROPE // 2]], axis=1)


def attend_back(starts, qn, qr, kn, kr, v, mg, cos2, sin2):
    def kernel(s, qn, qr, kn, kr, v, mg, cos, sin, qg, eg, rg, dkn, dkr, dv):
        step = pl.program_id(0)

        @pl.when(step == 0)
        def _():
            dkn[...] = jnp.zeros_like(dkn)
            dkr[...] = jnp.zeros_like(dkr)
            dv[...] = jnp.zeros_like(dv)

        p = probs_of(s, step * QB, qn[...], qr[...], kn[...], kr[...])
        m = mg[...]
        pg = dot(m, v[...], NT)
        sg = (p * (pg - jnp.sum(pg * p, axis=-1, keepdims=True))).astype(BF)
        qg[:, :NOPE] = (dot(sg, kn[...]) * SCALE).astype(BF)
        dqr = dot(sg, kr[...]) * SCALE
        rows = pl.ds(step * QB, QB)
        qg[:, NOPE:] = (dqr * cos[rows, :] - half_turn(dqr) * sin[rows, :]).astype(BF)
        dkn[...] += dot(sg, qn[...], TN) * SCALE
        dkr[...] += dot(sg, qr[...], TN) * SCALE
        dv[...] += dot(p.astype(BF), m, TN)

        @pl.when(step == LEN // QB - 1)
        def _():
            eg[:, :NOPE] = dkn[...].astype(BF)
            eg[:, NOPE:] = dv[...].astype(BF)
            d = dkr[...]
            rg[...] = (d * cos[...] - half_turn(d) * sin[...]).astype(BF)

    rows = lambda w: pl.BlockSpec((QB, w), lambda i: (i, 0))
    full = lambda w: pl.BlockSpec((LEN, w), lambda i: (0, 0))
    return pl.pallas_call(
        kernel,
        grid=(LEN // QB,),
        out_shape=[sds((LEN, w), BF) for w in (NOPE + ROPE, NOPE + VDIM, ROPE)],
        in_specs=[SM, rows(NOPE), rows(ROPE), full(NOPE), full(ROPE), full(VDIM), rows(VDIM), full(ROPE), full(ROPE)],
        out_specs=[rows(NOPE + ROPE), full(NOPE + VDIM), full(ROPE)],
        scratch_shapes=[pltpu.VMEM((LEN, w), F32) for w in (NOPE, ROPE, VDIM)],
        compiler_params=pltpu.CompilerParams(vmem_limit_bytes=18 * MB),
        cost_estimate=LIGHT,
    )(starts, qn, qr, kn, kr, v, mg, cos2, sin2)


def keys(normed1, place, lat_half, lat_other, gain, w_expand, cos2, sin2):
    n = lat_half.shape[0]

    def kernel(n1, place, a, b, gain, we, cos, sin, wl, lat, inv, comp, kn, kr, v):
        @pl.when(pl.program_id(0) == 0)
        def _():
            wl[...] = (dot(place[:, :n], a[...]) + dot(place[:, n:], b[...])).astype(BF)

        t = dot(n1[...], wl[...], NT).astype(BF)
        lat[...] = t
        t = t.astype(F32)
        c = t[:, :LATENT]
        r = lax.rsqrt(jnp.mean(c * c, axis=-1, keepdims=True) + EPS)
        c = (c * r * gain[...]).astype(BF)
        inv[...] = r
        comp[...] = c
        e = dot(c, we[...]).astype(BF)
        kn[...] = e[:, :NOPE]
        v[...] = e[:, NOPE:]
        d = t[:, LATENT : LATENT + ROPE]
        kr[...] = (d * cos[...] + half_turn(d) * sin[...]).astype(BF)

    rows = lambda w: pl.BlockSpec((QB, w), lambda i: (i, 0))
    full = lambda a: pl.BlockSpec(a.shape, lambda i: (0, 0))
    outs = [(LX, BF), (1, F32), (LATENT, BF), (NOPE, BF), (ROPE, BF), (VDIM, BF)]
    return pl.pallas_call(
        kernel,
        grid=(LEN // QB,),
        out_shape=[sds((LX, D), BF)] + [sds((LEN, w), t) for w, t in outs],
        in_specs=[rows(D), full(place), full(lat_half), full(lat_other), full(gain), full(w_expand), rows(ROPE), rows(ROPE)],
        out_specs=[pl.BlockSpec((LX, D), lambda i: (0, 0))] + [rows(w) for w, _ in outs],
        compiler_params=pltpu.CompilerParams(vmem_limit_bytes=26 * MB),
        cost_estimate=LIGHT,
    )(normed1, place, lat_half, lat_other, gain, w_expand, cos2, sin2)


def attention_part(which, mixed, w_out):
    def kernel(which, m, w, o):
        o[...] = dot(m[...], w[...]).astype(BF)

    return pl.pallas_call(
        kernel,
        grid_spec=pltpu.PrefetchScalarGridSpec(
            num_scalar_prefetch=1,
            grid=(2,),
            in_specs=[
                pl.BlockSpec((QB, VDIM), lambda i, which: (which[0] * 2 + i, 0)),
                pl.BlockSpec((VDIM, D), lambda i, which: (0, 0)),
            ],
            out_specs=pl.BlockSpec((QB, D), lambda i, which: (i, 0)),
        ),
        out_shape=sds((LEN // 2, D), BF),
        compiler_params=pltpu.CompilerParams(vmem_limit_bytes=16 * MB),
        cost_estimate=LIGHT,
    )(which, mixed, w_out)


def softmax(logits):
    e = jnp.exp(logits - jnp.max(logits, axis=-1, keepdims=True))
    return e / jnp.sum(e, axis=-1, keepdims=True)


def total_of(refs):
    t = refs[0][...].astype(F32)
    for r in refs[1:]:
        t = t + r[...].astype(F32)
    return t


def rows_mid(terms, x, gain, w_router):
    def kernel(a, b, x, gain, wr, hid, nrm, inv, probs):
        h = x[...].astype(F32) + total_of((a, b))
        r = lax.rsqrt(jnp.mean(h * h, axis=-1, keepdims=True) + EPS)
        n = (h * r * gain[...]).astype(BF)
        hid[...] = h
        nrm[...] = n
        inv[...] = r
        probs[...] = softmax(dot(n, wr[...]))

    outs = [sds((RB, D), F32), sds((RB, D), BF), sds((RB, 1), F32), sds((RB, EXPERTS), F32)]
    return whole(kernel, outs, [*terms, x, gain, w_router], 16)


def experts_front(starts, me, half, other, w_router, w_router_t, rank_row, grad, gu, dn):
    def kernel(s, me, a, b, wr, wrt, rank, g, gu, dn, n2, col, x, dy, dyg, dw, out, dx):
        lane = lax.broadcasted_iota(jnp.int32, (1, EXPERTS), 1)
        for n, ref in enumerate((a, b)):
            p = softmax(dot(ref[...], wr[...]))
            p = jnp.sum(jnp.where(lane == me[0], p, 0.0), axis=-1, keepdims=True)
            for i in range(4):
                rows = pl.ds(pl.multiple_of(s[n * 4 + i], RB), RB)
                n2[rows, :] = ref[i * RB : (i + 1) * RB]
                col[rows, :] = p[i * RB : (i + 1) * RB]
        nv, gv = n2[...], g[...]
        t = dot(wrt[...], nv, NT)
        t = jnp.exp(t - jnp.max(t, axis=0, keepdims=True))
        t = t / jnp.sum(t, axis=0, keepdims=True)
        mine = lax.broadcasted_iota(jnp.int32, (EXPERTS, 1), 0) == me[0]
        row = jnp.sum(jnp.where(mine, t, 0.0), axis=0, keepdims=True)
        hit = lax.broadcasted_iota(jnp.int32, (CAP, 1), 0) == rank[...]
        gate = jnp.sum(jnp.where(hit, row, 0.0), axis=-1, keepdims=True)
        pick = jnp.where(hit, 1.0, 0.0).astype(BF)
        x[...] = dot(pick, nv).astype(BF)
        got = dot(pick, gv)
        dyg[...] = got.astype(BF)
        dy[...] = (got * gate).astype(BF)
        h, da = ffn_back(nv, gv, gu[...], dn[...])
        dw[: 2 * FS] = dot(da, nv).astype(BF)
        dw[2 * FS :] = dot(h, gv).astype(BF)
        out[...] = dot(h, dn[...], TN).astype(BF)
        dx[...] = dot(da, gu[...], TN).astype(BF)

    outs = [sds((LEN, D), BF), sds((LEN, 1), F32)] + [sds((CAP, D), BF)] * 3
    outs += [sds((FA, D), BF)] + [sds((LEN, D), BF)] * 2
    ins = [(starts, SM), (me, SM), half, other, w_router, w_router_t, rank_row, grad, gu, dn]
    return whole(kernel, outs, ins, 56)


ANY = pl.BlockSpec(memory_space=pl.ANY)
FLOPS = 2 * 9 * FS * D


def ffn_back(x, dy, gu, dn):
    act = dot(gu, x, NT)
    g, u = act[:FS], act[FS:]
    sg = jax.nn.sigmoid(g)
    h = (g * sg * u).astype(BF)
    dh = dot(dn, dy, NT)
    dg = (dh * u * sg * (1.0 + g * (1.0 - sg))).astype(BF)
    du = (dh * g * sg).astype(BF)
    return h, jnp.concatenate([dg, du], axis=0)


def experts(x, dy, chunks, last=None):
    n = len(chunks)
    n_in = 2 if last is None else 6
    pieces = [(i, first, a) for i, c in enumerate(chunks) for first, a in zip((0, 2 * FS), c)]
    m = len(pieces)

    def kernel(*refs):
        if last is None:
            x, dy = refs[:2]
        else:
            me, x, dy, dyg, out0, dx0 = refs[:6]
        w, outs, (out, dx) = refs[n_in : n_in + m], refs[n_in + m : n_in + 2 * m], refs[n_in + 2 * m : n_in + 2 * m + 2]
        wgu, wdn, hs, das, grads, sem_in, sem_out = refs[n_in + 2 * m + 2 :]
        loads = [[] for _ in range(n)]
        for k, (i, first, a) in enumerate(pieces):
            for part, (size, ref) in enumerate(((2 * FS, wgu), (FS, wdn))):
                at = 2 * FS * part - first
                if 0 <= at < a.shape[0]:
                    src = w[k].at[pl.ds(at, size)]
                    loads[i].append(
                        pltpu.make_async_copy(src, ref.at[pl.ds(size * i, size)], sem_in.at[2 * i + part])
                    )
        for c in loads:
            for d in c:
                d.start()
        xv, dyv = x[...], dy[...]
        stores = []
        for i in range(n):
            for c in loads[i]:
                c.wait()
            h, da = ffn_back(xv, dyv, wgu[2 * FS * i : 2 * FS * (i + 1)], wdn[FS * i : FS * (i + 1)])
            hs[FS * i : FS * (i + 1)] = h
            das[2 * FS * i : 2 * FS * (i + 1)] = da
            grads[i, : 2 * FS] = dot(da, xv).astype(BF)
            grads[i, 2 * FS :] = dot(h, dyv).astype(BF)
            for k, (o, first, a) in enumerate(pieces):
                if o == i:
                    src = grads.at[i, pl.ds(first, a.shape[0])]
                    stores.append(pltpu.make_async_copy(src, outs[k], sem_out.at[k]))
                    stores[-1].start()
        sum_o = dot(hs[...], wdn[...], TN)
        sum_d = dot(das[...], wgu[...], TN)
        if last is None:
            out[...] = sum_o
            dx[...] = sum_d
        else:
            so = (out0[...] + sum_o).astype(BF)
            out[...] = so
            dx[:, :D] = (dx0[...] + sum_d).astype(BF)
            gg = jnp.sum(so.astype(F32) * dyg[...].astype(F32), axis=-1, keepdims=True)
            lane = lax.broadcasted_iota(jnp.int32, (1, 128), 1)
            dx[:, D:] = jnp.where(lane == me[0], gg, 0.0).astype(BF)
        for c in stores:
            c.wait()

    if last is None:
        arrays, specs = [x, dy], [VM] * 2
        ends = [sds((CAP, D), F32)] * 2
    else:
        dyg, out, dx, me = last
        arrays, specs = [me, x, dy, dyg, out, dx], [SM] + [VM] * 5
        ends = [sds((CAP, D), BF), sds((CAP, PW), BF)]
    res = pl.pallas_call(
        kernel,
        out_shape=[sds(a.shape, BF) for _, _, a in pieces] + ends,
        in_specs=specs + [ANY] * m,
        out_specs=[ANY] * m + [VM] * 2,
        scratch_shapes=[
            pltpu.VMEM((2 * FS * n, D), BF),
            pltpu.VMEM((FS * n, D), BF),
            pltpu.VMEM((FS * n, CAP), BF),
            pltpu.VMEM((2 * FS * n, CAP), BF),
            pltpu.VMEM((n, FA, D), BF),
            pltpu.SemaphoreType.DMA((2 * n,)),
            pltpu.SemaphoreType.DMA((m,)),
        ],
        compiler_params=pltpu.CompilerParams(vmem_limit_bytes=52 * MB),
        cost_estimate=LIGHT,
    )(*arrays, *[a for _, _, a in pieces])
    return res[:m], res[m], res[m + 1]


def combine_grad(which, rank_col, dx, shared_dx):
    rows_at = 256

    def kernel(which, rank, dx, sd, o):
        hit = rank[...] == lax.broadcasted_iota(jnp.int32, (1, CAP), 1)
        pick = jnp.where(hit, 1.0, 0.0).astype(BF)
        t = dot(pick, dx[...])
        o[:, :D] = (t[:, :D] + sd[...].astype(F32)).astype(BF)
        o[:, D:] = t[:, D:].astype(BF)

    at = lambda w: pl.BlockSpec((rows_at, w), lambda i, which: (which[0] * 2 + i, 0))
    return pl.pallas_call(
        kernel,
        grid_spec=pltpu.PrefetchScalarGridSpec(
            num_scalar_prefetch=1,
            grid=(2,),
            in_specs=[at(1), pl.BlockSpec((CAP, PW), lambda i, which: (0, 0)), at(D)],
            out_specs=pl.BlockSpec((rows_at, PW), lambda i, which: (i, 0)),
        ),
        out_shape=sds((LEN // 2, PW), BF),
        compiler_params=pltpu.CompilerParams(vmem_limit_bytes=40 * MB),
        cost_estimate=LIGHT,
    )(which, rank_col, dx, shared_dx)


def combine_out(rank_col, probs_col, slot_out, shared_out, mixed, w_out):
    rows_at = 256

    def kernel(rank, probs, so, sh, m, w, o):
        hit = rank[...] == lax.broadcasted_iota(jnp.int32, (1, CAP), 1)
        pick = jnp.where(hit, 1.0, 0.0).astype(BF)
        t = dot(pick, so[...]) * probs[...] + sh[...].astype(F32)
        t = (t + dot(m[...], w[...])).astype(BF)
        for i in range(D // 128):
            o[i] = t[:, 128 * i : 128 * (i + 1)]

    at = lambda w: pl.BlockSpec((rows_at, w), lambda i: (i, 0))
    return pl.pallas_call(
        kernel,
        grid=(LEN // rows_at,),
        out_shape=sds((D // 128, LEN, 128), BF),
        in_specs=[
            at(1),
            at(1),
            pl.BlockSpec((CAP, D), lambda i: (0, 0)),
            at(D),
            at(VDIM),
            pl.BlockSpec((VDIM, D), lambda i: (0, 0)),
        ],
        out_specs=pl.BlockSpec((D // 128, rows_at, 128), lambda i: (0, i, 0)),
        compiler_params=pltpu.CompilerParams(vmem_limit_bytes=24 * MB),
        cost_estimate=LIGHT,
    )(rank_col, probs_col, slot_out, shared_out, mixed, w_out)


def normed1_part(which, query_grad, expanded_grad, rope_grad, w_query, w_expand):
    rows_at = 256

    def kernel(which, q, e, r, wq, we, o):
        o[:, :D] = dot(q[...], wq[...]).astype(BF)
        o[:, D : D + LATENT] = dot(e[...], we[...], NT).astype(BF)
        o[:, D + LATENT :] = jnp.concatenate([r[...], jnp.zeros((rows_at, LX - LATENT - ROPE), BF)], axis=1)

    at = lambda w: pl.BlockSpec((rows_at, w), lambda i, which: (which[0] * 2 + i, 0))
    full = lambda a: pl.BlockSpec(a.shape, lambda i, which: (0, 0))
    return pl.pallas_call(
        kernel,
        grid_spec=pltpu.PrefetchScalarGridSpec(
            num_scalar_prefetch=1,
            grid=(2,),
            in_specs=[at(NOPE + ROPE), at(NOPE + VDIM), at(ROPE), full(w_query), full(w_expand)],
            out_specs=pl.BlockSpec((rows_at, QW), lambda i, which: (i, 0)),
        ),
        out_shape=sds((LEN // 2, QW), BF),
        compiler_params=pltpu.CompilerParams(vmem_limit_bytes=14 * MB),
        cost_estimate=LIGHT,
    )(which, query_grad, expanded_grad, rope_grad, w_query, w_expand)


def norm_back(v, inv, gain, incoming):
    weighted = incoming * gain
    inner = jnp.mean(weighted * v, axis=-1, keepdims=True)
    return inv * weighted - v * (inv * inv * inv) * inner, jnp.sum(incoming * v * inv, axis=0, keepdims=True)


def rows_two(terms, hidden, inv, probs, grad, gain, w_router_t):
    def kernel(a, b, h, inv, p, g, gain, wr, hg, pay, gg):
        t = total_of((a, b))
        gates = t[:, D : D + EXPERTS]
        pv = p[...]
        lg = (pv * (gates - jnp.sum(pv * gates, axis=-1, keepdims=True))).astype(BF)
        n2 = t[:, :D] + dot(lg, wr[...])
        r, gain_grad = norm_back(h[...], inv[...], gain[...], n2)
        r = r + g[...].astype(F32)
        hg[...] = r
        pay[:, :D] = r.astype(BF)
        pay[:, D:] = jnp.concatenate([lg, jnp.zeros((RB, 128 - EXPERTS), BF)], axis=1)
        gg[...] = gain_grad

    outs = [sds((RB, D), F32), sds((RB, PW), BF), sds((1, D), F32)]
    return whole(kernel, outs, [*terms, hidden, inv, probs, grad, gain, w_router_t], 16)


GAINS = 2 * D + LATENT
FREE = LX - LATENT - ROPE


def rows_one(terms, w_lat, x, inv, hg, gain, latent, inv_lat, gain_lat, gain_two):
    def kernel(a, b, wl, x, inv, hg, gain, lat, inv_lat, gain_lat, two, o):
        t = total_of((a, b))
        head, g_lat = norm_back(lat[:, :LATENT].astype(F32), inv_lat[...], gain_lat[...], t[:, D : D + LATENT])
        lg = jnp.concatenate([head, t[:, D + LATENT :]], axis=1).astype(BF)
        t = t[:, :D] + dot(lg, wl[...])
        r, g_one = norm_back(x[...].astype(F32), inv[...], gain[...], t)
        o[:, :D] = (hg[...] + r).astype(BF)
        o[:, D : D + LATENT] = lg[:, :LATENT]
        g = jnp.concatenate([g_one, two[...], g_lat], axis=1)
        g = [g[:, FREE * i : FREE * (i + 1)] for i in range(GAINS // FREE)]
        g = jnp.concatenate(g + [jnp.zeros((RB - len(g), FREE), F32)], axis=0)
        o[:, D + LATENT :] = jnp.concatenate([lg[:, LATENT : LATENT + ROPE], g.astype(BF)], axis=1)

    ins = [*terms, w_lat, x, inv, hg, gain, latent, inv_lat, gain_lat, gain_two]
    return whole(kernel, [sds((RB, QW), BF)], ins, 20)[0]


def mixed_back(starts, half, other, w_out):
    def kernel(s, a, b, w, o):
        for n, ref in enumerate((a, b)):
            t = dot(ref[:, :D], w[...], NT).astype(BF)
            for i in range(4):
                rows = pl.ds(pl.multiple_of(s[n * 4 + i], RB), RB)
                o[rows, :] = t[i * RB : (i + 1) * RB]

    return whole(kernel, [sds((LEN, VDIM), BF)], [(starts, SM), half, other, w_out], 16, 2 * LEN * D * VDIM)[0]


def output_grads(starts, half, other, mixed, normed2):
    def kernel(s, a, b, m, n2, wo, wr):
        sum_o = jnp.zeros((VDIM, D), F32)
        sum_r = jnp.zeros((EXPERTS, D), F32)
        for n, ref in enumerate((a, b)):
            at = [pl.ds(pl.multiple_of(s[n * 4 + i], RB), RB) for i in range(4)]
            mix = jnp.concatenate([m[r, :] for r in at], axis=0)
            sum_o = sum_o + dot(mix, ref[:, :D], TN)
            for i, r in enumerate(at):
                lg = ref[i * RB : (i + 1) * RB, D:]
                sum_r = sum_r + dot(lg, n2[r, :], TN)[:EXPERTS]
        wo[...] = sum_o.astype(BF)
        wr[...] = sum_r.astype(BF)

    outs = [sds((VDIM, D), BF), sds((EXPERTS, D), BF)]
    return whole(kernel, outs, [(starts, SM), half, other, mixed, normed2], 24, 2 * LEN * D * 256)


def column_blocks(offsets, blocks):
    for i, ref in enumerate(blocks):
        for j in range(2):
            off = pl.multiple_of(offsets[2 * i + j], 256)
            yield off, lambda a, b, ref=ref, j=j: ref[a:b, 256 * j : 256 * (j + 1)].astype(F32)


def finish_rest(offsets, blocks):
    def kernel(off, *refs):
        wq, wo, we, wr = refs[4:]
        for at, block in column_blocks(off, refs[:4]):
            cols = pl.ds(at, 256)
            wq[:, cols] = block(0, 192)
            wo[:, cols] = block(192, 320)
            we[pl.ds(pl.multiple_of(at // 4, 64), 64), :] = block(320, 384)
            wr[:, cols] = block(384, 400)

    outs = [sds((192, D), F32), sds((VDIM, D), F32), sds((LATENT, 256), F32), sds((EXPERTS, D), F32)]
    return whole(kernel, outs, [(offsets, SM), *blocks], 16)


def finish_shared(offsets, near, far):
    def kernel(off, a, b, gate, up, down):
        for i in range(8):
            ref, cols = (a, b)[i // 4], slice(256 * (i % 4), 256 * (i % 4 + 1))
            at = pl.ds(pl.multiple_of(off[i], 256), 256)
            gate[:, at] = ref[:FS, cols].astype(F32)
            up[:, at] = ref[FS : 2 * FS, cols].astype(F32)
            down[:, at] = ref[2 * FS :, cols].astype(F32)

    return whole(kernel, [sds((FS, D), F32)] * 3, [(offsets, SM), near, far], 16)


def finish_experts(gu, dn):
    def kernel(*refs):
        gu, dn, (gate, up, down) = refs[:5], refs[5:10], refs[10:]
        t = total_of(gu)
        gate[...] = t[:FS]
        up[...] = t[FS:]
        down[...] = total_of(dn)

    return whole(kernel, [sds((FS, D), F32)] * 3, [*gu, *dn], 24)


def latent_w_grad(starts, half, other, normed1, pick):
    def kernel(s, a, b, n1, pick, o, gains, parts):
        total = jnp.zeros((LW48, D), F32)
        for n, ref in enumerate((a, b)):
            at = [pl.multiple_of(s[n * 4 + i], RB) for i in range(4)]
            rows = jnp.concatenate([n1[pl.ds(r, RB), :] for r in at], axis=0)
            own = dot(pick[...], ref[:, D:], NT).astype(BF)
            total = total + dot(own, rows)
            for i, r in enumerate(at):
                parts[pl.ds(r, RB), :] = ref[i * RB : (i + 1) * RB, QW - 128 :].astype(F32)
        o[...] = total.astype(BF)
        g = parts[:RB]
        for i in range(1, LEN // RB):
            g = g + parts[i * RB : (i + 1) * RB]
        gains[...] = g

    return pl.pallas_call(
        kernel,
        out_shape=[sds((LW48, D), BF), sds((RB, 128), F32)],
        in_specs=[SM, VM, VM, VM, VM],
        out_specs=[VM, VM],
        scratch_shapes=[pltpu.VMEM((LEN, 128), F32)],
        compiler_params=pltpu.CompilerParams(vmem_limit_bytes=24 * MB),
        cost_estimate=LIGHT,
    )(starts, half, other, normed1, pick)


def spread(starts, half, other):
    def kernel(s, a, b, o):
        for n, ref in enumerate((a, b)):
            for i in range(4):
                rows = pl.ds(pl.multiple_of(s[n * 4 + i], RB), RB)
                o[rows, :] = ref[i * RB : (i + 1) * RB, :D].astype(F32)

    return whole(kernel, [sds((LEN, D), F32)], [(starts, SM), half, other], 24)[0]


def local(
    tokens,
    cotangent,
    expert_ids,
    slot_order,
    image_starts,
    norm1_gain,
    w_query,
    w_latent,
    latent_gain,
    w_expand,
    w_output,
    norm2_gain,
    w_router,
    expert_gate,
    expert_up,
    expert_down,
    shared_gate,
    shared_up,
    shared_down,
):
    tr = lax.axis_index("tensor")
    dr = lax.axis_index("dp")
    zh, yy, cc = tr // 8, tr // 2 % 4, tr % 2
    peers = [((yy + y) % 4, (cc + c) % 2) for c in range(2) for y in range(4)]
    starts8 = jnp.stack([(c * 4 + y) * RB for y, c in peers]).astype(jnp.int32)
    starts4 = jnp.stack([y * RB for y, c in peers[:4]]).astype(jnp.int32)
    own_row = (cc * 4 + yy) * RB
    own_rows = lambda a: lax.dynamic_slice_in_dim(a, own_row, RB, 0)
    me = jnp.full((1,), tr, jnp.int32)

    half_at = lambda k: jnp.full((1,), k, jnp.int32)
    half_rows = lambda a, k: lax.dynamic_slice_in_dim(a, k * (LEN // 2), LEN // 2, 0)

    x, z = dr // 2, dr % 2

    out_grad = lax.all_gather(cotangent, "tensor", axis=1, tiled=True)
    lat_t = w_latent.T
    lat_z = recv_t(lat_t, zh=1)
    own_gu = cat(expert_gate[0].T, expert_up[0].T)
    own_dn = expert_down[0].T
    resid = tokens.astype(F32)
    inv1 = lax.rsqrt(jnp.mean(resid * resid, axis=-1, keepdims=True) + EPS)
    normed1 = (resid * inv1 * norm1_gain).astype(BF)
    lat_z, lat_t, own_gu, own_dn, normed1 = sync(lat_z, lat_t, own_gu, own_dn, normed1)

    lat = jnp.pad(cat(lat_t, lat_z), [(0, LP - 2 * LW), (0, 0)])
    lat_y = from_y(lat)
    ap_dn, zz_dn = recv_d(own_dn, x=1), recv_d(own_dn, z=1)
    chosen = jnp.any(expert_ids == tr, axis=1)
    order = slot_order[0]
    token = jnp.arange(LEN, dtype=jnp.int32)
    place = jnp.sum(jnp.where(order[:, None] == token[None, :], token[:, None], 0), axis=0)
    before = (place[:, None] < place[None, :]) & chosen[:, None]
    rank = jnp.sum(before.astype(jnp.int32), axis=0)
    rank = jnp.where(chosen, rank, -1)
    rank_row, rank_col = rank[None, :], rank[:, None]
    cos, sin = rotary_tables(LEN)
    cos2, sin2 = jnp.concatenate([cos, cos], axis=1), jnp.concatenate([-sin, sin], axis=1)
    w_query_t = w_query.T
    query = dot(normed1, w_query_t, NT)
    qn = query[:, :NOPE].astype(BF)
    qr = rotate(query[:, NOPE:], cos, sin).astype(BF)
    column = jnp.arange(LP, dtype=jnp.int32)
    owner = jnp.stack([(zh + column // LW) % 2 * 8 + y * 2 + c for y, c in peers])
    target = jnp.where(column < 2 * LW, owner * LW + column % LW, -1).reshape(-1)
    lat_place = (jnp.arange(LX, dtype=jnp.int32)[:, None] == target[None, :]).astype(BF)
    lat, *lat_y, ap_dn, zz_dn, qn, qr, rank_row, rank_col, own_gu, own_dn, lat_place, cos2, sin2 = sync(
        lat, *lat_y, ap_dn, zz_dn, qn, qr, rank_row, rank_col, own_gu, own_dn, lat_place, cos2, sin2
    )

    lat_half = stack(lat, *lat_y)
    lat_other = recv_t(lat_half, c=1)
    zz_gu, ap_gu, am_gu = recv_d(own_gu, z=1), recv_d(own_gu, x=1), recv_d(own_gu, x=-1)
    sh_gu = cat(shared_gate.T, shared_up.T)
    lat_half, lat_other, sh_gu = sync(lat_half, lat_other, sh_gu)

    w_lat, latent, inv_lat, compressed, kn, kr, v = keys(
        normed1, lat_place, lat_half, lat_other, latent_gain[None, :], w_expand, cos2, sin2
    )
    mixed = attend(image_starts, qn, qr, kn, kr, v)
    at_send = attention_part(half_at(1 - cc), mixed, w_output)
    at_send, zz_gu, ap_gu, am_gu, own_dn, own_gu = sync(at_send, zz_gu, ap_gu, am_gu, own_dn, own_gu)
    at_got = recv_t(at_send, c=1)
    at_keep = attention_part(half_at(cc), mixed, w_output)
    bp_gu, am_dn = recv_d(ap_gu, z=1), recv_d(own_dn, x=-1)
    at_got, at_keep, own_gu = sync(at_got, at_keep, own_gu)

    at_b = split_sum(at_keep, at_got, starts4)
    at_y1, at_y3 = recv_t(at_b[1], y=-1), recv_t(at_b[3], y=1)
    at_y1, at_y3, at_b2, am_dn, own_gu = sync(at_y1, at_y3, at_b[2], am_dn, own_gu)
    at_y = [at_y1, recv_t(at_b2, y=2), at_y3]
    a2_gu = recv_d(own_gu, x=2)
    *at_y, bp_gu, ap_dn, own_dn, am_gu = sync(*at_y, bp_gu, ap_dn, own_dn, am_gu)
    at_sum = add(at_b[0], *at_y)
    at_other = recv_t(at_sum, zh=1)
    at_sum, at_other, ap_dn, am_gu, own_dn = sync(at_sum, at_other, ap_dn, am_gu, own_dn)
    own_tokens = own_rows(tokens)
    hidden, rows2, inv2, probs = rows_mid((at_sum, at_other), own_tokens, norm2_gain[None, :], w_router)
    n2_y1, n2_y3 = recv_t(rows2, y=1), recv_t(rows2, y=-1)
    bp_dn = recv_d(ap_dn, z=1)
    own_inv1, own_lat, own_inv_lat = own_rows(inv1), own_rows(latent), own_rows(inv_lat)
    rows2, n2_y1, n2_y3, a2_gu, own_dn, own_inv1, own_lat, own_inv_lat = sync(
        rows2, n2_y1, n2_y3, a2_gu, own_dn, own_inv1, own_lat, own_inv_lat
    )
    n2_y2 = recv_t(rows2, y=2)
    a2_dn = recv_d(own_dn, x=2)
    rows2, n2_y1, n2_y2, n2_y3, bp_dn, am_gu, am_dn, zz_gu, zz_dn, a2_dn = sync(
        rows2, n2_y1, n2_y2, n2_y3, bp_dn, am_gu, am_dn, zz_gu, zz_dn, a2_dn
    )
    n2_y = [n2_y1, n2_y2, n2_y3]
    n2_half = stack(rows2, *n2_y)
    n2_other = recv_t(n2_half, c=1)
    bm_gu, bm_dn = recv_d(am_gu, z=1), recv_d(am_dn, z=1)
    b2_gu, b2_dn = recv_d(zz_gu, x=2), recv_d(zz_dn, x=2)
    w_router_t = w_router.T
    n2_half, n2_other, out_grad, rank_row, w_router_t = sync(n2_half, n2_other, out_grad, rank_row, w_router_t)

    normed2, probs_col, slots, dy, dyg, sh_sum, s_out, s_dx = experts_front(
        starts8, me, n2_half, n2_other, w_router, w_router_t, rank_row, out_grad, sh_gu, shared_down
    )
    near, part_out, part_dx = experts(
        slots, dy, [(own_gu, own_dn), (ap_gu, ap_dn), (am_gu, am_dn), (zz_gu, zz_dn)]
    )
    sh_half, sh_send = halves(sh_sum, z)
    part_out, part_dx, bm_gu, bm_dn, b2_gu, b2_dn, sh_half, sh_send = sync(
        part_out, part_dx, bm_gu, bm_dn, b2_gu, b2_dn, sh_half, sh_send
    )
    sh_got = recv_d(sh_send, z=1)
    far, slot_out, dx = experts(
        slots,
        dy,
        [(a2_gu, a2_dn), (bp_gu, bp_dn), (b2_gu, b2_dn), (bm_gu, bm_dn)],
        (dyg, part_out, part_dx, me),
    )
    g_own_gu, g_own_dn, g_ap_gu, g_ap_dn, g_am_gu, g_am_dn, g_z_gu, g_z_dn = near
    g_a2_gu, g_a2_dn, g_bp_gu, g_bp_dn, g_b2_gu, g_b2_dn, g_bm_gu, g_bm_dn = far
    dx, sh_half, sh_got, g_b2_gu, g_bp_gu, slot_out = sync(dx, sh_half, sh_got, g_b2_gu, g_bp_gu, slot_out)

    n2_send = combine_grad(half_at(1 - cc), rank_col, dx, s_dx)
    n2_send, g_b2_gu, g_bp_gu, slot_out = sync(n2_send, g_b2_gu, g_bp_gu, slot_out)
    n2_got = recv_t(n2_send, c=1)
    n2_keep = combine_grad(half_at(cc), rank_col, dx, s_dx)
    r_b2_gu, r_bp_gu = recv_d(g_b2_gu, x=2), recv_d(g_bp_gu, z=1)
    n2_got, n2_keep, slot_out, sh_half, sh_got = sync(n2_got, n2_keep, slot_out, sh_half, sh_got)
    n2_b = split_sum(n2_keep, n2_got, starts4)
    n2_y1, n2_y3 = recv_t(n2_b[1], y=-1), recv_t(n2_b[3], y=1)
    sh_keep, sh_send = halves(add(sh_half, sh_got), x // 2)
    branch = combine_out(rank_col, probs_col, slot_out, s_out, mixed, w_output)
    n2_y1, n2_y3, n2_b2, sh_keep, sh_send, g_b2_dn, branch = sync(
        n2_y1, n2_y3, n2_b[2], sh_keep, sh_send, g_b2_dn, branch
    )
    branch_sum = lax.psum_scatter(branch.reshape(-1, 128), "tensor", scatter_dimension=0, tiled=True)
    n2_y = [n2_y1, recv_t(n2_b2, y=2), n2_y3]
    r_b2_dn = recv_d(g_b2_dn, x=2)
    *n2_y, r_b2_gu, r_bp_gu, g_bp_dn, g_a2_gu = sync(*n2_y, r_b2_gu, r_bp_gu, g_bp_dn, g_a2_gu)
    n2_sum = add(n2_b[0], *n2_y)
    n2_other = recv_t(n2_sum, zh=1)
    r_a2_gu = recv_d(g_a2_gu, x=2)
    r_bm_gu = recv_d(g_bm_gu, z=1)
    n2_sum, n2_other, r_b2_dn, g_bp_dn, sh_keep, sh_send, r_b2_gu, r_bp_gu, g_z_gu, g_ap_gu, g_z_dn = sync(
        n2_sum, n2_other, r_b2_dn, g_bp_dn, sh_keep, sh_send, r_b2_gu, r_bp_gu, g_z_gu, g_ap_gu, g_z_dn
    )
    hid_grad, payload, gain2 = rows_two(
        (n2_sum, n2_other), hidden, inv2, probs, own_rows(out_grad), norm2_gain[None, :], w_router_t
    )
    p_y = from_y(payload)
    z_gu_sum, ap_gu_sum, z_dn_sum = add(g_z_gu, r_b2_gu), add(g_ap_gu, r_bp_gu), add(g_z_dn, r_b2_dn)
    payload, *p_y, r_bm_gu, r_a2_gu, g_a2_dn, g_bp_dn, sh_keep, sh_send, z_gu_sum, ap_gu_sum, z_dn_sum = sync(
        payload, *p_y, r_bm_gu, r_a2_gu, g_a2_dn, g_bp_dn, sh_keep, sh_send, z_gu_sum, ap_gu_sum, z_dn_sum
    )
    r_a2_dn, r_bp_dn, sh_got = recv_d(g_a2_dn, x=2), recv_d(g_bp_dn, z=1), recv_d(sh_send, x=2)
    pay_half = stack(payload, *p_y)
    pay_other = recv_t(pay_half, c=1)
    pay_half, pay_other = sync(pay_half, pay_other)
    mixed_grad = mixed_back(starts8, pay_half, pay_other, w_output)

    query_grad, expanded_grad, rope_grad = attend_back(image_starts, qn, qr, kn, kr, v, mixed_grad, cos2, sin2)
    n1_send = normed1_part(half_at(1 - cc), query_grad, expanded_grad, rope_grad, w_query_t, w_expand)
    n1_send, r_a2_dn, r_bp_dn, z_gu_sum = sync(n1_send, r_a2_dn, r_bp_dn, z_gu_sum)
    n1_got = recv_t(n1_send, c=1)
    r_z_gu = recv_d(z_gu_sum, z=1)
    n1_keep = normed1_part(half_at(cc), query_grad, expanded_grad, rope_grad, w_query_t, w_expand)
    n1_got, n1_keep, query_grad, expanded_grad, g_am_gu, mixed, pay_half = sync(
        n1_got, n1_keep, query_grad, expanded_grad, g_am_gu, mixed, pay_half
    )
    n1_b = split_sum(n1_keep, n1_got, starts4)
    n1_y1, n1_y3 = recv_t(n1_b[1], y=-1), recv_t(n1_b[3], y=1)

    w_query_g = dot(query_grad, normed1, TN).astype(BF)
    w_expand_g = dot(compressed, expanded_grad, TN).astype(BF)
    w_expand_g = jnp.concatenate([w_expand_g[64 * i : 64 * (i + 1)] for i in range(8)], axis=1)
    w_out_g, w_router_g = output_grads(starts8, pay_half, pay_other, mixed, normed2)
    rest = cat(w_query_g, w_out_g, w_expand_g, w_router_g)
    rest_half, rest_send = halves(rest, x // 2)
    rest_got = recv_d(rest_send, x=2)
    n1_y1, n1_y3, n1_b2, rest_half, g_am_gu, g_ap_dn, sh_keep, sh_got = sync(
        n1_y1, n1_y3, n1_b[2], rest_half, g_am_gu, g_ap_dn, sh_keep, sh_got
    )
    n1_y2 = recv_t(n1_b2, y=2)
    am_gu_sum, ap_dn_sum = add(g_am_gu, r_bm_gu), add(g_ap_dn, r_bp_dn)
    sh_keep, sh_send = halves(add(sh_keep, sh_got), x % 2)
    sh_got = swap_x(sh_send)
    n1_y1, n1_y3, n1_y2, rest_half, rest_got, r_z_gu, am_gu_sum, ap_dn_sum, sh_keep, sh_got = sync(
        n1_y1, n1_y3, n1_y2, rest_half, rest_got, r_z_gu, am_gu_sum, ap_dn_sum, sh_keep, sh_got
    )
    n1_sum = add(n1_b[0], n1_y1, n1_y2, n1_y3)
    n1_other = recv_t(n1_sum, zh=1)
    rest_keep, rest_send = halves(add(rest_half, rest_got), x % 2)
    rest_got = swap_x(rest_send)
    sh_own = add(sh_keep, sh_got)
    sh_next = swap_x(sh_own)
    n1_sum, n1_other, rest_keep, rest_got, sh_own, sh_next, am_gu_sum, ap_gu_sum, g_bm_dn = sync(
        n1_sum, n1_other, rest_keep, rest_got, sh_own, sh_next, am_gu_sum, ap_gu_sum, g_bm_dn
    )
    tok_rows = rows_one(
        (n1_sum, n1_other),
        w_lat,
        own_tokens,
        own_inv1,
        hid_grad,
        norm1_gain[None, :],
        own_lat,
        own_inv_lat,
        latent_gain[None, :],
        gain2,
    )
    t1, t3 = recv_t(tok_rows, y=1), recv_t(tok_rows, y=-1)
    r_ap_gu, r_am_gu = recv_d(ap_gu_sum, x=-1), recv_d(am_gu_sum, x=1)
    r_bm_dn = recv_d(g_bm_dn, z=1)
    sh_pair = jnp.concatenate([sh_own, sh_next], axis=1)
    rest_keep, rest_send = halves(add(rest_keep, rest_got), z)
    tok_rows, t1, t3, rest_keep, rest_send, sh_pair, r_bm_dn, g_am_dn, z_dn_sum = sync(
        tok_rows, t1, t3, rest_keep, rest_send, sh_pair, r_bm_dn, g_am_dn, z_dn_sum
    )
    t2 = recv_t(tok_rows, y=2)
    rest_got = recv_d(rest_send, z=1)
    r_z_dn = recv_d(z_dn_sum, z=1)
    am_dn_sum = add(g_am_dn, r_bm_dn)
    tok_rows, t1, t2, t3, rest_keep, rest_got, sh_pair, ap_dn_sum, am_dn_sum, r_z_dn, r_ap_gu, r_am_gu = sync(
        tok_rows, t1, t2, t3, rest_keep, rest_got, sh_pair, ap_dn_sum, am_dn_sum, r_z_dn, r_ap_gu, r_am_gu
    )
    rest_own = add(rest_keep, rest_got)
    rest_pair = recv_d(rest_own, z=1)
    sh_far = recv_d(sh_pair, x=2)
    r_ap_dn, r_am_dn = recv_d(ap_dn_sum, x=-1), recv_d(am_dn_sum, x=1)
    tok_half = stack(tok_rows, t1, t2, t3)
    tok_other = recv_t(tok_half, c=1)
    tok_half, tok_other, rest_own, rest_pair, sh_pair, sh_far, branch_sum = sync(
        tok_half, tok_other, rest_own, rest_pair, sh_pair, sh_far, branch_sum
    )
    pair = jnp.concatenate([rest_own, rest_pair], axis=1)
    blocks = [pair] + [recv_d(pair, x=i) for i in (1, 2, 3)]
    pick = (
        (jnp.arange(LX, dtype=jnp.int32)[None, :] == tr * LW + column[:LW48, None]) & (column[:LW48, None] < LW)
    ).astype(BF)
    offsets = jnp.stack([((x + i) % 4 * 2 + (z + j) % 2) * 256 for i in range(4) for j in range(2)])
    w_lat_g, gains = latent_w_grad(starts8, tok_half, tok_other, normed1, pick)
    gains = jnp.pad(gains[: GAINS // FREE, 128 - FREE :].reshape(-1), (0, 16 * D - GAINS)).reshape(16, D)
    small = cat(w_lat_g, gains.astype(BF))
    own_cols = lax.dynamic_slice_in_dim(tokens, tr * 128, 128, 1).astype(F32)
    small = sum_d(small, 0)
    sh_half = jnp.concatenate([sh_pair, sh_far], axis=1)
    small, sh_half, r_ap_dn, r_am_dn = sync(small, sh_half, r_ap_dn, r_am_dn)
    small = sum_d(small, 1)
    sh_across = recv_d(sh_half, z=1)
    tokens_grad = spread(starts8, tok_half, tok_other)
    wq_grad, wo_grad, we_grad, wr_grad = finish_rest(offsets, blocks)
    small, tokens_grad, wq_grad = sync(small, tokens_grad, wq_grad)
    small = sum_d(small, 2)
    output = (own_cols + branch_sum.astype(F32)).astype(BF)
    small, wq_grad, wo_grad, we_grad, wr_grad, output, sh_across = sync(
        small, wq_grad, wo_grad, we_grad, wr_grad, output, sh_across
    )
    sh_offsets = jnp.stack([((z + j) % 2 * 4 + (x ^ i)) * 256 for j in range(2) for i in range(4)])
    sg_grad, su_grad, sd_grad = finish_shared(sh_offsets, sh_half, sh_across)
    eg_grad, eu_grad, ed_grad = finish_experts(
        (g_own_gu, r_a2_gu, r_ap_gu, r_am_gu, r_z_gu), (g_own_dn, r_a2_dn, r_ap_dn, r_am_dn, r_z_dn)
    )
    small = small.astype(F32)
    gains = small[LW48:].reshape(-1)

    return (
        output,
        tokens_grad,
        gains[:D],
        wq_grad.T,
        small[:LW].T,
        gains[2 * D : GAINS],
        we_grad,
        wo_grad,
        gains[D : 2 * D],
        wr_grad.T,
        eg_grad.T[None],
        eu_grad.T[None],
        ed_grad.T[None],
        sg_grad.T,
        su_grad.T,
        sd_grad,
    )


def solution(mesh):
    in_specs = (
        P("dp", None),
        P("dp", "tensor"),
        P("dp", None),
        P("dp", None),
        P("dp", None),
        P(),
        P(None, "tensor"),
        P(None, "tensor"),
        P(),
        P(None, "tensor"),
        P("tensor", None),
        P(),
        P(),
        P("tensor", None, "dp"),
        P("tensor", None, "dp"),
        P("tensor", None, "dp"),
        P(None, "tensor"),
        P(None, "tensor"),
        P("tensor", None),
    )
    out_specs = (
        P("dp", "tensor"),
        P("dp", None),
        P(),
        P(None, "tensor"),
        P(None, "tensor"),
        P(),
        P(None, "tensor"),
        P("tensor", None),
        P(),
        P(),
        P("tensor", None, "dp"),
        P("tensor", None, "dp"),
        P("tensor", None, "dp"),
        P(None, "tensor"),
        P(None, "tensor"),
        P("tensor", None),
    )
    return jax.shard_map(local, mesh=mesh, in_specs=in_specs, out_specs=out_specs, check_vma=False)
```
